32 devices in a mesh: dp: 4 (over y, core), ctx: 2 (over x), tp: 4 (over z).
Axes of the slice: x: 2, y: 2, z: 4, core: 2. Of those that a mesh axis runs over, the one named last changes fastest.
Arguments:
- tokens: bfloat16 [32768, 2048], P(('dp', 'ctx')), may hold values from -6 to 6
- cotangent: bfloat16 [32768, 2048], P(('dp', 'ctx')), may hold values from -6 to 6
- membership: int32 [4, 16], P('dp'), may hold values from 0 to 1
- ln_gain: bfloat16 [2048], replicated, may hold values from 0.099609375 to 1.8984375
- ln_bias: bfloat16 [2048], replicated, may hold values from -1.5 to 1.5
- w_query: bfloat16 [2048, 2048], P(('dp', 'ctx'), 'tp'), may hold values from -0.125 to 0.125
- b_query: bfloat16 [2048], P('tp'), may hold values from -1.5 to 1.5
- w_key: bfloat16 [2048, 2048], P(('dp', 'ctx'), 'tp'), may hold values from -0.125 to 0.125
- b_key: bfloat16 [2048], P('tp'), may hold values from -1.5 to 1.5
- w_value: bfloat16 [2048, 2048], P(('dp', 'ctx'), 'tp'), may hold values from -0.125 to 0.125
- b_value: bfloat16 [2048], P('tp'), may hold values from -1.5 to 1.5
- w_dense: bfloat16 [2048, 2048], P('tp', ('dp', 'ctx')), may hold values from -1 to 1
- b_dense: bfloat16 [2048], replicated, may hold values from -1.5 to 1.5
- w_fc1: bfloat16 [2048, 8192], P(('dp', 'ctx'), 'tp'), may hold values from -0.125 to 0.125
- b_fc1: bfloat16 [8192], P('tp'), may hold values from -1.5 to 1.5
- w_fc2: bfloat16 [8192, 2048], P('tp', ('dp', 'ctx')), may hold values from -0.0625 to 0.0625
- b_fc2: bfloat16 [2048], replicated, may hold values from -1.5 to 1.5
Outputs:
- layer_out: bfloat16 [32768, 2048], P(('dp', 'ctx'))
- grad_tokens: float32 [32768, 2048], P(('dp', 'ctx'))
- grad_ln_gain: float32 [2048], replicated
- grad_ln_bias: float32 [2048], replicated
- grad_w_query: float32 [2048, 2048], P(('dp', 'ctx'), 'tp')
- grad_b_query: float32 [2048], P('tp')
- grad_w_key: float32 [2048, 2048], P(('dp', 'ctx'), 'tp')
- grad_b_key: float32 [2048], P('tp')
- grad_w_value: float32 [2048, 2048], P(('dp', 'ctx'), 'tp')
- grad_b_value: float32 [2048], P('tp')
- grad_w_dense: float32 [2048, 2048], P('tp', ('dp', 'ctx'))
- grad_b_dense: float32 [2048], replicated
- grad_w_fc1: float32 [2048, 8192], P(('dp', 'ctx'), 'tp')
- grad_b_fc1: float32 [8192], P('tp')
- grad_w_fc2: float32 [8192, 2048], P('tp', ('dp', 'ctx'))
- grad_b_fc2: float32 [2048], replicated
The draws below stay inside these ranges and needn't reach their ends.
Inputs may be any that keep to these rules, and one draw needn't show every extreme that they name: `membership`: entry c of row r names the group, among the 2 of row r, whose prompt continuation c of row r attends to.
All inputs are finite; a program needn't handle non-finite values.
Results may differ from the reference program's by a relative error of at most 0.012.
The reference program's roundings to bfloat16 on the way count: a program that leaves them out, or rounds other values in their place, can miss the bound.
Values may be sent and summed in bfloat16 or wider, within the bound.
A program may use at most 512 MiB of HBM per device.

```python
import jax
import jax.numpy as jnp
from jax import lax

D = 2048
HEADS = 32
HDIM = 64
ROT = 32
FF = 8192
PLEN = 2048
CLEN = 256
GPR = 2
CONTS = 16
TOKENS = 32768
N_DP = 4


def with_ends(array, rng, smallest, largest):
    dims = array.shape
    place = [jax.random.randint(jax.random.fold_in(rng, axis), (), 0, dims[axis]) for axis in range(len(dims))]
    array = array.at[tuple(place)].set(smallest)
    longest = dims.index(max(dims))
    place[longest] = (place[longest] + 1) % dims[longest]
    return array.at[tuple(place)].set(largest)


def strengthened(values, key, source, target, parts, factor):
    def block_of(axis_at):
        return (jnp.arange(values.shape[axis_at]) // (values.shape[axis_at] // parts)).reshape((-1,) + (1,) * (values.ndim - 1 - axis_at))

    first = jax.random.permutation(key, parts)[block_of(target)]
    other_side = (block_of(target) + parts // 2) % parts
    return jnp.where((block_of(source) == first) | (block_of(source) == other_side), factor * values, values)


def block_levels(key, extent, pieces, low, high):
    loudness = 1.0
    for dim, parts in pieces:
        draws = jax.random.uniform(jax.random.fold_in(jax.random.fold_in(key, 6), dim), (parts,), jnp.float32, low / len(pieces), high / len(pieces))
        loudness = loudness * jnp.repeat(jnp.exp(draws), extent[dim] // parts).reshape((-1,) + (1,) * (len(extent) - 1 - dim))
    return loudness


def centred(stream_key, extent, width, most, shards=(), kind=jnp.bfloat16):
    level = block_levels(stream_key, extent, shards, -0.22, 0.18) if shards else 1.0
    entries = jax.random.normal(stream_key, extent, jnp.float32) * width * level
    return jnp.minimum(jnp.maximum(entries, -most), most).astype(kind)


def heavy_noise(key, extent, scale, most, shards, heavy, kind=jnp.bfloat16):
    values = scale * jax.random.normal(key, extent, jnp.float32)
    if shards:
        values = values * block_levels(key, extent, shards, -0.22, 0.18)
    return jnp.clip(strengthened(values, jax.random.fold_in(key, 3), *heavy), -most, most).astype(kind)


def setup_inputs(seed: int = 0) -> dict:
    key_list = jax.random.split(jax.random.key(seed), 18)
    tokens = centred(key_list[0], (TOKENS, D), 1.0, 6.0, ((0, 8),))
    cotangent = heavy_noise(key_list[1], (TOKENS, D), 1.0, 6.0, ((0, 8),), (0, 1, 8, 2.0))
    membership = with_ends(jax.random.randint(key_list[2], (N_DP, CONTS), 0, GPR), jax.random.fold_in(key_list[2], 1), 0, GPR - 1).astype(jnp.int32)
    ln_gain = jnp.clip(1.0 + 0.18 * jax.random.normal(key_list[3], (D,), jnp.float32), 0.099609375, 1.8984375).astype(jnp.bfloat16)
    ln_bias = centred(key_list[4], (D,), 0.3, 1.5)
    w_query = centred(key_list[5], (D, D), D ** -0.5, 0.125, ((0, 8), (1, 4)))
    b_query = centred(key_list[6], (D,), 0.3, 1.5, ((0, 4),))
    w_key = centred(key_list[7], (D, D), D ** -0.5, 0.125, ((0, 8), (1, 4)))
    b_key = centred(key_list[8], (D,), 0.3, 1.5, ((0, 4),))
    w_value = centred(key_list[9], (D, D), D ** -0.5, 0.125, ((0, 8), (1, 4)))
    b_value = centred(key_list[10], (D,), 0.3, 1.5, ((0, 4),))
    w_dense = centred(key_list[11], (D, D), (D // 64) ** -0.5, 1.0, ((0, 4), (1, 8)))
    b_dense = centred(key_list[12], (D,), 0.3, 1.5)
    w_fc1 = centred(key_list[13], (D, FF), D ** -0.5, 0.125, ((0, 8), (1, 4)))
    b_fc1 = centred(key_list[14], (FF,), 0.3, 1.5, ((0, 4),))
    w_fc2 = centred(key_list[15], (FF, D), FF ** -0.5, 0.0625, ((0, 4), (1, 8)))
    b_fc2 = centred(key_list[16], (D,), 0.3, 1.5)
    return {"tokens": tokens, "cotangent": cotangent, "membership": membership, "ln_gain": ln_gain, "ln_bias": ln_bias, "w_query": w_query, "b_query": b_query, "w_key": w_key, "b_key": b_key, "w_value": w_value, "b_value": b_value, "w_dense": w_dense, "b_dense": b_dense, "w_fc1": w_fc1, "b_fc1": b_fc1, "w_fc2": w_fc2, "b_fc2": b_fc2}


@jax.custom_vjp
def low(v):
    return lax.optimization_barrier(v.astype(jnp.bfloat16)).astype(jnp.float32)

@jax.custom_vjp
def low_back(v):
    return v

def low_keep(v):
    return (low(v), None)

def low_pass(kept, grad):
    return (grad,)

def back_keep(v):
    return (v, None)

def back_low(kept, grad):
    return (low(grad),)
low.defvjp(low_keep, low_pass)
low_back.defvjp(back_keep, back_low)

def layer_norm(matrix, norm_gain, norm_shift):
    center = matrix - lax.optimization_barrier(jnp.mean(matrix, axis=-1, keepdims=True))
    spread = lax.optimization_barrier(jnp.mean(center * center, axis=-1, keepdims=True))
    return center * lax.rsqrt(spread + 1e-05) * norm_gain + norm_shift

def rotary_tables(positions):
    half_rot = ROT // 2
    frequency = 10000.0 ** (-2.0 * jnp.arange(half_rot, dtype=jnp.float32) / ROT)
    angles = positions.astype(jnp.float32)[:, None] * frequency[None, :]
    return (jnp.cos(angles)[:, None, :], jnp.sin(angles)[:, None, :])

def rotate_heads(head_values, cosine, sine_table):
    half_rot = ROT // 2
    first_half = head_values[..., :half_rot]
    second_half = head_values[..., half_rot:ROT]
    return jnp.concatenate([first_half * cosine - second_half * sine_table, second_half * cosine + first_half * sine_table, head_values[..., ROT:]], axis=-1)

def attend(queries, key_rows, values, allowed):
    scores = low_back(jnp.einsum('qhd,khd->hqk', queries, key_rows, precision=lax.Precision.HIGHEST) * HDIM ** (-0.5))
    scores = jnp.where(allowed[None], scores, -1e+30)
    row_peak = lax.optimization_barrier(jnp.max(scores, axis=-1, keepdims=True))
    exponent = jnp.exp(scores - row_peak)
    chance = exponent / lax.optimization_barrier(jnp.sum(exponent, axis=-1, keepdims=True))
    return jnp.einsum('hqk,khd->qhd', low(chance), values, precision=lax.Precision.HIGHEST)

def prompt_block(element, prompt_queries, prompt_keys, prompt_values):
    block_rows = min(512, PLEN)
    per_prompt = PLEN // block_rows
    which = element // per_prompt
    first_row = element % per_prompt * block_rows
    query_rows = lax.dynamic_slice_in_dim(lax.dynamic_index_in_dim(prompt_queries, which, 0, keepdims=False), first_row, block_rows, 0)
    key_rows = lax.dynamic_index_in_dim(prompt_keys, which, 0, keepdims=False)
    value_rows = lax.dynamic_index_in_dim(prompt_values, which, 0, keepdims=False)
    allowed = (first_row + jnp.arange(block_rows, dtype=jnp.int32))[:, None] >= jnp.arange(PLEN, dtype=jnp.int32)[None, :]
    return attend(query_rows, key_rows, value_rows, allowed)

def cont_block(query_rows, own_keys, own_values, which, prompt_keys, prompt_values):
    key_rows = jnp.concatenate([lax.dynamic_index_in_dim(prompt_keys, which, 0, keepdims=False), own_keys], axis=0)
    value_rows = jnp.concatenate([lax.dynamic_index_in_dim(prompt_values, which, 0, keepdims=False), own_values], axis=0)
    causal = jnp.arange(CLEN, dtype=jnp.int32)[:, None] >= jnp.arange(CLEN, dtype=jnp.int32)[None, :]
    allowed = jnp.concatenate([jnp.ones((CLEN, PLEN), dtype=bool), causal], axis=1)
    return attend(query_rows, key_rows, value_rows, allowed)

def row_forward(token_rows, member_row, params):
    norm_gain, norm_shift, query_w, query_b, key_w, key_b, value_w, value_b, dense_w, dense_b, expand_w, expand_b, shrink_w, shrink_b = params
    row_count = token_rows.shape[0]
    prompt_total = GPR * PLEN
    token_index = jnp.arange(row_count, dtype=jnp.int32)
    positions = jnp.where(token_index < prompt_total, token_index % PLEN, PLEN + (token_index - prompt_total) % CLEN)
    cosine, sine_table = rotary_tables(positions)
    hidden = low(layer_norm(token_rows, norm_gain, norm_shift))

    def project(weight_matrix, bias_row):
        return jnp.dot(hidden, weight_matrix, precision=lax.Precision.HIGHEST) + bias_row
    queries = low(rotate_heads(low_back(project(query_w, query_b)).reshape(row_count, HEADS, HDIM), cosine, sine_table))
    key_rows = low(rotate_heads(low_back(project(key_w, key_b)).reshape(row_count, HEADS, HDIM), cosine, sine_table))
    values = low(low_back(project(value_w, value_b))).reshape(row_count, HEADS, HDIM)
    prompt_queries = queries[:prompt_total].reshape(GPR, PLEN, HEADS, HDIM)
    prompt_keys = key_rows[:prompt_total].reshape(GPR, PLEN, HEADS, HDIM)
    prompt_values = values[:prompt_total].reshape(GPR, PLEN, HEADS, HDIM)
    per_prompt = PLEN // min(512, PLEN)
    checked_prompt = jax.checkpoint(prompt_block)
    prompt_out = lax.map(lambda element: checked_prompt(element, prompt_queries, prompt_keys, prompt_values), jnp.arange(GPR * per_prompt, dtype=jnp.int32))
    prompt_out = prompt_out.reshape(prompt_total, HEADS, HDIM)
    cont_queries = queries[prompt_total:].reshape(CONTS, CLEN, HEADS, HDIM)
    cont_keys = key_rows[prompt_total:].reshape(CONTS, CLEN, HEADS, HDIM)
    cont_values = values[prompt_total:].reshape(CONTS, CLEN, HEADS, HDIM)
    checked_cont = jax.checkpoint(cont_block)
    cont_out = lax.map(lambda element: checked_cont(element[0], element[1], element[2], element[3], prompt_keys, prompt_values), (cont_queries, cont_keys, cont_values, member_row))
    cont_out = cont_out.reshape(row_count - prompt_total, HEADS, HDIM)
    attended = low_back(low(jnp.concatenate([prompt_out, cont_out], axis=0).reshape(row_count, HEADS * HDIM)))
    expand = low_back(project(expand_w, expand_b))
    activated = low(jax.nn.gelu(expand, approximate=True))
    attn_branch = jnp.dot(attended, dense_w, precision=lax.Precision.HIGHEST) + dense_b
    mlp_branch = jnp.dot(activated, shrink_w, precision=lax.Precision.HIGHEST) + shrink_b
    return token_rows + attn_branch + mlp_branch

def reference(tokens, cotangent, membership, ln_gain, ln_bias, w_query, b_query, w_key, b_key, w_value, b_value, w_dense, b_dense, w_fc1, b_fc1, w_fc2, b_fc2):
    params = tuple((element.astype(jnp.float32) for element in (ln_gain, ln_bias, w_query, b_query, w_key, b_key, w_value, b_value, w_dense, b_dense, w_fc1, b_fc1, w_fc2, b_fc2)))
    inputs = tokens.astype(jnp.float32).reshape(N_DP, -1, D)
    seeds = cotangent.astype(jnp.float32).reshape(N_DP, -1, D)
    checked_row = jax.checkpoint(row_forward)

    def whole(inputs, params):

        def step(running, element):
            return (running, checked_row(element[0], element[1], params))
        _, result = lax.scan(step, jnp.float32(0.0), (inputs, membership))
        return result
    result, pullback = jax.vjp(whole, inputs, params)
    grad_inputs, grads = pullback(seeds)
    grad_gain, grad_shift, grad_wq, grad_bq, grad_wk, grad_bk, grad_wv, grad_bv, grad_wd, grad_bd, grad_w1, grad_b1, grad_w2, grad_b2 = grads
    return (result.reshape(-1, D).astype(jnp.bfloat16), grad_inputs.reshape(-1, D), grad_gain, grad_shift, grad_wq, grad_bq, grad_wk, grad_bk, grad_wv, grad_bv, grad_wd, grad_bd, grad_w1, grad_b1, grad_w2, grad_b2)
```

```python
import functools

import jax
import jax.numpy as jnp
from jax import lax
from jax.experimental import pallas as pl
from jax.experimental.pallas import tpu as pltpu
from jax.sharding import PartitionSpec as P

HDIM = 64
ROT = 32
PLEN = 2048
CLEN = 256
GPR = 2
ROWS_OUT = 1024
VMEM = 56 * 2**20
F32 = jnp.float32
BF16 = jnp.bfloat16
NT = (((1,), (1,)), ((), ()))
NN = (((1,), (0,)), ((), ()))


def dot(left, right, dims):
    return lax.dot_general(left, right, dims, preferred_element_type=F32)


def transpose_dot(left, right):
    return jnp.einsum("ra,rb->ab", left, right, preferred_element_type=F32)


def dot_back(left, right):
    return jnp.einsum("rb,ab->ra", left, right, preferred_element_type=F32)


def norm_apply(matrix, norm_gain, norm_shift):
    center = matrix - jnp.mean(matrix, axis=-1, keepdims=True)
    spread = jnp.mean(center * center, axis=-1, keepdims=True)
    return center * lax.rsqrt(spread + 1e-05) * norm_gain + norm_shift


def gelu_tanh(inputs):
    return jax.nn.gelu(inputs, approximate=True)


def rotary_tables():
    half = ROT // 2
    positions = jnp.arange(PLEN + CLEN, dtype=F32)
    frequency = 10000.0 ** (-2.0 * jnp.arange(half, dtype=F32) / ROT)
    angles = positions[:, None] * frequency[None, :]
    cosine, sine = jnp.cos(angles), jnp.sin(angles)
    ones = jnp.ones((PLEN + CLEN, HDIM - ROT), F32)
    zeros = jnp.zeros_like(ones)
    none = jnp.zeros_like(sine)
    head = (
        jnp.concatenate([cosine, cosine, ones], axis=1),
        jnp.concatenate([-sine, none, zeros], axis=1),
        jnp.concatenate([none, sine, zeros], axis=1),
    )
    return tuple(jnp.concatenate([table, table], axis=1) for table in head)


def rotated(values, cosine, first, second):
    half = ROT // 2
    return (
        values * cosine
        + pltpu.roll(values, 2 * HDIM - half, 1) * first
        + pltpu.roll(values, half, 1) * second
    )


def qkv_kernel(
    share, where_ref, x_ref, gain_ref, shift_ref, weight_ref, bias_ref, cos_ref, first_ref,
    second_ref, hidden_ref, out_ref,
):
    x = x_ref[...].astype(F32)
    hidden = norm_apply(x, gain_ref[...], shift_ref[...]).astype(BF16)
    hidden_ref[...] = hidden
    cosine, first, second = cos_ref[...], first_ref[...], second_ref[...]
    lane = lax.broadcasted_iota(jnp.int32, (1, 2 * HDIM), 1)
    for begin in range(0, out_ref.shape[1], 512):
        lin = dot(hidden, weight_ref[:, begin : begin + 512], NN) + bias_ref[:, begin : begin + 512]
        for column in range(0, 512, 2 * HDIM):
            part = lin[:, column : column + 2 * HDIM]
            turns = [((begin + column + off) // share) % 3 < 2 for off in (0, HDIM)]
            if any(turns):
                turned = rotated(part, cosine, first, second)
                if not all(turns):
                    keep = lane < HDIM if turns[0] else lane >= HDIM
                    turned = jnp.where(keep, turned, part)
                part = turned
            out_ref[:, begin + column : begin + column + 2 * HDIM] = part.astype(BF16)


def qkv_project(x, gain, shift, weight, bias, tables, spots, share):
    rows, width = x.shape
    outs = weight.shape[1]
    count = 256
    whole = lambda shape: pl.BlockSpec(shape, lambda i, *_: (0, 0))
    table = pl.BlockSpec((count, 2 * HDIM), lambda i, spots: (spots[i], 0))
    return pl.pallas_call(
        functools.partial(qkv_kernel, share),
        grid_spec=pltpu.PrefetchScalarGridSpec(
            num_scalar_prefetch=1,
            grid=(rows // count,),
            in_specs=[
                pl.BlockSpec((count, width), lambda i, *_: (i, 0)),
                whole((1, width)),
                whole((1, width)),
                whole((width, outs)),
                whole((1, outs)),
                table,
                table,
                table,
            ],
            out_specs=[
                pl.BlockSpec((count, width), lambda i, *_: (i, 0)),
                pl.BlockSpec((count, outs), lambda i, *_: (i, 0)),
            ],
        ),
        out_shape=[
            jax.ShapeDtypeStruct((rows, width), BF16),
            jax.ShapeDtypeStruct((rows, outs), BF16),
        ],
        compiler_params=pltpu.CompilerParams(vmem_limit_bytes=VMEM),
        cost_estimate=pl.CostEstimate(
            flops=2 * rows * width * outs, bytes_accessed=2 * rows * (2 * width + outs),
            transcendentals=0,
        ),
        name="qkv_project",
    )(spots, x, gain, shift, weight, bias, *tables)


def heads_split(array, heads):
    if heads == 1:
        return [array]
    lane = lax.broadcasted_iota(jnp.int32, array.shape, 1)
    return [jnp.where(lane // HDIM == h, array, jnp.zeros((), array.dtype)) for h in range(heads)]


def near_mask():
    key = lax.broadcasted_iota(jnp.int32, (CLEN, CLEN), 0)
    query = lax.broadcasted_iota(jnp.int32, (CLEN, CLEN), 1)
    return key <= query


def over_far(base, count, big, step):
    per = big // CLEN
    full = count // per

    @pl.loop(0, full)
    def _(i):
        step(pl.multiple_of(base + i * big, CLEN), big)

    @pl.loop(full * per, count)
    def _(i):
        step(pl.multiple_of(base + i * CLEN, CLEN), CLEN)


def attend_kernel(
    big, group_ref, far_ref, q_ref, ko_ref, vo_ref, kp_ref, vp_ref, o_ref, ot_ref, lse_ref,
    vt_s, m_s, l_s, acc_s,
):
    heads = q_ref.shape[1] // HDIM
    item = pl.program_id(1)
    base = group_ref[item] * PLEN

    @pl.when(item == 0)
    def _():
        @pl.loop(0, vp_ref.shape[0] // CLEN)
        def _(i):
            rows = pl.ds(pl.multiple_of(i * CLEN, CLEN), CLEN)
            vt_s[:, rows] = vp_ref[rows, :].T

    queries = heads_split(q_ref[...] * BF16(HDIM**-0.5), heads)
    mask = near_mask()
    keys = ko_ref[...]
    values = vo_ref[...].T
    spans = [slice(h * HDIM, (h + 1) * HDIM) for h in range(heads)]
    scores = [dot(keys, queries[h], NT) for h in range(heads)]
    for h in range(heads):
        s = jnp.where(mask, scores[h], -1e30)
        m = jnp.max(s, axis=0, keepdims=True)
        p = jnp.exp(s - m)
        m_s[h] = m
        l_s[h] = jnp.sum(p, axis=0, keepdims=True)
        acc_s[h] = dot(values[spans[h]], p.astype(BF16), NN)

    def step(first, size):
        k = kp_ref[pl.ds(first, size), :]
        scores = [dot(k, queries[h], NT) for h in range(heads)]
        for h in range(heads):
            old = m_s[h]
            m = jnp.maximum(old, jnp.max(scores[h], axis=0, keepdims=True))
            p = jnp.exp(scores[h] - m)
            a = jnp.exp(old - m)
            m_s[h] = m
            l_s[h] = l_s[h] * a + jnp.sum(p, axis=0, keepdims=True)
            acc_s[h] = acc_s[h] * a + dot(vt_s[spans[h], pl.ds(first, size)], p.astype(BF16), NN)

    over_far(base, far_ref[item], big, step)
    for h in range(heads):
        ot_ref[spans[h], :] = acc_s[h] * (1.0 / l_s[h])
        lse_ref[0, h : h + 1, :] = m_s[h] + jnp.log(l_s[h])
    o_ref[...] = ot_ref[...].T.astype(BF16)


def attend_back_kernel(
    big, group_ref, far_ref, spot_ref, q_ref, ko_ref, vo_ref, do_ref, ot_ref, lse_ref, kp_ref,
    vp_ref, cos_ref, first_ref, second_ref, dq_ref, dk_ref, dv_ref, kt_s, dq_s, dk_s, dv_s,
):
    width = q_ref.shape[1]
    heads = width // HDIM
    item = pl.program_id(1)
    base = group_ref[item] * PLEN

    @pl.when(item == 0)
    def _():
        dk_s[...] = jnp.zeros_like(dk_s)
        dv_s[...] = jnp.zeros_like(dv_s)

        @pl.loop(0, kp_ref.shape[0] // CLEN)
        def _(i):
            rows = pl.ds(pl.multiple_of(i * CLEN, CLEN), CLEN)
            kt_s[:, rows] = kp_ref[rows, :].T

    do = do_ref[...]
    queries = heads_split(q_ref[...] * BF16(HDIM**-0.5), heads)
    grads = heads_split(do, heads)
    query_cat = jnp.concatenate(queries, axis=0)
    grad_cat = jnp.concatenate(grads, axis=0)
    spans = [slice(h * HDIM, (h + 1) * HDIM) for h in range(heads)]
    product = ot_ref[...] * do.astype(F32).T
    center = [jnp.sum(product[span], axis=0, keepdims=True) for span in spans]
    lse = [lse_ref[0, h : h + 1, :] for h in range(heads)]
    mask = near_mask()

    def piece(k, v, kt, row, size, near):
        chance, grad_scores = [], []
        scores = [dot(k, queries[h], NT) for h in range(heads)]
        grad_chance = [dot(v, grads[h], NT) for h in range(heads)]
        for h in range(heads):
            p = jnp.exp(scores[h] - lse[h])
            if near:
                p = jnp.where(mask, p, 0.0)
            grad_scores.append((p * (grad_chance[h] - center[h])).astype(BF16))
            chance.append(p.astype(BF16))
        for h in range(heads):
            step = dot(kt(spans[h]), grad_scores[h], NN)
            if near:
                dq_s[spans[h], :] = step
            else:
                dq_s[spans[h], :] += step
        dk_s[pl.ds(row, size), :] += dot(jnp.concatenate(grad_scores, axis=1), query_cat, NN)
        dv_s[pl.ds(row, size), :] += dot(jnp.concatenate(chance, axis=1), grad_cat, NN)

    own = ko_ref[...]
    own_t = own.T
    piece(
        own, vo_ref[...], lambda span: own_t[span], pl.multiple_of(item * CLEN, CLEN), CLEN, True
    )

    def step(first, size):
        rows = pl.ds(first, size)
        piece(kp_ref[rows, :], vp_ref[rows, :], lambda span: kt_s[span, rows], first, size, False)

    over_far(base, far_ref[item], big, step)

    def turned_back(values, spot):
        rows = pl.ds(pl.multiple_of(spot * CLEN, CLEN), CLEN)
        wide = 2 * HDIM
        if width < wide:
            values = jnp.concatenate([values, values], axis=1)
        parts = [
            rotated(
                values[:, c : c + wide], cos_ref[rows, :], -first_ref[rows, :], -second_ref[rows, :]
            )
            for c in range(0, values.shape[1], wide)
        ]
        out = parts[0] if len(parts) == 1 else jnp.concatenate(parts, axis=1)
        return out[:, :width].astype(BF16)

    dq_ref[...] = turned_back((dq_s[...] * (HDIM**-0.5)).T, spot_ref[item])

    @pl.when(item == pl.num_programs(1) - 1)
    def _():
        @pl.loop(0, dk_ref.shape[0] // CLEN)
        def _(i):
            rows = pl.ds(pl.multiple_of(i * CLEN, CLEN), CLEN)
            dk_ref[rows, :] = turned_back(dk_s[rows, :], spot_ref[i])
            dv_ref[rows, :] = dv_s[rows, :].astype(BF16)


def attention_specs(rows, width):
    wide = min(4 * HDIM, width)
    heads = wide // HDIM
    block = lambda at: pl.BlockSpec((CLEN, wide), lambda h, i, *_: (i, at + h))
    return (
        wide,
        heads,
        block,
        pl.BlockSpec((wide, CLEN), lambda h, i, *_: (h, i)),
        lambda at: pl.BlockSpec((GPR * PLEN, wide), lambda h, i, *_: (0, at + h)),
        pl.BlockSpec((1, heads, CLEN), lambda h, i, *_: (h, 0, i)),
    )


def split_columns(qkv, width):
    wide = min(4 * HDIM, width)
    if wide % 128 == 0:
        return (qkv, qkv, qkv), tuple(t * width // wide for t in range(3))
    return tuple(qkv[:, t * width : (t + 1) * width] for t in range(3)), (0, 0, 0)


def attend(qkv, width, group, far):
    rows = qkv.shape[0]
    wide, heads, block, turned, prompts, stats = attention_specs(rows, width)
    (q, k, v), (qa, ka, va) = split_columns(qkv, width)
    pairs = rows * (PLEN + CLEN) * width // HDIM
    return pl.pallas_call(
        functools.partial(attend_kernel, 1024),
        grid_spec=pltpu.PrefetchScalarGridSpec(
            num_scalar_prefetch=2,
            grid=(width // wide, rows // CLEN),
            in_specs=[block(qa), block(ka), block(va), prompts(ka), prompts(va)],
            out_specs=[block(0), turned, stats],
            scratch_shapes=[
                pltpu.VMEM((wide, GPR * PLEN), BF16),
                pltpu.VMEM((heads, 1, CLEN), F32),
                pltpu.VMEM((heads, 1, CLEN), F32),
                pltpu.VMEM((heads, HDIM, CLEN), F32),
            ],
        ),
        out_shape=[
            jax.ShapeDtypeStruct((rows, width), BF16),
            jax.ShapeDtypeStruct((width, rows), F32),
            jax.ShapeDtypeStruct((width // wide, heads, rows), F32),
        ],
        compiler_params=pltpu.CompilerParams(vmem_limit_bytes=VMEM),
        cost_estimate=pl.CostEstimate(
            flops=4 * pairs * 256, bytes_accessed=rows * width * 12, transcendentals=pairs
        ),
        name="attend",
    )(group, far, q, k, v, k, v)


def attend_back(qkv, width, grad, turned_out, lse, tables, group, far, spots):
    rows = qkv.shape[0]
    wide, heads, block, turned, prompts, stats = attention_specs(rows, width)
    (q, k, v), (qa, ka, va) = split_columns(qkv, width)
    table = pl.BlockSpec(tables[0].shape, lambda h, i, *_: (0, 0))
    column = pl.BlockSpec((rows, wide), lambda h, i, *_: (0, h))
    pairs = rows * (PLEN + CLEN) * width // HDIM
    return pl.pallas_call(
        functools.partial(attend_back_kernel, 1024),
        grid_spec=pltpu.PrefetchScalarGridSpec(
            num_scalar_prefetch=3,
            grid=(width // wide, rows // CLEN),
            in_specs=[
                block(qa), block(ka), block(va), block(0), turned, stats, prompts(ka), prompts(va),
                table, table, table,
            ],
            out_specs=[block(0), column, column],
            scratch_shapes=[
                pltpu.VMEM((wide, GPR * PLEN), BF16),
                pltpu.VMEM((wide, CLEN), F32),
                pltpu.VMEM((rows, wide), F32),
                pltpu.VMEM((rows, wide), F32),
            ],
        ),
        out_shape=[jax.ShapeDtypeStruct((rows, width), BF16)] * 3,
        compiler_params=pltpu.CompilerParams(vmem_limit_bytes=VMEM),
        cost_estimate=pl.CostEstimate(
            flops=8 * pairs * 256, bytes_accessed=rows * width * 24, transcendentals=pairs
        ),
        name="attend_back",
    )(group, far, spots, q, k, v, grad, turned_out, lse, k, v, *tables)


def tp_sum(part, extra=None):
    total = lax.psum(part, "tp").astype(F32)
    if extra is not None:
        total = total + extra[0].astype(F32) + extra[1]
    return total.astype(BF16)


def body(
    tokens, cotangent, membership, ln_gain, ln_bias, w_query, b_query, w_key, b_key, w_value,
    b_value, w_dense, b_dense, w_fc1, b_fc1, w_fc2, b_fc2,
):
    rows, width = tokens.shape
    ctx_count = lax.axis_size("ctx")
    ctx_index = lax.axis_index("ctx")
    local = w_query.shape[1]
    share = local // ctx_count

    def mixed(query, key, value):
        lead = query.shape[:-1]
        stacked = jnp.stack(
            [a.reshape(*lead, ctx_count, share) for a in (query, key, value)], axis=-2
        )
        return stacked.reshape(*lead, 3 * local)

    gather = functools.partial(lax.all_gather, axis_name=("dp", "ctx"), tiled=True)
    qkv_weight = gather(mixed(w_query, w_key, w_value), axis=0)
    dense_weight = gather(w_dense, axis=1)
    expand_weight = gather(w_fc1, axis=0)
    shrink_weight = gather(w_fc2, axis=1)
    qkv_bias = mixed(b_query, b_key, b_value).astype(F32)[None]

    per_prompt = PLEN // CLEN
    prompt_items = GPR * per_prompt
    all_items = rows * ctx_count // CLEN
    items = jnp.arange(all_items, dtype=jnp.int32)
    spots = jnp.where(items < prompt_items, items % per_prompt, per_prompt)
    far = spots
    group = jnp.concatenate([items[:prompt_items] // per_prompt, membership[0]])
    own_spots = lax.dynamic_slice_in_dim(spots, ctx_index * (rows // CLEN), rows // CLEN)
    tables = rotary_tables()

    gain = ln_gain.astype(F32)
    shift = ln_bias.astype(F32)
    hidden, qkv = qkv_project(
        tokens, gain[None], shift[None], qkv_weight, qkv_bias, tables, own_spots, share
    )
    swap = functools.partial(lax.all_to_all, axis_name="ctx", tiled=True)
    qkv_all = swap(qkv, split_axis=1, concat_axis=0)
    grad_attended = dot_back(cotangent, dense_weight).astype(BF16)
    grad_all = swap(grad_attended, split_axis=1, concat_axis=0)

    out_all, turned_out, lse = attend(qkv_all, share, group, far)
    attended = swap(out_all, split_axis=0, concat_axis=1)
    grads_all = attend_back(
        qkv_all, share, grad_all, turned_out, lse, tables, group, far, spots
    )
    grad_qkv = swap(jnp.concatenate(grads_all, axis=1), split_axis=0, concat_axis=1)

    expand_lin = jnp.dot(hidden, expand_weight, preferred_element_type=F32) + b_fc1.astype(F32)
    activated = gelu_tanh(expand_lin).astype(BF16)
    _, gelu_pull = jax.vjp(gelu_tanh, expand_lin)
    grad_expand = gelu_pull(dot_back(cotangent, shrink_weight))[0].astype(BF16)

    blocks = rows // ROWS_OUT
    cut = lambda array, i: array[i * ROWS_OUT : (i + 1) * ROWS_OUT]
    biases = b_dense.astype(F32) + b_fc2.astype(F32)
    outs = []
    for i in range(blocks):
        part = jnp.dot(cut(attended, i), dense_weight, preferred_element_type=F32) + jnp.dot(
            cut(activated, i), shrink_weight, preferred_element_type=F32
        )
        outs.append(tp_sum(part.astype(BF16), (cut(tokens, i), biases)))
    layer_out = jnp.concatenate(outs, axis=0)

    sums = []
    for i in range(blocks):
        part = dot_back(cut(grad_expand, i), expand_weight) + dot_back(cut(grad_qkv, i), qkv_weight)
        sums.append(tp_sum(part.astype(BF16)))
    hidden_total = jnp.concatenate(sums, axis=0).astype(F32)
    _, norm_pull = jax.vjp(norm_apply, tokens.astype(F32), gain, shift)
    grad_x, grad_gain, grad_shift = norm_pull(hidden_total)
    grad_tokens = cotangent.astype(F32) + grad_x

    small = (
        grad_gain,
        grad_shift,
        jnp.sum(grad_qkv.astype(F32), axis=0),
        jnp.sum(grad_expand.astype(F32), axis=0),
        jnp.sum(cotangent.astype(F32), axis=0),
    )
    sizes = [array.shape[0] for array in small]
    packed = lax.psum(jnp.concatenate(small), ("dp", "ctx"))
    ends = [sum(sizes[: i + 1]) for i in range(len(sizes))]
    gain_sum, shift_sum, qkv_sum, expand_sum, out_sum = (
        packed[end - size : end] for end, size in zip(ends, sizes)
    )

    def scatter(array, axis):
        summed = lax.psum_scatter(
            array.astype(BF16), ("dp", "ctx"), scatter_dimension=axis, tiled=True
        )
        return summed.astype(F32)

    def unmixed(array):
        lead = array.shape[:-1]
        parts = array.reshape(*lead, ctx_count, 3, share)
        return tuple(parts[..., t, :].reshape(*lead, local) for t in range(3))

    grad_query, grad_key, grad_value = unmixed(scatter(transpose_dot(hidden, grad_qkv), 0))
    grad_dense = scatter(transpose_dot(attended, cotangent), 1)
    grad_fc1 = scatter(transpose_dot(hidden, grad_expand), 0)
    grad_fc2 = scatter(transpose_dot(activated, cotangent), 1)
    sum_query, sum_key, sum_value = unmixed(qkv_sum)
    return (
        layer_out, grad_tokens, gain_sum, shift_sum, grad_query, sum_query, grad_key, sum_key,
        grad_value, sum_value, grad_dense, out_sum, grad_fc1, expand_sum, grad_fc2, out_sum,
    )


def solution(mesh):
    rows = P(("dp", "ctx"), None)
    down, across = P(("dp", "ctx"), "tp"), P("tp", ("dp", "ctx"))
    wide = P("tp")
    ins = (
        rows, rows, P("dp", None), P(), P(), down, wide, down, wide, down, wide, across, P(), down,
        wide, across, P(),
    )
    outs = (
        rows, rows, P(), P(), down, wide, down, wide, down, wide, across, P(), down, wide, across,
        P(),
    )
    return jax.shard_map(body, mesh=mesh, in_specs=ins, out_specs=outs, check_vma=False)
```

```python
import functools

import jax
import jax.numpy as jnp
from jax import lax
from jax.experimental import pallas as pl
from jax.experimental.pallas import tpu as pltpu
from jax.sharding import PartitionSpec as P

HDIM = 64
ROT = 32
PLEN = 2048
CLEN = 256
GPR = 2
BLOCK = 1024
VMEM = 56 * 2**20
F32 = jnp.float32
BF16 = jnp.bfloat16
NT = (((1,), (1,)), ((), ()))
NN = (((1,), (0,)), ((), ()))


def dot(left, right, dims):
    return lax.dot_general(left, right, dims, preferred_element_type=F32)


def transpose_dot(left, right):
    return jnp.einsum("ra,rb->ab", left, right, preferred_element_type=F32)


def dot_back(left, right):
    return jnp.einsum("rb,ab->ra", left, right, preferred_element_type=F32)


def norm_apply(matrix, norm_gain, norm_shift):
    center = matrix - jnp.mean(matrix, axis=-1, keepdims=True)
    spread = jnp.mean(center * center, axis=-1, keepdims=True)
    return center * lax.rsqrt(spread + 1e-05) * norm_gain + norm_shift


def gelu_parts(v):
    scale = (2.0 / jnp.pi) ** 0.5
    t = jnp.tanh(scale * (v + 0.044715 * v * v * v))
    value = 0.5 * v * (1.0 + t)
    slope = 0.5 * (1.0 + t) + 0.5 * v * (1.0 - t * t) * (scale * (1.0 + 3 * 0.044715 * v * v))
    return value, slope


def rotary_tables():
    half = ROT // 2
    positions = jnp.arange(PLEN + CLEN, dtype=F32)
    frequency = 10000.0 ** (-2.0 * jnp.arange(half, dtype=F32) / ROT)
    angles = positions[:, None] * frequency[None, :]
    cosine, sine = jnp.cos(angles), jnp.sin(angles)
    ones = jnp.ones((PLEN + CLEN, HDIM - ROT), F32)
    zeros = jnp.zeros_like(ones)
    none = jnp.zeros_like(sine)
    head = (
        jnp.concatenate([cosine, cosine, ones], axis=1),
        jnp.concatenate([-sine, none, zeros], axis=1),
        jnp.concatenate([none, sine, zeros], axis=1),
    )
    return tuple(jnp.concatenate([table, table], axis=1) for table in head)


def rotated(values, cosine, first, second):
    half = ROT // 2
    return (
        values * cosine
        + pltpu.roll(values, 2 * HDIM - half, 1) * first
        + pltpu.roll(values, half, 1) * second
    )


def qkv_kernel(
    share, where_ref, x_ref, gain_ref, shift_ref, weight_ref, bias_ref, cos_ref, first_ref,
    second_ref, hidden_ref, out_ref,
):
    x = x_ref[...].astype(F32)
    hidden = norm_apply(x, gain_ref[...], shift_ref[...]).astype(BF16)
    hidden_ref[...] = hidden
    cosine, first, second = cos_ref[...], first_ref[...], second_ref[...]
    lane = lax.broadcasted_iota(jnp.int32, (1, 2 * HDIM), 1)
    member_width = out_ref.shape[2]
    for begin in range(0, weight_ref.shape[1], 512):
        lin = dot(hidden, weight_ref[:, begin : begin + 512], NN) + bias_ref[:, begin : begin + 512]
        for column in range(0, 512, 2 * HDIM):
            part = lin[:, column : column + 2 * HDIM]
            turns = [((begin + column + off) // share) % 3 < 2 for off in (0, HDIM)]
            if any(turns):
                turned = rotated(part, cosine, first, second)
                if not all(turns):
                    keep = lane < HDIM if turns[0] else lane >= HDIM
                    turned = jnp.where(keep, turned, part)
                part = turned
            part = part.astype(BF16)
            for off in range(0, 2 * HDIM, min(2 * HDIM, share)):
                size = min(2 * HDIM, share)
                member, place = divmod(begin + column + off, member_width)
                out_ref[member, :, place : place + size] = part[:, off : off + size]


def qkv_project(x, gain, shift, weight, bias, tables, spots, share):
    rows, width = x.shape
    outs = weight.shape[1]
    count = 256
    whole = lambda shape: pl.BlockSpec(shape, lambda i, *_: (0, 0))
    table = pl.BlockSpec((count, 2 * HDIM), lambda i, spots: (spots[i], 0))
    return pl.pallas_call(
        functools.partial(qkv_kernel, share),
        grid_spec=pltpu.PrefetchScalarGridSpec(
            num_scalar_prefetch=1,
            grid=(rows // count,),
            in_specs=[
                pl.BlockSpec((count, width), lambda i, *_: (i, 0)),
                whole((1, width)),
                whole((1, width)),
                whole((width, outs)),
                whole((1, outs)),
                table,
                table,
                table,
            ],
            out_specs=[
                pl.BlockSpec((count, width), lambda i, *_: (i, 0)),
                pl.BlockSpec((outs // (3 * share), count, 3 * share), lambda i, *_: (0, i, 0)),
            ],
        ),
        out_shape=[
            jax.ShapeDtypeStruct((rows, width), BF16),
            jax.ShapeDtypeStruct((outs // (3 * share), rows, 3 * share), BF16),
        ],
        compiler_params=pltpu.CompilerParams(vmem_limit_bytes=VMEM),
        cost_estimate=pl.CostEstimate(
            flops=2 * rows * width * outs, bytes_accessed=2 * rows * (2 * width + outs),
            transcendentals=0,
        ),
        name="qkv_project",
    )(spots, x, gain, shift, weight, bias, *tables)


def expand_kernel(hidden_ref, weight_ref, bias_ref, lin_ref, out_ref):
    hidden = hidden_ref[...]
    for begin in range(0, weight_ref.shape[1], 512):
        at = slice(begin, begin + 512)
        lin = dot(hidden, weight_ref[:, at], NN) + bias_ref[:, at]
        lin_ref[:, at] = lin
        out_ref[:, at] = gelu_parts(lin)[0].astype(BF16)


def shrink_kernel(act_ref, cot_ref, lin_ref, weight_ref, out_ref, grad_ref, sum_ref, cot_sum_ref):
    @pl.when(pl.program_id(0) == 0)
    def _():
        sum_ref[...] = jnp.zeros_like(sum_ref)
        cot_sum_ref[...] = jnp.zeros_like(cot_sum_ref)

    act, cot = act_ref[...], cot_ref[...]
    for begin in range(0, weight_ref.shape[0], 512):
        at = slice(begin, begin + 512)
        slope = gelu_parts(lin_ref[:, at])[1]
        grad = (slope * dot(cot, weight_ref[at, :], NT)).astype(BF16)
        grad_ref[:, at] = grad
        sum_ref[:, at] += jnp.sum(grad.astype(F32), axis=0, keepdims=True)
    for begin in range(0, weight_ref.shape[1], 512):
        at = slice(begin, begin + 512)
        out_ref[:, at] = dot(act, weight_ref[:, at], NN).astype(BF16)
        cot_sum_ref[:, at] += jnp.sum(cot_ref[:, at].astype(F32), axis=0, keepdims=True)


def row_call(kernel, name, count, rows, in_arrays, outs, flops):
    def spec(shape):
        if shape[0] == rows:
            return pl.BlockSpec((count, shape[1]), lambda i: (i, 0))
        return pl.BlockSpec(shape, lambda i: (0, 0))

    return pl.pallas_call(
        kernel,
        grid=(rows // count,),
        in_specs=[spec(a.shape) for a in in_arrays],
        out_specs=[spec(o.shape) for o in outs],
        out_shape=outs,
        compiler_params=pltpu.CompilerParams(vmem_limit_bytes=VMEM),
        cost_estimate=pl.CostEstimate(
            flops=flops,
            bytes_accessed=sum(a.size * a.dtype.itemsize for a in (*in_arrays, *outs)),
            transcendentals=0,
        ),
        name=name,
    )(*in_arrays)


def products_kernel(kinds, has_base, *refs):
    out_ref = refs[-1]
    base_ref = refs[0] if has_base else None
    pairs = refs[has_base:-1]
    count = 256

    @pl.loop(0, out_ref.shape[0] // count)
    def _(i):
        rows = pl.ds(pl.multiple_of(i * count, count), count)
        total = base_ref[rows, :].astype(F32) if has_base else None
        for n, dims in enumerate(kinds):
            step = dot(pairs[2 * n][rows, :], pairs[2 * n + 1][...], dims)
            total = step if total is None else total + step
        out_ref[rows, :] = total.astype(BF16)


def products(count, outs, base, pairs, name):
    tile = 512
    arrays, specs, kinds = [], [], []
    flops = 0
    if base is not None:
        arrays.append(base[0])
        specs.append(pl.BlockSpec((count, tile), lambda n, at=base[1]: (at, n)))
    for left, at, right, right_at in pairs:
        depth = left.shape[1]
        arrays += [left, right]
        specs.append(pl.BlockSpec((count, depth), lambda n, at=at: (at, 0)))
        if right_at is None:
            specs.append(pl.BlockSpec((tile, depth), lambda n: (n, 0)))
            kinds.append(NT)
        else:
            specs.append(pl.BlockSpec((depth, tile), lambda n, at=right_at: (at, n)))
            kinds.append(NN)
        flops += 2 * count * depth * outs
    return pl.pallas_call(
        functools.partial(products_kernel, kinds, base is not None),
        grid=(outs // tile,),
        in_specs=specs,
        out_specs=pl.BlockSpec((count, tile), lambda n: (0, n)),
        out_shape=jax.ShapeDtypeStruct((count, outs), BF16),
        compiler_params=pltpu.CompilerParams(vmem_limit_bytes=VMEM),
        cost_estimate=pl.CostEstimate(
            flops=flops, bytes_accessed=flops // 512, transcendentals=0
        ),
        name=name,
    )(*arrays)


def heads_split(array, heads):
    if heads == 1:
        return [array]
    lane = lax.broadcasted_iota(jnp.int32, array.shape, 1)
    return [jnp.where(lane // HDIM == h, array, jnp.zeros((), array.dtype)) for h in range(heads)]


def near_mask():
    key = lax.broadcasted_iota(jnp.int32, (CLEN, CLEN), 0)
    query = lax.broadcasted_iota(jnp.int32, (CLEN, CLEN), 1)
    return key <= query


def over_far(base, count, big, step):
    per = big // CLEN
    full = count // per

    @pl.loop(0, full)
    def _(i):
        step(pl.multiple_of(base + i * big, CLEN), big)

    @pl.loop(full * per, count)
    def _(i):
        step(pl.multiple_of(base + i * CLEN, CLEN), CLEN)


def attend_kernel(
    big, group_ref, far_ref, item_ref, q_ref, ko_ref, vo_ref, kp_ref, vt_s, o_ref, ot_ref,
    lse_ref, m_s, l_s, acc_s,
):
    heads = q_ref.shape[1] // HDIM
    item = item_ref[pl.program_id(1)]
    base = group_ref[item] * PLEN

    queries = heads_split(q_ref[...] * BF16(HDIM**-0.5), heads)
    mask = near_mask()
    keys = ko_ref[...]
    values = vo_ref[...].T
    spans = [slice(h * HDIM, (h + 1) * HDIM) for h in range(heads)]
    scores = [dot(keys, queries[h], NT) for h in range(heads)]
    for h in range(heads):
        s = jnp.where(mask, scores[h], -1e30)
        m = jnp.max(s, axis=0, keepdims=True)
        p = jnp.exp(s - m)
        m_s[h] = m
        l_s[h] = jnp.sum(p, axis=0, keepdims=True)
        acc_s[h] = dot(values[spans[h]], p.astype(BF16), NN)

    def step(first, size):
        k = kp_ref[pl.ds(first, size), :]
        scores = [dot(k, queries[h], NT) for h in range(heads)]
        for h in range(heads):
            old = m_s[h]
            m = jnp.maximum(old, jnp.max(scores[h], axis=0, keepdims=True))
            p = jnp.exp(scores[h] - m)
            a = jnp.exp(old - m)
            m_s[h] = m
            l_s[h] = l_s[h] * a + jnp.sum(p, axis=0, keepdims=True)
            acc_s[h] = acc_s[h] * a + dot(vt_s[spans[h], pl.ds(first, size)], p.astype(BF16), NN)

    over_far(base, far_ref[item], big, step)
    for h in range(heads):
        ot_ref[spans[h], :] = acc_s[h] * (1.0 / l_s[h])
        lse_ref[0, h : h + 1, :] = m_s[h] + jnp.log(l_s[h])
    o_ref[...] = ot_ref[...].T.astype(BF16)


def turn_kernel(k_ref, v_ref, kt_ref, vt_ref):
    kt_ref[...] = k_ref[...].T
    vt_ref[...] = v_ref[...].T


def turn_prompts(qkv, width):
    wide = min(4 * HDIM, width)
    (_, k, v), (_, ka, va) = split_columns(qkv, width)
    block = lambda at: pl.BlockSpec((CLEN, wide), lambda h, i: (i, at + h))
    turned = pl.BlockSpec((wide, CLEN), lambda h, i: (h, i))
    return pl.pallas_call(
        turn_kernel,
        grid=(width // wide, GPR * PLEN // CLEN),
        in_specs=[block(ka), block(va)],
        out_specs=[turned, turned],
        out_shape=[jax.ShapeDtypeStruct((width, GPR * PLEN), BF16)] * 2,
        compiler_params=pltpu.CompilerParams(vmem_limit_bytes=VMEM),
        name="turn_prompts",
    )(k, v)


def turned_back(values, tables):
    width = values.shape[1]
    cosine, first, second = (ref[...] for ref in tables)
    wide = 2 * HDIM
    if width < wide:
        values = jnp.concatenate([values, values], axis=1)
    parts = [
        rotated(values[:, c : c + wide], cosine, -first, -second)
        for c in range(0, values.shape[1], wide)
    ]
    out = parts[0] if len(parts) == 1 else jnp.concatenate(parts, axis=1)
    return out[:, :width].astype(BF16)


def attend_back_kernel(big, first_piece, prompt_items, prompt_count, *refs):
    group_ref, far_ref, item_ref = refs[:3]
    q_ref, ko_ref, vo_ref, do_ref, ot_ref, lse_ref, kp_ref, vp_ref, kt_s = refs[3:12]
    tables = refs[12:15]
    before = () if first_piece else refs[15:17]
    dq_ref, dk_ref, dv_ref, dk_s, dv_s, dq_s, near_k, near_v = refs[15 + len(before) :]
    width = q_ref.shape[1]
    heads = width // HDIM
    turn = pl.program_id(1)
    item = item_ref[turn]
    base = group_ref[item] * PLEN

    @pl.when(turn == 0)
    def _():
        if first_piece:
            dk_s[...] = jnp.zeros_like(dk_s)
            dv_s[...] = jnp.zeros_like(dv_s)
        else:
            dk_s[...] = before[0][...]
            dv_s[...] = before[1][...]

    do = do_ref[...]
    queries = heads_split(q_ref[...] * BF16(HDIM**-0.5), heads)
    grads = heads_split(do, heads)
    query_cat = jnp.concatenate(queries, axis=0)
    grad_cat = jnp.concatenate(grads, axis=0)
    spans = [slice(h * HDIM, (h + 1) * HDIM) for h in range(heads)]
    product = ot_ref[...] * do.astype(F32).T
    center = [jnp.sum(product[span], axis=0, keepdims=True) for span in spans]
    lse = [lse_ref[0, h : h + 1, :] for h in range(heads)]
    mask = near_mask()

    def piece(k, v, kt, near):
        chance, grad_scores = [], []
        scores = [dot(k, queries[h], NT) for h in range(heads)]
        grad_chance = [dot(v, grads[h], NT) for h in range(heads)]
        for h in range(heads):
            p = jnp.exp(scores[h] - lse[h])
            if near:
                p = jnp.where(mask, p, 0.0)
            grad_scores.append((p * (grad_chance[h] - center[h])).astype(BF16))
            chance.append(p.astype(BF16))
        for h in range(heads):
            step = dot(kt(spans[h]), grad_scores[h], NN)
            if near:
                dq_s[spans[h], :] = step
            else:
                dq_s[spans[h], :] += step
        return (
            dot(jnp.concatenate(grad_scores, axis=1), query_cat, NN),
            dot(jnp.concatenate(chance, axis=1), grad_cat, NN),
        )

    own = ko_ref[...]
    own_t = own.T
    near_k[...], near_v[...] = piece(own, vo_ref[...], lambda span: own_t[span], True)

    @pl.when(turn < prompt_count)
    def _():
        rows = pl.ds(pl.multiple_of(item * CLEN, CLEN), CLEN)
        dk_s[rows, :] += near_k[...]
        dv_s[rows, :] += near_v[...]

    @pl.when(turn >= prompt_count)
    def _():
        dk_ref[...] = turned_back(near_k[...], tables)
        dv_ref[...] = near_v[...].astype(BF16)

    def step(first, size):
        rows = pl.ds(first, size)
        k_step, v_step = piece(
            kp_ref[rows, :], vp_ref[rows, :], lambda span: kt_s[span, rows], False
        )
        dk_s[rows, :] += k_step
        dv_s[rows, :] += v_step

    over_far(base, far_ref[item], big, step)
    dq_ref[...] = turned_back((dq_s[...] * (HDIM**-0.5)).T, tables)


def finish_kernel(dk_ref, dv_ref, cos_ref, first_ref, second_ref, ok_ref, ov_ref):
    ok_ref[...] = turned_back(dk_ref[...], (cos_ref, first_ref, second_ref))
    ov_ref[...] = dv_ref[...].astype(BF16)


def finish_prompts(dk, dv, tables):
    rows, width = dk.shape
    wide = min(4 * HDIM, width)
    block = pl.BlockSpec((CLEN, wide), lambda h, i: (i, h))
    table = pl.BlockSpec((CLEN, 2 * HDIM), lambda h, i: (i % (PLEN // CLEN), 0))
    return pl.pallas_call(
        finish_kernel,
        grid=(width // wide, rows // CLEN),
        in_specs=[block, block, table, table, table],
        out_specs=[block, block],
        out_shape=[jax.ShapeDtypeStruct((rows, width), BF16)] * 2,
        compiler_params=pltpu.CompilerParams(vmem_limit_bytes=VMEM),
        name="finish_prompts",
    )(dk, dv, *tables)


def split_columns(qkv, width):
    wide = min(4 * HDIM, width)
    if wide % 128 == 0:
        return (qkv, qkv, qkv), tuple(t * width // wide for t in range(3))
    return tuple(qkv[:, t * width : (t + 1) * width] for t in range(3)), (0, 0, 0)


def attention_specs(width):
    wide = min(4 * HDIM, width)
    heads = wide // HDIM
    return (
        wide,
        heads,
        lambda at: pl.BlockSpec((CLEN, wide), lambda h, i, g, f, items: (items[i], at + h)),
        pl.BlockSpec((CLEN, wide), lambda h, i, *_: (i, h)),
        pl.BlockSpec((wide, CLEN), lambda h, i, *_: (h, i)),
        lambda at: pl.BlockSpec((GPR * PLEN, wide), lambda h, i, *_: (0, at + h)),
        pl.BlockSpec((1, heads, CLEN), lambda h, i, *_: (h, 0, i)),
    )


def attend(qkv, turned_v, width, group, far, items):
    rows = items.shape[0] * CLEN
    wide, heads, picked, block, turned, prompts, stats = attention_specs(width)
    (q, k, v), (qa, ka, va) = split_columns(qkv, width)
    pairs = rows * (PLEN + CLEN) * width // HDIM
    return pl.pallas_call(
        functools.partial(attend_kernel, 1024),
        grid_spec=pltpu.PrefetchScalarGridSpec(
            num_scalar_prefetch=3,
            grid=(width // wide, rows // CLEN),
            in_specs=[
                picked(qa), picked(ka), picked(va), prompts(ka),
                pl.BlockSpec((wide, GPR * PLEN), lambda h, i, *_: (h, 0)),
            ],
            out_specs=[block, turned, stats],
            scratch_shapes=[
                pltpu.VMEM((heads, 1, CLEN), F32),
                pltpu.VMEM((heads, 1, CLEN), F32),
                pltpu.VMEM((heads, HDIM, CLEN), F32),
            ],
        ),
        out_shape=[
            jax.ShapeDtypeStruct((rows, width), BF16),
            jax.ShapeDtypeStruct((width, rows), F32),
            jax.ShapeDtypeStruct((width // wide, heads, rows), F32),
        ],
        compiler_params=pltpu.CompilerParams(vmem_limit_bytes=VMEM),
        cost_estimate=pl.CostEstimate(
            flops=4 * pairs * 256, bytes_accessed=rows * width * 12, transcendentals=pairs
        ),
        name="attend",
    )(group, far, items, q, k, v, k, turned_v)


def attend_back(
    qkv, turned_k, width, grad, turned_out, lse, tables, group, far, items, prompt_count, before
):
    rows = items.shape[0] * CLEN
    wide, heads, picked, block, turned, prompts, stats = attention_specs(width)
    (q, k, v), (qa, ka, va) = split_columns(qkv, width)
    table = pl.BlockSpec((CLEN, 2 * HDIM), lambda h, i, g, f, items: (f[items[i]], 0))
    total = pl.BlockSpec((GPR * PLEN, wide), lambda h, i, *_: (0, h))
    late = pl.BlockSpec((CLEN, wide), lambda h, i, *_: (jnp.maximum(i - prompt_count, 0), h))
    pairs = rows * (PLEN + CLEN) * width // HDIM
    first = not before
    late_rows = rows - prompt_count * CLEN
    return pl.pallas_call(
        functools.partial(attend_back_kernel, 1024, first, GPR * PLEN // CLEN, prompt_count),
        grid_spec=pltpu.PrefetchScalarGridSpec(
            num_scalar_prefetch=3,
            grid=(width // wide, rows // CLEN),
            in_specs=[
                picked(qa), picked(ka), picked(va), picked(0), turned, stats, prompts(ka),
                prompts(va), pl.BlockSpec((wide, GPR * PLEN), lambda h, i, *_: (h, 0)), table, table,
                table,
            ]
            + [total] * len(before),
            out_specs=[block, late, late, total, total],
            scratch_shapes=[
                pltpu.VMEM((wide, CLEN), F32),
                pltpu.VMEM((CLEN, wide), F32),
                pltpu.VMEM((CLEN, wide), F32),
            ],
        ),
        out_shape=[jax.ShapeDtypeStruct((rows, width), BF16)]
        + [jax.ShapeDtypeStruct((late_rows, width), BF16)] * 2
        + [jax.ShapeDtypeStruct((GPR * PLEN, width), F32)] * 2,
        input_output_aliases={} if first else {15: 3, 16: 4},
        compiler_params=pltpu.CompilerParams(vmem_limit_bytes=VMEM),
        cost_estimate=pl.CostEstimate(
            flops=8 * pairs * 256, bytes_accessed=rows * width * 24, transcendentals=pairs
        ),
        name="attend_back",
    )(group, far, items, q, k, v, grad, turned_out, lse, k, v, turned_k, *tables, *before)


def tie(*trees):
    return lax.optimization_barrier(trees)


COUNT = 128


def begin_kernel(names, flag_ref, *refs):
    refs = dict(zip(names, refs))
    outer = flag_ref[0] == 1
    out_ref = refs["out"]

    @pl.when(outer)
    def _():
        out_ref[...] = refs["next"][...] if "next" in refs else jnp.zeros_like(out_ref)

    @pl.when(flag_ref[0] == 0)
    def _():
        if "part" not in refs:
            out_ref[...] = jnp.zeros_like(out_ref)
            return
        total = (
            refs["part"][...].astype(F32)
            + refs["swapped"][...].astype(F32)
            + refs["crossed"][...].astype(F32)
        )
        if "tokens" in refs:
            total = total + refs["tokens"][...].astype(F32) + refs["bias"][...]
        out_ref[...] = total.astype(BF16)


def middle_kernel(names, flag_ref, *refs):
    refs = dict(zip(names, refs))
    outer = flag_ref[0] == 1
    swap_ref = refs["swap"]

    @pl.when(outer)
    def _():
        swap_ref[...] = refs["near"][...] if "near" in refs else jnp.zeros_like(swap_ref)

    @pl.when(flag_ref[0] == 0)
    def _():
        swap_ref[...] = refs["crossed"][...] if "crossed" in refs else jnp.zeros_like(swap_ref)

    if "far" in refs:
        refs["cross"][...] = (
            refs["far"][...].astype(F32) + refs["swapped"][...].astype(F32)
        ).astype(BF16)


def line_call(kernel, flags, rows, width, ins, outs, name):
    steps = rows // COUNT

    def spec(shape, first, who):
        if shape[0] == 1:
            return pl.BlockSpec(shape, lambda i, flag: (0, 0))

        def index(i, flag):
            needed = {"all": 1, "outer": flag[0], "inner": 1 - flag[0]}[who]
            return (first(flag[1], steps) + i * needed, 0)

        return pl.BlockSpec((COUNT, width), index)

    return pl.pallas_call(
        functools.partial(kernel, [i[0] for i in ins] + outs),
        grid_spec=pltpu.PrefetchScalarGridSpec(
            num_scalar_prefetch=1,
            grid=(steps,),
            in_specs=[spec(array.shape, first, who) for _, array, first, who in ins],
            out_specs=[pl.BlockSpec((COUNT, width), lambda i, flag: (i, 0)) for _ in outs],
        ),
        out_shape=[jax.ShapeDtypeStruct((rows, width), BF16) for _ in outs],
        compiler_params=pltpu.CompilerParams(vmem_limit_bytes=VMEM),
        name=name,
    )(flags, *[i[1] for i in ins])


def total_specs(half, width):
    outer = lambda flag: flag[0]
    inner = lambda flag: 1 - flag[0]

    def spec(part, who):
        return pl.BlockSpec((COUNT, width), lambda p, i, flag: (i * who(flag) * (p == part), 0))

    return [spec(0, outer), spec(0, inner), spec(1, outer), spec(1, inner)]


def total_of(flag_ref, refs, keep):
    part = pl.program_id(0)
    for at, ref in enumerate(refs):
        right = (part == at // 2) & (flag_ref[0] == 1 - at % 2)

        @pl.when(right)
        def _(ref=ref):
            keep(ref[...])


def rows_of(block, half):
    steps = half // COUNT

    def index(p, i, flag):
        return ((2 * block + (flag[1] + p) % 2) * steps + i, 0)

    return index


def place_kernel(flag_ref, a, b, c, d, *rest):
    out_ref = rest[-1]

    def keep(value):
        out_ref[...] = value

    total_of(flag_ref, (a, b, c, d), keep)


def place_total(flags, four, block, rows, before):
    half, width = four[0].shape
    return pl.pallas_call(
        place_kernel,
        grid_spec=pltpu.PrefetchScalarGridSpec(
            num_scalar_prefetch=1,
            grid=(2, half // COUNT),
            in_specs=total_specs(half, width)
            + [pl.BlockSpec(memory_space=pl.ANY)] * (before is not None),
            out_specs=pl.BlockSpec((COUNT, width), rows_of(block, half)),
        ),
        out_shape=jax.ShapeDtypeStruct((rows, width), BF16),
        input_output_aliases={} if before is None else {5: 0},
        compiler_params=pltpu.CompilerParams(vmem_limit_bytes=VMEM),
        name="place_total",
    )(flags, *four, *(() if before is None else (before,)))


def norm_back_kernel(flag_ref, a, b, c, d, x_ref, cot_ref, gain_ref, *rest):
    out_ref, gain_sum, shift_sum, held = rest[-4:]

    @pl.when((pl.program_id(0) == 0) & (pl.program_id(1) == 0))
    def _():
        gain_sum[...] = jnp.zeros_like(gain_sum)
        shift_sum[...] = jnp.zeros_like(shift_sum)

    def keep(value):
        held[...] = value.astype(F32)

    total_of(flag_ref, (a, b, c, d), keep)
    x = x_ref[...].astype(F32)
    center = x - jnp.mean(x, axis=-1, keepdims=True)
    inverse = lax.rsqrt(jnp.mean(center * center, axis=-1, keepdims=True) + 1e-05)
    normed = center * inverse
    total = held[...]
    gain_sum[...] += jnp.sum(total * normed, axis=0, keepdims=True)
    shift_sum[...] += jnp.sum(total, axis=0, keepdims=True)
    scaled = total * gain_ref[...]
    grad = scaled - jnp.mean(scaled, axis=-1, keepdims=True)
    grad = inverse * (grad - normed * jnp.mean(scaled * normed, axis=-1, keepdims=True))
    out_ref[...] = cot_ref[...].astype(F32) + grad


def norm_back(flags, four, block, tokens, cotangent, gain, before):
    half, width = four[0].shape
    row = pl.BlockSpec((1, width), lambda p, i, flag: (0, 0))
    whole = pl.BlockSpec((COUNT, width), rows_of(block, half))
    return pl.pallas_call(
        norm_back_kernel,
        grid_spec=pltpu.PrefetchScalarGridSpec(
            num_scalar_prefetch=1,
            grid=(2, half // COUNT),
            in_specs=total_specs(half, width)
            + [whole, whole, row]
            + [pl.BlockSpec(memory_space=pl.ANY)] * (before is not None),
            out_specs=[whole, row, row],
            scratch_shapes=[pltpu.VMEM((COUNT, width), F32)],
        ),
        out_shape=[
            jax.ShapeDtypeStruct(tokens.shape, F32),
            jax.ShapeDtypeStruct((1, width), F32),
            jax.ShapeDtypeStruct((1, width), F32),
        ],
        input_output_aliases={} if before is None else {8: 0},
        compiler_params=pltpu.CompilerParams(vmem_limit_bytes=VMEM),
        name="norm_back",
    )(flags, *four, tokens, cotangent, gain, *(() if before is None else (before,)))


class Line:
    def __init__(self, flags, tokens, bias):
        self.flags, self.tokens, self.bias = flags, tokens, bias
        self.part = self.near = None
        self.block = -1

    def begin(self, part, with_input):
        zero = lambda side, steps: 0
        near = lambda side, steps: side * steps
        ins = []
        if self.part is not None:
            ins += [
                ("part", self.part, near, "inner"),
                ("swapped", self.swapped, zero, "inner"),
                ("crossed", self.crossed, zero, "inner"),
            ]
            if self.with_input:
                block = self.block
                ins += [
                    ("tokens", self.tokens, lambda side, steps: (2 * block + side) * steps, "inner"),
                    ("bias", self.bias, zero, "all"),
                ]
        if part is not None:
            ins.append(("next", part, lambda side, steps: (1 - side) * steps, "outer"))
        shape = (self.part if part is None else part).shape
        (out,) = line_call(
            begin_kernel, self.flags, shape[0] // 2, shape[1], ins, ["out"], "line_begin"
        )
        had = self.part is not None
        self.part, self.with_input = part, with_input
        self.block += 1
        self.near = out if had else None
        return out, self.near

    def middle(self, swapped, crossed):
        self.first, self.other = swapped, crossed
        ins = []
        if self.part is not None:
            ins += [
                ("near", self.part, lambda side, steps: side * steps, "outer"),
                ("far", self.part, lambda side, steps: (1 - side) * steps, "inner"),
                ("swapped", swapped, lambda side, steps: 0, "inner"),
            ]
        if crossed is not None:
            ins.append(("crossed", crossed, lambda side, steps: 0, "inner"))
        if self.part is None:
            return crossed, None
        return tuple(
            line_call(
                middle_kernel, self.flags, *swapped.shape, ins, ["swap", "cross"], "line_middle"
            )
        )

    def end(self, swapped, crossed):
        self.swapped, self.crossed = swapped, crossed
        if self.near is None:
            return None
        return self.first, self.near, swapped, self.other


def send(swap, cross):
    outer, middle = [(0, 1), (3, 2), (1, 0), (2, 3)], [(1, 2), (2, 1)]
    return (
        None if swap is None else lax.ppermute(swap, "tp", outer),
        None if cross is None else lax.ppermute(cross, "tp", middle),
    )


def body(
    tokens, cotangent, membership, ln_gain, ln_bias, w_query, b_query, w_key, b_key, w_value,
    b_value, w_dense, b_dense, w_fc1, b_fc1, w_fc2, b_fc2,
):
    rows, width = tokens.shape
    ctx_count = lax.axis_size("ctx")
    ctx_index = lax.axis_index("ctx")
    local = w_query.shape[1]
    share = local // ctx_count
    mine = 3 * share
    block = min(BLOCK, rows // 2)
    blocks = rows // block

    def mixed(query, key, value):
        lead = query.shape[:-1]
        stacked = jnp.stack(
            [a.reshape(*lead, ctx_count, share) for a in (query, key, value)], axis=-2
        )
        return stacked.reshape(*lead, 3 * local)

    gather = functools.partial(lax.all_gather, axis_name=("dp", "ctx"), tiled=True)
    qkv_weight = gather(mixed(w_query, w_key, w_value), axis=0)
    expand_weight = gather(w_fc1, axis=0)
    shrink_weight = gather(w_fc2, axis=1)
    dense_weight = gather(w_dense, axis=1)
    qkv_bias = mixed(b_query, b_key, b_value).astype(F32)[None]

    per_prompt = PLEN // CLEN
    prompt_items = GPR * per_prompt
    own_items = rows // CLEN
    items = jnp.arange(own_items * ctx_count, dtype=jnp.int32)
    far = jnp.where(items < prompt_items, items % per_prompt, per_prompt)
    group = jnp.concatenate([items[:prompt_items] // per_prompt, membership[0]])
    own_spots = lax.dynamic_slice_in_dim(far, ctx_index * own_items, own_items)
    tables = rotary_tables()
    per_block = block // CLEN
    item_table = items.reshape(ctx_count, blocks, per_block)
    piece_items = [item_table[:, b].reshape(-1) for b in range(blocks)]
    prompt_count = ctx_count // 2 * per_block

    gain = ln_gain.astype(F32)
    shift = ln_bias.astype(F32)
    hidden, qkv = qkv_project(
        tokens, gain[None], shift[None], qkv_weight, qkv_bias, tables, own_spots, share
    )

    def exchange(parts):
        if ctx_count == 2:
            low = ctx_index == 0
            away = jnp.where(low, parts[1], parts[0])
            stay = jnp.where(low, parts[0], parts[1])
            came = lax.ppermute(away, "ctx", [(0, 1), (1, 0)])
            return [jnp.where(low, stay, came), jnp.where(low, came, stay)]
        came = lax.all_to_all(jnp.stack(parts), "ctx", split_axis=0, concat_axis=0, tiled=True)
        return [came[c] for c in range(ctx_count)]

    def swap_whole(array):
        swapped = lax.all_to_all(array, "ctx", split_axis=0, concat_axis=0, tiled=True)
        return swapped.reshape(-1, array.shape[-1])

    qkv_all = swap_whole(qkv)
    cut = lambda array, i: array[i * block : (i + 1) * block]

    expand_lin, activated = row_call(
        expand_kernel, "expand", 256, rows, (hidden, expand_weight, b_fc1.astype(F32)[None]),
        (
            jax.ShapeDtypeStruct((rows, expand_weight.shape[1]), F32),
            jax.ShapeDtypeStruct((rows, expand_weight.shape[1]), BF16),
        ),
        2 * rows * width * expand_weight.shape[1],
    )
    mlp_out, grad_expand, expand_sum, cot_sum = row_call(
        shrink_kernel, "shrink", 256, rows, (activated, cotangent, expand_lin, shrink_weight),
        (
            jax.ShapeDtypeStruct((rows, width), BF16),
            jax.ShapeDtypeStruct(activated.shape, BF16),
            jax.ShapeDtypeStruct((1, activated.shape[1]), F32),
            jax.ShapeDtypeStruct((1, width), F32),
        ),
        4 * rows * width * expand_weight.shape[1],
    )
    _, cot_late = tie(hidden, cotangent)
    grad_att = jnp.stack(
        [
            dot_back(cot_late, dense_weight[c * share : (c + 1) * share]).astype(BF16)
            for c in range(ctx_count)
        ]
    )
    grad_all = swap_whole(grad_att)
    qkv_all, mlp_out, grad_att = tie(qkv_all, mlp_out, grad_att)
    turned_k, turned_v = turn_prompts(qkv_all, share)

    place = lax.axis_index("tp")
    flags = jnp.stack([((place == 0) | (place == 3)).astype(jnp.int32), place // 2])
    gain_row = gain[None]

    env = {}

    def forward(b):
        def run(qkv_in, turned_in):
            return attend(qkv_in, turned_in, share, group, far, piece_items[b])

        def keep(out):
            o, env["turned", b], env["lse", b] = out
            env["attended", b] = exchange([cut(o, c) for c in range(ctx_count)])

        return run, (qkv_all, turned_v), keep

    def out_part(b):
        def run(mlp, weight, *heads_out):
            pairs = [(part, 0, weight, c) for c, part in enumerate(heads_out)]
            return products(block, width, (mlp, b), pairs, "out_part")

        def keep(out):
            env["part", b] = out

        return run, (mlp_out, dense_weight, *env["attended", b]), keep

    def backward(b):
        before = () if b == 0 else env["totals"]

        def run(qkv_in, turned_in, grad_in, turned, lse, *before):
            return attend_back(
                qkv_in, turned_in, share, grad_in, turned, lse, tables, group, far, piece_items[b],
                prompt_count, before,
            )

        def keep(out):
            env["dq", b], env["dk", b], env["dv", b] = out[:3]
            env["totals"] = out[3:]

        return run, (qkv_all, turned_k, grad_all, env["turned", b], env["lse", b], *before), keep

    def finish():
        def run(dk, dv):
            return finish_prompts(dk, dv, tables)

        def keep(out):
            env["prompt_grads"] = [array.reshape(ctx_count // 2, rows, share) for array in out]

        return run, env["totals"], keep

    def give_back(b):
        def run(prompts, dq, dk, dv):
            parts = []
            for c in range(ctx_count):
                at = c - ctx_count // 2
                near = slice(b * block, (b + 1) * block)
                key = prompts[0][c, near] if at < 0 else cut(dk, at)
                value = prompts[1][c, near] if at < 0 else cut(dv, at)
                parts.append(jnp.concatenate([cut(dq, c), key, value], axis=1))
            return jnp.concatenate(exchange(parts), axis=1)

        def keep(out):
            env["grad_qkv", b] = out

        return run, (env["prompt_grads"], env["dq", b], env["dk", b], env["dv", b]), keep

    def grad_part(b):
        def run(grad_exp, exp_weight, grad, weight):
            pairs = [(grad_exp, b, exp_weight, None), (grad, 0, weight, None)]
            return products(block, width, None, pairs, "grad_part")

        def keep(out):
            env["part", blocks + b] = out

        return run, (grad_expand, expand_weight, env["grad_qkv", b], qkv_weight), keep

    def weight_grad(name, left, right, axis):
        def run(left, right):
            return transpose_dot(left, right).astype(BF16)

        def keep(out):
            env[name] = lax.psum_scatter(
                out, ("dp", "ctx"), scatter_dimension=axis, tiled=True
            ).astype(F32)

        return run, (left, right), keep

    def put_out(b):
        def run(four, before):
            return place_total(flags, four, b, rows, before)

        def keep(out):
            env["layer_out"] = out

        return run, (env["total", b], env.get("layer_out")), keep

    def put_grad(b):
        def run(four, tokens_in, cot_in, before):
            return norm_back(flags, four, b, tokens_in, cot_in, gain_row, before)

        def keep(out):
            env["grad_tokens"], env["gain", b], env["shift", b] = out

        return run, (env["total", blocks + b], tokens, cotangent, env.get("grad_tokens")), keep

    def all_attended():
        return jnp.concatenate(
            [
                jnp.concatenate([env["attended", b][c] for b in range(blocks)], axis=0)
                for c in range(ctx_count)
            ],
            axis=1,
        )

    def all_grad_qkv():
        return jnp.concatenate([env["grad_qkv", b] for b in range(blocks)], axis=0)

    ticks = 4 * blocks + 2
    plan = [[] for _ in range(ticks + 8)]
    spot = 2 * blocks - 2
    for b in range(blocks):
        if b >= 2:
            plan[b - 2].append(functools.partial(forward, b))
        if b >= 1:
            plan[b - 1].append(functools.partial(out_part, b))
        plan[blocks - 2 + b].append(functools.partial(backward, b))
        plan[2 * b + 4].append(functools.partial(put_out, b))
        plan[spot + 1 + 2 * b].append(functools.partial(grad_part, b))
        plan[2 * blocks + 2 * b + 4].append(functools.partial(put_grad, b))
    after = [[] for _ in plan]
    after[spot - 1].append(finish)
    for b in range(blocks):
        plan[spot + 2 * b].append(functools.partial(give_back, b))
    plan[spot].append(lambda: weight_grad("dense", all_attended(), cotangent, 1))
    plan[spot].append(lambda: weight_grad("fc2", activated, cotangent, 1))
    plan[spot + 3].append(lambda: weight_grad("fc1", hidden, grad_expand, 0))
    plan[spot + 2 * blocks].append(lambda: weight_grad("qkv", hidden, all_grad_qkv(), 0))

    def perform(make):
        run, ins, keep = make()
        keep(run(*ins))

    for b in range(min(2, blocks)):
        perform(functools.partial(forward, b))
    perform(functools.partial(out_part, 0))

    line = Line(flags, tokens, (b_dense.astype(F32) + b_fc2.astype(F32))[None])
    arrived = (None, None)
    for t in range(ticks):
        b, second = divmod(t, 2)
        if second:
            operands = line.middle(*arrived)
        else:
            if t > 0:
                total = line.end(*arrived)
                if total is not None:
                    env["total", b - 2] = total
            operands = line.begin(env.get(("part", b)), b < blocks)
        stages = [s for s in (plan[t], after[t]) if s]
        sent = None
        for n, stage in enumerate(stages):
            work = [make() for make in stage]
            operands, ins = tie(operands, [w[1] for w in work])
            if sent is None:
                sent = send(*operands)
            outs = [w[0](*i) for w, i in zip(work, ins)]
            if n == len(stages) - 1:
                arrived, outs = tie(sent, outs)
            for w, out in zip(work, outs):
                w[2](out)
        if not stages:
            arrived = send(*operands)
    env["total", 2 * blocks - 1] = line.end(*arrived)
    for late in plan[ticks:]:
        for make in late:
            perform(make)

    layer_out, grad_tokens = env["layer_out"], env["grad_tokens"]
    small = (
        sum(env["gain", b][0] for b in range(blocks)),
        sum(env["shift", b][0] for b in range(blocks)),
        jnp.sum(all_grad_qkv().astype(F32), axis=0),
        expand_sum[0],
        cot_sum[0],
    )
    sizes = [array.shape[0] for array in small]
    packed = lax.psum(jnp.concatenate(small), ("dp", "ctx"))
    ends = [sum(sizes[: i + 1]) for i in range(len(sizes))]
    gain_sum, shift_sum, qkv_sum, expand_total, out_sum = (
        packed[end - size : end] for end, size in zip(ends, sizes)
    )

    def unmixed(array):
        lead = array.shape[:-1]
        parts = array.reshape(*lead, ctx_count, 3, share)
        return tuple(parts[..., t, :].reshape(*lead, local) for t in range(3))

    grad_query, grad_key, grad_value = unmixed(env["qkv"])
    sum_query, sum_key, sum_value = unmixed(qkv_sum)
    return (
        layer_out, grad_tokens, gain_sum, shift_sum, grad_query, sum_query, grad_key, sum_key,
        grad_value, sum_value, env["dense"], out_sum, env["fc1"], expand_total, env["fc2"], out_sum,
    )


def solution(mesh):
    rows = P(("dp", "ctx"), None)
    down, across = P(("dp", "ctx"), "tp"), P("tp", ("dp", "ctx"))
    wide = P("tp")
    ins = (
        rows, rows, P("dp", None), P(), P(), down, wide, down, wide, down, wide, across, P(), down,
        wide, across, P(),
    )
    outs = (
        rows, rows, P(), P(), down, wide, down, wide, down, wide, across, P(), down, wide, across,
        P(),
    )
    return jax.shard_map(body, mesh=mesh, in_specs=ins, out_specs=outs, check_vma=False)
```

```python
import functools

import jax
import jax.numpy as jnp
from jax import lax
from jax.experimental import pallas as pl
from jax.experimental.pallas import tpu as pltpu
from jax.sharding import PartitionSpec as P

HDIM = 64
ROT = 32
PLEN = 2048
CLEN = 256
GPR = 2
BLOCK = 1024
VMEM = 56 * 2**20
F32 = jnp.float32
BF16 = jnp.bfloat16
NT = (((1,), (1,)), ((), ()))
NN = (((1,), (0,)), ((), ()))


def cost(bytes_accessed, flops=0):
    return pl.CostEstimate(flops=flops, bytes_accessed=bytes_accessed, transcendentals=0)


def dot(left, right, dims):
    return lax.dot_general(left, right, dims, preferred_element_type=F32)


def transpose_dot(left, right):
    return jnp.einsum("ra,rb->ab", left, right, preferred_element_type=F32)


def dot_back(left, right):
    return jnp.einsum("rb,ab->ra", left, right, preferred_element_type=F32)


def norm_apply(matrix, norm_gain, norm_shift):
    center = matrix - jnp.mean(matrix, axis=-1, keepdims=True)
    spread = jnp.mean(center * center, axis=-1, keepdims=True)
    return center * lax.rsqrt(spread + 1e-05) * norm_gain + norm_shift


def gelu_parts(v):
    scale = (2.0 / jnp.pi) ** 0.5
    square = v * v
    t = jnp.tanh(v * (scale + (scale * 0.044715) * square))
    half = 0.5 * v
    value = half + half * t
    slope = (0.5 + 0.5 * t) + (half - half * t * t) * (scale + (scale * 3 * 0.044715) * square)
    return value, slope


def rotary_tables():
    half = ROT // 2
    positions = jnp.arange(PLEN + CLEN, dtype=F32)
    frequency = 10000.0 ** (-2.0 * jnp.arange(half, dtype=F32) / ROT)
    angles = positions[:, None] * frequency[None, :]
    cosine, sine = jnp.cos(angles), jnp.sin(angles)
    ones = jnp.ones((PLEN + CLEN, HDIM - ROT), F32)
    zeros = jnp.zeros_like(ones)
    none = jnp.zeros_like(sine)
    head = (
        jnp.concatenate([cosine, cosine, ones], axis=1),
        jnp.concatenate([-sine, none, zeros], axis=1),
        jnp.concatenate([none, sine, zeros], axis=1),
    )
    return tuple(jnp.concatenate([table, table], axis=1) for table in head)


def rotated(values, cosine, first, second):
    half = ROT // 2
    return (
        values * cosine
        + pltpu.roll(values, 2 * HDIM - half, 1) * first
        + pltpu.roll(values, half, 1) * second
    )


def ahead(count, first, second):
    held = first(0)
    for i in range(count):
        following = first(i + 1) if i + 1 < count else None
        second(i, held)
        held = following


def norm_kernel(x_ref, gain_ref, shift_ref, out_ref):
    x = x_ref[...].astype(F32)
    out_ref[...] = norm_apply(x, gain_ref[...], shift_ref[...]).astype(BF16)


def qkv_kernel(
    share, where_ref, hidden_ref, weight_ref, bias_ref, cos_ref, first_ref, second_ref, out_ref
):
    hidden = hidden_ref[...]
    cosine, first, second = cos_ref[...], first_ref[...], second_ref[...]
    lane = lax.broadcasted_iota(jnp.int32, (1, 2 * HDIM), 1)
    member_width = out_ref.shape[2]

    def linear(i):
        at = slice(i * 512, (i + 1) * 512)
        return dot(hidden, weight_ref[:, at], NN) + bias_ref[:, at]

    def turn(i, lin):
        begin = i * 512
        for column in range(0, 512, 2 * HDIM):
            part = lin[:, column : column + 2 * HDIM]
            turns = [((begin + column + off) // share) % 3 < 2 for off in (0, HDIM)]
            if any(turns):
                turned = rotated(part, cosine, first, second)
                if not all(turns):
                    keep = lane < HDIM if turns[0] else lane >= HDIM
                    turned = jnp.where(keep, turned, part)
                part = turned
            part = part.astype(BF16)
            size = min(2 * HDIM, share)
            for off in range(0, 2 * HDIM, size):
                member, place = divmod(begin + column + off, member_width)
                out_ref[member, :, place : place + size] = part[:, off : off + size]

    ahead(weight_ref.shape[1] // 512, linear, turn)


def qkv_project(hidden, weight, bias, tables, spots, share):
    rows, width = hidden.shape
    outs = weight.shape[1]
    count = 256
    whole = lambda shape: pl.BlockSpec(shape, lambda i, *_: (0, 0))
    table = pl.BlockSpec((count, 2 * HDIM), lambda i, spots: (spots[i], 0))
    return pl.pallas_call(
        functools.partial(qkv_kernel, share),
        grid_spec=pltpu.PrefetchScalarGridSpec(
            num_scalar_prefetch=1,
            grid=(rows // count,),
            in_specs=[
                pl.BlockSpec((count, width), lambda i, *_: (i, 0)),
                whole((width, outs)),
                whole((1, outs)),
                table,
                table,
                table,
            ],
            out_specs=pl.BlockSpec(
                (outs // (3 * share), count, 3 * share), lambda i, *_: (0, i, 0)
            ),
        ),
        out_shape=jax.ShapeDtypeStruct((outs // (3 * share), rows, 3 * share), BF16),
        compiler_params=pltpu.CompilerParams(vmem_limit_bytes=VMEM),
        cost_estimate=pl.CostEstimate(
            flops=2 * rows * width * outs, bytes_accessed=2 * rows * (2 * width + outs),
            transcendentals=0,
        ),
        name="qkv_project",
    )(spots, hidden, weight, bias, *tables)


def expand_kernel(hidden_ref, weight_ref, bias_ref, slope_ref, out_ref):
    hidden = hidden_ref[...]

    def linear(i):
        at = slice(i * 512, (i + 1) * 512)
        return dot(hidden, weight_ref[:, at], NN) + bias_ref[:, at]

    def keep(i, lin):
        at = slice(i * 512, (i + 1) * 512)
        value, slope = gelu_parts(lin)
        out_ref[:, at] = value.astype(BF16)
        slope_ref[:, at] = slope.astype(BF16)

    ahead(weight_ref.shape[1] // 512, linear, keep)


def shrink_kernel(act_ref, weight_ref, out_ref):
    out_ref[...] = dot(act_ref[...], weight_ref[...], NN).astype(BF16)


def slope_kernel(cot_ref, slope_ref, weight_ref, grad_ref, sum_ref, cot_sum_ref):
    @pl.when(pl.program_id(0) == 0)
    def _():
        sum_ref[...] = jnp.zeros_like(sum_ref)
        cot_sum_ref[...] = jnp.zeros_like(cot_sum_ref)

    cot = cot_ref[...]
    cot_sum_ref[...] += jnp.sum(cot.astype(F32), axis=0, keepdims=True)

    def back(i):
        return dot(cot, weight_ref[i * 512 : (i + 1) * 512, :], NT)

    def keep(i, grad):
        at = slice(i * 512, (i + 1) * 512)
        grad = (slope_ref[:, at].astype(F32) * grad).astype(BF16)
        grad_ref[:, at] = grad
        sum_ref[:, at] += jnp.sum(grad.astype(F32), axis=0, keepdims=True)

    ahead(weight_ref.shape[0] // 512, back, keep)


def grad_attended_kernel(cot_ref, weight_ref, out_ref):
    cot = cot_ref[...]
    share = out_ref.shape[2]
    whole = dot(cot, weight_ref[...], NT).astype(BF16)
    for c in range(out_ref.shape[0]):
        out_ref[c] = whole[:, c * share : (c + 1) * share]


def grad_attended(cotangent, weight, share):
    rows, width = cotangent.shape
    local = weight.shape[0]
    count = 512
    return pl.pallas_call(
        grad_attended_kernel,
        grid=(rows // count,),
        in_specs=[
            pl.BlockSpec((count, width), lambda i: (i, 0)),
            pl.BlockSpec((local, width), lambda i: (0, 0)),
        ],
        out_specs=pl.BlockSpec((local // share, count, share), lambda i: (0, i, 0)),
        out_shape=jax.ShapeDtypeStruct((local // share, rows, share), BF16),
        compiler_params=pltpu.CompilerParams(vmem_limit_bytes=VMEM),
        cost_estimate=pl.CostEstimate(
            flops=2 * rows * width * local, bytes_accessed=2 * rows * (width + local),
            transcendentals=0,
        ),
        name="grad_attended",
    )(cotangent, weight)


def row_call(kernel, name, count, rows, in_arrays, outs, flops):
    def spec(shape):
        if shape[0] == rows:
            return pl.BlockSpec((count, shape[1]), lambda i: (i, 0))
        return pl.BlockSpec(shape, lambda i: (0, 0))

    return pl.pallas_call(
        kernel,
        grid=(rows // count,),
        in_specs=[spec(a.shape) for a in in_arrays],
        out_specs=[spec(o.shape) for o in outs],
        out_shape=outs,
        compiler_params=pltpu.CompilerParams(vmem_limit_bytes=VMEM),
        cost_estimate=pl.CostEstimate(
            flops=flops,
            bytes_accessed=sum(a.size * a.dtype.itemsize for a in (*in_arrays, *outs)),
            transcendentals=0,
        ),
        name=name,
    )(*in_arrays)


def products_kernel(kinds, has_base, *refs):
    out_ref = refs[-1]
    base_ref = refs[0] if has_base else None
    pairs = refs[has_base:-1]
    count = 256

    @pl.loop(0, out_ref.shape[0] // count)
    def _(i):
        rows = pl.ds(pl.multiple_of(i * count, count), count)
        total = base_ref[rows, :].astype(F32) if has_base else None
        for n, dims in enumerate(kinds):
            step = dot(pairs[2 * n][rows, :], pairs[2 * n + 1][...], dims)
            total = step if total is None else total + step
        out_ref[rows, :] = total.astype(BF16)


def products(count, outs, base, pairs, name):
    tile = 512
    arrays, specs, kinds = [], [], []
    flops = 0
    if base is not None:
        arrays.append(base[0])
        specs.append(pl.BlockSpec((count, tile), lambda n, at=base[1]: (at, n)))
    for left, at, right, right_at in pairs:
        depth = left.shape[1]
        arrays += [left, right]
        specs.append(pl.BlockSpec((count, depth), lambda n, at=at: (at, 0)))
        if right_at is None:
            specs.append(pl.BlockSpec((tile, depth), lambda n: (n, 0)))
            kinds.append(NT)
        else:
            specs.append(pl.BlockSpec((depth, tile), lambda n, at=right_at: (at, n)))
            kinds.append(NN)
        flops += 2 * count * depth * outs
    return pl.pallas_call(
        functools.partial(products_kernel, kinds, base is not None),
        grid=(outs // tile,),
        in_specs=specs,
        out_specs=pl.BlockSpec((count, tile), lambda n: (0, n)),
        out_shape=jax.ShapeDtypeStruct((count, outs), BF16),
        compiler_params=pltpu.CompilerParams(vmem_limit_bytes=VMEM),
        cost_estimate=pl.CostEstimate(
            flops=flops, bytes_accessed=flops // 512, transcendentals=0
        ),
        name=name,
    )(*arrays)


def heads_split(array, heads):
    if heads == 1:
        return [array]
    lane = lax.broadcasted_iota(jnp.int32, array.shape, 1)
    return [jnp.where(lane // HDIM == h, array, jnp.zeros((), array.dtype)) for h in range(heads)]


def near_mask():
    key = lax.broadcasted_iota(jnp.int32, (CLEN, CLEN), 0)
    query = lax.broadcasted_iota(jnp.int32, (CLEN, CLEN), 1)
    return key <= query


def over_far(base, count, big, step):
    per = big // CLEN
    full = count // per

    @pl.loop(0, full)
    def _(i):
        step(pl.multiple_of(base + i * big, CLEN), big)

    @pl.loop(full * per, count)
    def _(i):
        step(pl.multiple_of(base + i * CLEN, CLEN), CLEN)


def attend_kernel(
    big, group_ref, far_ref, item_ref, q_ref, ko_ref, vo_ref, kp_ref, vt_s, o_ref, ot_ref,
    lse_ref, m_s, l_s, acc_s,
):
    heads = q_ref.shape[1] // HDIM
    item = item_ref[pl.program_id(1)]
    base = group_ref[item] * PLEN

    queries = heads_split(q_ref[...] * BF16(HDIM**-0.5), heads)
    mask = near_mask()
    keys = ko_ref[...]
    values = vo_ref[...].T
    spans = [slice(h * HDIM, (h + 1) * HDIM) for h in range(heads)]
    scores = [dot(keys, queries[h], NT) for h in range(heads)]
    for h in range(heads):
        s = jnp.where(mask, scores[h], -1e30)
        m = jnp.max(s, axis=0, keepdims=True)
        p = jnp.exp(s - m)
        m_s[h] = m
        l_s[h] = jnp.sum(p, axis=0, keepdims=True)
        acc_s[h] = dot(values[spans[h]], p.astype(BF16), NN)

    def step(first, size):
        k = kp_ref[pl.ds(first, size), :]
        scores = [dot(k, queries[h], NT) for h in range(heads)]
        for h in range(heads):
            old = m_s[h]
            m = jnp.maximum(old, jnp.max(scores[h], axis=0, keepdims=True))
            p = jnp.exp(scores[h] - m)
            a = jnp.exp(old - m)
            m_s[h] = m
            l_s[h] = l_s[h] * a + jnp.sum(p, axis=0, keepdims=True)
            acc_s[h] = acc_s[h] * a + dot(vt_s[spans[h], pl.ds(first, size)], p.astype(BF16), NN)

    over_far(base, far_ref[item], big, step)
    for h in range(heads):
        ot_ref[spans[h], :] = acc_s[h] * (1.0 / l_s[h])
        lse_ref[0, h : h + 1, :] = m_s[h] + jnp.log(l_s[h])
    o_ref[...] = ot_ref[...].T.astype(BF16)


def turn_kernel(in_ref, out_ref):
    for begin in range(0, in_ref.shape[0], CLEN):
        out_ref[:, begin : begin + CLEN] = in_ref[begin : begin + CLEN, :].T


def turn_prompts(qkv, width, which):
    wide = min(4 * HDIM, width)
    arrays, ats = split_columns(qkv, width)
    count = PLEN // 2
    return pl.pallas_call(
        turn_kernel,
        grid=(width // wide, GPR * PLEN // count),
        in_specs=[pl.BlockSpec((count, wide), lambda h, i: (i, ats[which] + h))],
        out_specs=pl.BlockSpec((wide, count), lambda h, i: (h, i)),
        out_shape=jax.ShapeDtypeStruct((width, GPR * PLEN), BF16),
        compiler_params=pltpu.CompilerParams(vmem_limit_bytes=VMEM),
        cost_estimate=cost(width * GPR * PLEN * 8),
        name="turn_prompts",
    )(arrays[which])


def turned_back(values, tables):
    width = values.shape[1]
    cosine, first, second = (ref[...] for ref in tables)
    wide = 2 * HDIM
    if width < wide:
        values = jnp.concatenate([values, values], axis=1)
    parts = [
        rotated(values[:, c : c + wide], cosine, -first, -second)
        for c in range(0, values.shape[1], wide)
    ]
    out = parts[0] if len(parts) == 1 else jnp.concatenate(parts, axis=1)
    return out[:, :width].astype(BF16)


def attend_back_kernel(big, first_piece, prompt_items, prompt_count, *refs):
    group_ref, far_ref, item_ref = refs[:3]
    q_ref, ko_ref, vo_ref, do_ref, ot_ref, lse_ref, kp_ref, vp_ref, kt_s = refs[3:12]
    tables = refs[12:15]
    before = () if first_piece else refs[15:17]
    dq_ref, dk_ref, dv_ref, dk_s, dv_s, dq_s, near_k, near_v = refs[15 + len(before) :]
    width = q_ref.shape[1]
    heads = width // HDIM
    turn = pl.program_id(1)
    item = item_ref[turn]
    base = group_ref[item] * PLEN

    @pl.when(turn == 0)
    def _():
        if first_piece:
            dk_s[...] = jnp.zeros_like(dk_s)
            dv_s[...] = jnp.zeros_like(dv_s)
        else:
            dk_s[...] = before[0][...]
            dv_s[...] = before[1][...]

    do = do_ref[...]
    queries = heads_split(q_ref[...] * BF16(HDIM**-0.5), heads)
    grads = heads_split(do, heads)
    query_cat = jnp.concatenate(queries, axis=0)
    grad_cat = jnp.concatenate(grads, axis=0)
    spans = [slice(h * HDIM, (h + 1) * HDIM) for h in range(heads)]
    product = ot_ref[...] * do.astype(F32).T
    center = [jnp.sum(product[span], axis=0, keepdims=True) for span in spans]
    lse = [lse_ref[0, h : h + 1, :] for h in range(heads)]
    mask = near_mask()

    def piece(k, v, kt, near):
        chance, grad_scores = [], []
        scores = [dot(k, queries[h], NT) for h in range(heads)]
        grad_chance = [dot(v, grads[h], NT) for h in range(heads)]
        for h in range(heads):
            p = jnp.exp(scores[h] - lse[h])
            if near:
                p = jnp.where(mask, p, 0.0)
            grad_scores.append((p * (grad_chance[h] - center[h])).astype(BF16))
            chance.append(p.astype(BF16))
        for h in range(heads):
            step = dot(kt(spans[h]), grad_scores[h], NN)
            if near:
                dq_s[spans[h], :] = step
            else:
                dq_s[spans[h], :] += step
        return (
            dot(jnp.concatenate(grad_scores, axis=1), query_cat, NN),
            dot(jnp.concatenate(chance, axis=1), grad_cat, NN),
        )

    own = ko_ref[...]
    own_t = own.T
    near_k[...], near_v[...] = piece(own, vo_ref[...], lambda span: own_t[span], True)

    @pl.when(turn < prompt_count)
    def _():
        rows = pl.ds(pl.multiple_of(item * CLEN, CLEN), CLEN)
        dk_s[rows, :] += near_k[...]
        dv_s[rows, :] += near_v[...]

    @pl.when(turn >= prompt_count)
    def _():
        dk_ref[...] = turned_back(near_k[...], tables)
        dv_ref[...] = near_v[...].astype(BF16)

    def step(first, size):
        rows = pl.ds(first, size)
        k_step, v_step = piece(
            kp_ref[rows, :], vp_ref[rows, :], lambda span: kt_s[span, rows], False
        )
        dk_s[rows, :] += k_step
        dv_s[rows, :] += v_step

    over_far(base, far_ref[item], big, step)
    dq_ref[...] = turned_back((dq_s[...] * (HDIM**-0.5)).T, tables)


def finish_kernel(dk_ref, dv_ref, cos_ref, first_ref, second_ref, ok_ref, ov_ref):
    ok_ref[...] = turned_back(dk_ref[...], (cos_ref, first_ref, second_ref))
    ov_ref[...] = dv_ref[...].astype(BF16)


def finish_prompts(dk, dv, tables):
    rows, width = dk.shape
    wide = min(4 * HDIM, width)
    count = PLEN // 2
    block = pl.BlockSpec((count, wide), lambda h, i: (i, h))
    table = pl.BlockSpec((count, 2 * HDIM), lambda h, i: (i % (PLEN // count), 0))
    return pl.pallas_call(
        finish_kernel,
        grid=(width // wide, rows // count),
        in_specs=[block, block, table, table, table],
        out_specs=[block, block],
        out_shape=[jax.ShapeDtypeStruct((rows, width), BF16)] * 2,
        compiler_params=pltpu.CompilerParams(vmem_limit_bytes=VMEM),
        cost_estimate=cost(rows * width * 30),
        name="finish_prompts",
    )(dk, dv, *tables)


def split_columns(qkv, width):
    wide = min(4 * HDIM, width)
    if wide % 128 == 0:
        return (qkv, qkv, qkv), tuple(t * width // wide for t in range(3))
    return tuple(qkv[:, t * width : (t + 1) * width] for t in range(3)), (0, 0, 0)


def attention_specs(width):
    wide = min(4 * HDIM, width)
    heads = wide // HDIM
    return (
        wide,
        heads,
        lambda at: pl.BlockSpec((CLEN, wide), lambda h, i, g, f, items: (items[i], at + h)),
        pl.BlockSpec((CLEN, wide), lambda h, i, *_: (i, h)),
        pl.BlockSpec((wide, CLEN), lambda h, i, *_: (h, i)),
        lambda at: pl.BlockSpec((GPR * PLEN, wide), lambda h, i, *_: (0, at + h)),
        pl.BlockSpec((1, heads, CLEN), lambda h, i, *_: (h, 0, i)),
    )


def attend(qkv, turned_v, width, group, far, items):
    rows = items.shape[0] * CLEN
    wide, heads, picked, block, turned, prompts, stats = attention_specs(width)
    (q, k, v), (qa, ka, va) = split_columns(qkv, width)
    pairs = rows * (PLEN + CLEN) * width // HDIM
    return pl.pallas_call(
        functools.partial(attend_kernel, 1024),
        grid_spec=pltpu.PrefetchScalarGridSpec(
            num_scalar_prefetch=3,
            grid=(width // wide, rows // CLEN),
            in_specs=[
                picked(qa), picked(ka), picked(va), prompts(ka),
                pl.BlockSpec((wide, GPR * PLEN), lambda h, i, *_: (h, 0)),
            ],
            out_specs=[block, turned, stats],
            scratch_shapes=[
                pltpu.VMEM((heads, 1, CLEN), F32),
                pltpu.VMEM((heads, 1, CLEN), F32),
                pltpu.VMEM((heads, HDIM, CLEN), F32),
            ],
        ),
        out_shape=[
            jax.ShapeDtypeStruct((rows, width), BF16),
            jax.ShapeDtypeStruct((width, rows), F32),
            jax.ShapeDtypeStruct((width // wide, heads, rows), F32),
        ],
        compiler_params=pltpu.CompilerParams(vmem_limit_bytes=VMEM),
        cost_estimate=pl.CostEstimate(
            flops=4 * pairs * 256, bytes_accessed=rows * width * 12, transcendentals=pairs
        ),
        name="attend",
    )(group, far, items, q, k, v, k, turned_v)


def attend_back(
    qkv, turned_k, width, grad, turned_out, lse, tables, group, far, items, prompt_count, before
):
    rows = items.shape[0] * CLEN
    wide, heads, picked, block, turned, prompts, stats = attention_specs(width)
    (q, k, v), (qa, ka, va) = split_columns(qkv, width)
    table = pl.BlockSpec((CLEN, 2 * HDIM), lambda h, i, g, f, items: (f[items[i]], 0))
    total = pl.BlockSpec((GPR * PLEN, wide), lambda h, i, *_: (0, h))
    late = pl.BlockSpec((CLEN, wide), lambda h, i, *_: (jnp.maximum(i - prompt_count, 0), h))
    pairs = rows * (PLEN + CLEN) * width // HDIM
    first = not before
    late_rows = rows - prompt_count * CLEN
    return pl.pallas_call(
        functools.partial(attend_back_kernel, 1024, first, GPR * PLEN // CLEN, prompt_count),
        grid_spec=pltpu.PrefetchScalarGridSpec(
            num_scalar_prefetch=3,
            grid=(width // wide, rows // CLEN),
            in_specs=[
                picked(qa), picked(ka), picked(va), picked(0), turned, stats, prompts(ka),
                prompts(va), pl.BlockSpec((wide, GPR * PLEN), lambda h, i, *_: (h, 0)), table, table,
                table,
            ]
            + [total] * len(before),
            out_specs=[block, late, late, total, total],
            scratch_shapes=[
                pltpu.VMEM((wide, CLEN), F32),
                pltpu.VMEM((CLEN, wide), F32),
                pltpu.VMEM((CLEN, wide), F32),
            ],
        ),
        out_shape=[jax.ShapeDtypeStruct((rows, width), BF16)]
        + [jax.ShapeDtypeStruct((late_rows, width), BF16)] * 2
        + [jax.ShapeDtypeStruct((GPR * PLEN, width), F32)] * 2,
        input_output_aliases={} if first else {15: 3, 16: 4},
        compiler_params=pltpu.CompilerParams(vmem_limit_bytes=VMEM),
        cost_estimate=pl.CostEstimate(
            flops=8 * pairs * 256, bytes_accessed=rows * width * 24, transcendentals=pairs
        ),
        name="attend_back",
    )(group, far, items, q, k, v, grad, turned_out, lse, k, v, turned_k, *tables, *before)


def tie(*trees):
    return lax.optimization_barrier(trees)


COUNT = 256


def begin_kernel(names, flag_ref, *refs):
    refs = dict(zip(names, refs))
    outer = flag_ref[0] == 1
    out_ref = refs["out"]

    @pl.when(outer)
    def _():
        out_ref[...] = refs["next"][...] if "next" in refs else jnp.zeros_like(out_ref)

    @pl.when(flag_ref[0] == 0)
    def _():
        if "part" not in refs:
            out_ref[...] = jnp.zeros_like(out_ref)
            return
        total = (
            refs["part"][...].astype(F32)
            + refs["swapped"][...].astype(F32)
            + refs["crossed"][...].astype(F32)
        )
        if "tokens" in refs:
            total = total + refs["tokens"][...].astype(F32) + refs["bias"][...]
        out_ref[...] = total.astype(BF16)


def middle_kernel(names, flag_ref, *refs):
    refs = dict(zip(names, refs))
    outer = flag_ref[0] == 1
    swap_ref = refs["swap"]

    @pl.when(outer)
    def _():
        swap_ref[...] = refs["near"][...] if "near" in refs else jnp.zeros_like(swap_ref)

    @pl.when(flag_ref[0] == 0)
    def _():
        swap_ref[...] = refs["crossed"][...] if "crossed" in refs else jnp.zeros_like(swap_ref)

    if "far" in refs:
        refs["cross"][...] = (
            refs["far"][...].astype(F32) + refs["swapped"][...].astype(F32)
        ).astype(BF16)


def line_call(kernel, flags, rows, width, ins, outs, name):
    steps = rows // COUNT

    def spec(shape, first, who):
        if shape[0] == 1:
            return pl.BlockSpec(shape, lambda i, flag: (0, 0))

        def index(i, flag):
            needed = {"all": 1, "outer": flag[0], "inner": 1 - flag[0]}[who]
            return (first(flag[1], steps) + i * needed, 0)

        return pl.BlockSpec((COUNT, width), index)

    return pl.pallas_call(
        functools.partial(kernel, [i[0] for i in ins] + outs),
        grid_spec=pltpu.PrefetchScalarGridSpec(
            num_scalar_prefetch=1,
            grid=(steps,),
            in_specs=[spec(array.shape, first, who) for _, array, first, who in ins],
            out_specs=[pl.BlockSpec((COUNT, width), lambda i, flag: (i, 0)) for _ in outs],
        ),
        out_shape=[jax.ShapeDtypeStruct((rows, width), BF16) for _ in outs],
        compiler_params=pltpu.CompilerParams(vmem_limit_bytes=VMEM),
        cost_estimate=cost(rows * width * 16),
        name=name,
    )(flags, *[i[1] for i in ins])


def total_specs(half, width, begin):
    outer = lambda flag: flag[0]
    inner = lambda flag: 1 - flag[0]

    def spec(part, who):
        return pl.BlockSpec(
            (COUNT, width), lambda p, i, flag: (i * who(flag) * (p + begin == part), 0)
        )

    return [spec(0, outer), spec(0, inner), spec(1, outer), spec(1, inner)]


def total_of(flag_ref, refs, keep, begin):
    part = pl.program_id(0) + begin
    for at, ref in enumerate(refs):
        right = (part == at // 2) & (flag_ref[0] == 1 - at % 2)

        @pl.when(right)
        def _(ref=ref):
            keep(ref[...])


def rows_of(block, half, begin):
    steps = half // COUNT

    def index(p, i, flag):
        return ((2 * block + (flag[1] + p + begin) % 2) * steps + i, 0)

    return index


def place_kernel(flag_ref, a, b, c, d, *rest):
    out_ref = rest[-1]

    def keep(value):
        out_ref[...] = value

    total_of(flag_ref, (a, b, c, d), keep, 0)


def place_total(flags, four, block, rows, before):
    half, width = four[0].shape
    return pl.pallas_call(
        place_kernel,
        grid_spec=pltpu.PrefetchScalarGridSpec(
            num_scalar_prefetch=1,
            grid=(2, half // COUNT),
            in_specs=total_specs(half, width, 0)
            + [pl.BlockSpec(memory_space=pl.ANY)] * (before is not None),
            out_specs=pl.BlockSpec((COUNT, width), rows_of(block, half, 0)),
        ),
        out_shape=jax.ShapeDtypeStruct((rows, width), BF16),
        input_output_aliases={} if before is None else {5: 0},
        compiler_params=pltpu.CompilerParams(vmem_limit_bytes=VMEM),
        cost_estimate=cost(half * width * 24),
        name="place_total",
    )(flags, *four, *(() if before is None else (before,)))


def normed_rows(x_ref):
    x = x_ref[...].astype(F32)
    center = x - jnp.mean(x, axis=-1, keepdims=True)
    inverse = lax.rsqrt(jnp.mean(center * center, axis=-1, keepdims=True) + 1e-05)
    return center * inverse, inverse


def norm_back_kernel(begin, flag_ref, a, b, c, d, x_ref, cot_ref, gain_ref, *rest):
    out_ref, held = rest[-2:]

    def keep(value):
        held[...] = value.astype(F32) * gain_ref[...]

    total_of(flag_ref, (a, b, c, d), keep, begin)
    normed, inverse = normed_rows(x_ref)
    scaled = held[...]
    grad = scaled - jnp.mean(scaled, axis=-1, keepdims=True)
    grad = inverse * (grad - normed * jnp.mean(scaled * normed, axis=-1, keepdims=True))
    out_ref[...] = cot_ref[...].astype(F32) + grad


def norm_back(flags, four, block, tokens, cotangent, gain, before, begin, count):
    half, width = four[0].shape
    row = pl.BlockSpec((1, width), lambda p, i, flag: (0, 0))
    whole = pl.BlockSpec((COUNT, width), rows_of(block, half, begin))
    return pl.pallas_call(
        functools.partial(norm_back_kernel, begin),
        grid_spec=pltpu.PrefetchScalarGridSpec(
            num_scalar_prefetch=1,
            grid=(count, half // COUNT),
            in_specs=total_specs(half, width, begin)
            + [whole, whole, row]
            + [pl.BlockSpec(memory_space=pl.ANY)] * (before is not None),
            out_specs=whole,
            scratch_shapes=[pltpu.VMEM((COUNT, width), F32)],
        ),
        out_shape=jax.ShapeDtypeStruct(tokens.shape, F32),
        input_output_aliases={} if before is None else {8: 0},
        compiler_params=pltpu.CompilerParams(vmem_limit_bytes=VMEM),
        cost_estimate=cost(half * width * 24 * count),
        name="norm_back",
    )(flags, *four, tokens, cotangent, gain, *(() if before is None else (before,)))


def norm_sums_kernel(flag_ref, total_ref, x_ref, gain_sum, shift_sum):
    @pl.when(pl.program_id(0) == 0)
    def _():
        gain_sum[...] = jnp.zeros_like(gain_sum)
        shift_sum[...] = jnp.zeros_like(shift_sum)

    @pl.when(flag_ref[0] == 0)
    def _():
        total = total_ref[...].astype(F32)
        gain_sum[...] += jnp.sum(total * normed_rows(x_ref)[0], axis=0, keepdims=True)
        shift_sum[...] += jnp.sum(total, axis=0, keepdims=True)


def norm_sums(flags, near, block, tokens):
    half, width = near.shape
    steps = half // COUNT
    row = pl.BlockSpec((1, width), lambda i, flag: (0, 0))
    return pl.pallas_call(
        norm_sums_kernel,
        grid_spec=pltpu.PrefetchScalarGridSpec(
            num_scalar_prefetch=1,
            grid=(steps,),
            in_specs=[
                pl.BlockSpec((COUNT, width), lambda i, flag: (i * (1 - flag[0]), 0)),
                pl.BlockSpec(
                    (COUNT, width),
                    lambda i, flag: ((2 * block + flag[1]) * steps + i * (1 - flag[0]), 0),
                ),
            ],
            out_specs=[row, row],
        ),
        out_shape=[jax.ShapeDtypeStruct((1, width), F32)] * 2,
        compiler_params=pltpu.CompilerParams(vmem_limit_bytes=VMEM),
        cost_estimate=cost(half * width * 10),
        name="norm_sums",
    )(flags, near, tokens)


class Line:
    def __init__(self, flags, tokens, bias):
        self.flags, self.tokens, self.bias = flags, tokens, bias
        self.outer = flags[0] == 1
        self.part = self.near = None
        self.block = -1

    def begin(self, part, with_input):
        zero = lambda side, steps: 0
        near = lambda side, steps: side * steps
        ins = []
        if self.part is not None:
            ins += [
                ("part", self.part, near, "inner"),
                ("swapped", self.swapped, zero, "inner"),
                ("crossed", self.crossed, zero, "inner"),
            ]
            if self.with_input:
                block = self.block
                ins += [
                    ("tokens", self.tokens, lambda side, steps: (2 * block + side) * steps, "inner"),
                    ("bias", self.bias, zero, "all"),
                ]
        if part is not None:
            ins.append(("next", part, lambda side, steps: (1 - side) * steps, "outer"))
        shape = (self.part if part is None else part).shape
        (out,) = line_call(
            begin_kernel, self.flags, shape[0] // 2, shape[1], ins, ["out"], "line_begin"
        )
        had = self.part is not None
        self.part, self.with_input = part, with_input
        self.block += 1
        self.near = out if had else None
        return out, self.near

    def middle(self, swapped, crossed):
        self.first, self.other = swapped, crossed
        ins = []
        if self.part is not None:
            ins += [
                ("near", self.part, lambda side, steps: side * steps, "outer"),
                ("far", self.part, lambda side, steps: (1 - side) * steps, "inner"),
                ("swapped", swapped, lambda side, steps: 0, "inner"),
            ]
        if crossed is not None:
            ins.append(("crossed", crossed, lambda side, steps: 0, "inner"))
        if self.part is None:
            return crossed, None
        return tuple(
            line_call(
                middle_kernel, self.flags, *swapped.shape, ins, ["swap", "cross"], "line_middle"
            )
        )

    def end(self, swapped, crossed):
        self.swapped, self.crossed = swapped, crossed
        if self.near is None:
            return None
        return self.first, self.near, swapped, self.other


def send(swap, cross):
    outer, middle = [(0, 1), (3, 2), (1, 0), (2, 3)], [(1, 2), (2, 1)]
    return (
        None if swap is None else lax.ppermute(swap, "tp", outer),
        None if cross is None else lax.ppermute(cross, "tp", middle),
    )


def body(
    tokens, cotangent, membership, ln_gain, ln_bias, w_query, b_query, w_key, b_key, w_value,
    b_value, w_dense, b_dense, w_fc1, b_fc1, w_fc2, b_fc2,
):
    rows, width = tokens.shape
    ctx_count = lax.axis_size("ctx")
    ctx_index = lax.axis_index("ctx")
    local = w_query.shape[1]
    share = local // ctx_count
    mine = 3 * share
    block = min(BLOCK, rows // 2)
    blocks = rows // block

    def mixed(query, key, value):
        lead = query.shape[:-1]
        stacked = jnp.stack(
            [a.reshape(*lead, ctx_count, share) for a in (query, key, value)], axis=-2
        )
        return stacked.reshape(*lead, 3 * local)

    gather = functools.partial(lax.all_gather, axis_name=("dp", "ctx"), tiled=True)
    qkv_weight = gather(mixed(w_query, w_key, w_value), axis=0)
    expand_weight = gather(w_fc1, axis=0)
    qkv_bias = mixed(b_query, b_key, b_value).astype(F32)[None]

    per_prompt = PLEN // CLEN
    prompt_items = GPR * per_prompt
    own_items = rows // CLEN
    items = jnp.arange(own_items * ctx_count, dtype=jnp.int32)
    far = jnp.where(items < prompt_items, items % per_prompt, per_prompt)
    group = jnp.concatenate([items[:prompt_items] // per_prompt, membership[0]])
    own_spots = lax.dynamic_slice_in_dim(far, ctx_index * own_items, own_items)
    tables = rotary_tables()
    per_block = block // CLEN
    item_table = items.reshape(ctx_count, blocks, per_block)
    piece_items = [item_table[:, b].reshape(-1) for b in range(blocks)]
    prompt_count = ctx_count // 2 * per_block

    gain = ln_gain.astype(F32)
    shift = ln_bias.astype(F32)
    (hidden,) = row_call(
        norm_kernel, "norm", 256, rows, (tokens, gain[None], shift[None]),
        (jax.ShapeDtypeStruct((rows, width), BF16),), 0,
    )
    hidden, tables, qkv_weight, fc2_shard = tie(hidden, tables, qkv_weight, w_fc2)
    shrink_weight = gather(fc2_shard, axis=1)
    qkv = qkv_project(hidden, qkv_weight, qkv_bias, tables, own_spots, share)

    def start_exchange(parts):
        if ctx_count == 2:
            low = ctx_index == 0
            away = jnp.where(low, parts[1], parts[0])
            stay = jnp.where(low, parts[0], parts[1])
            return stay, lax.ppermute(away, "ctx", [(0, 1), (1, 0)])
        return (lax.all_to_all(jnp.stack(parts), "ctx", split_axis=0, concat_axis=0, tiled=True),)

    def end_exchange(came):
        if ctx_count == 2:
            low = ctx_index == 0
            stay, came = came
            return [jnp.where(low, stay, came), jnp.where(low, came, stay)]
        return [came[0][c] for c in range(ctx_count)]

    def swap_whole(array):
        swapped = lax.all_to_all(array, "ctx", split_axis=0, concat_axis=0, tiled=True)
        return swapped.reshape(-1, array.shape[-1])

    qkv, hidden = tie(qkv, hidden)
    qkv_all = swap_whole(qkv)
    cut = lambda array, i: array[i * block : (i + 1) * block]

    gelu_slope, activated = row_call(
        expand_kernel, "expand", 256, rows, (hidden, expand_weight, b_fc1.astype(F32)[None]),
        (
            jax.ShapeDtypeStruct((rows, expand_weight.shape[1]), BF16),
            jax.ShapeDtypeStruct((rows, expand_weight.shape[1]), BF16),
        ),
        2 * rows * width * expand_weight.shape[1],
    )
    activated, dense_shard = tie(activated, w_dense)
    dense_weight = gather(dense_shard, axis=1)
    (mlp_out,) = row_call(
        shrink_kernel, "shrink", 256, rows, (activated, shrink_weight),
        (jax.ShapeDtypeStruct((rows, width), BF16),),
        2 * rows * width * expand_weight.shape[1],
    )
    mlp_out, cot_late = tie(mlp_out, cotangent)
    grad_att = grad_attended(cot_late, dense_weight, share)
    qkv_all, mlp_out, grad_att = tie(qkv_all, mlp_out, grad_att)
    grad_all = swap_whole(grad_att)
    turned_v = turn_prompts(qkv_all, share, 2)

    place = lax.axis_index("tp")
    flags = jnp.stack([((place == 0) | (place == 3)).astype(jnp.int32), place // 2])
    gain_row = gain[None]

    env = {}

    def forward(b):
        def run(qkv_in, turned_in):
            o, turned, lse = attend(qkv_in, turned_in, share, group, far, piece_items[b])
            return start_exchange([cut(o, c) for c in range(ctx_count)]), turned, lse

        def keep(out):
            came, env["turned", b], env["lse", b] = out
            env["attended", b] = end_exchange(came)
            for c, part in enumerate(env["attended", b]):
                before = env.get(("whole", c), jnp.zeros((rows, share), BF16))
                env["whole", c] = lax.dynamic_update_slice(before, part, (b * block, 0))

        return run, (qkv_all, turned_v), keep

    def out_part(b):
        def run(mlp, weight, *heads_out):
            pairs = [(part, 0, weight, c) for c, part in enumerate(heads_out)]
            return products(block, width, (mlp, b), pairs, "out_part")

        def keep(out):
            env["part", b] = out

        return run, (mlp_out, dense_weight, *env["attended", b]), keep

    def slope():
        def run(cot, gelu_slope, weight):
            return row_call(
                slope_kernel, "slope", 256, rows, (cot, gelu_slope, weight),
                (
                    jax.ShapeDtypeStruct(gelu_slope.shape, BF16),
                    jax.ShapeDtypeStruct((1, gelu_slope.shape[1]), F32),
                    jax.ShapeDtypeStruct((1, width), F32),
                ),
                2 * rows * width * gelu_slope.shape[1],
            )

        def keep(out):
            env["grad_expand"], env["expand_sum"], env["cot_sum"] = out

        return run, (cotangent, gelu_slope, shrink_weight), keep

    def turn_keys():
        def run(qkv_in):
            return turn_prompts(qkv_in, share, 1)

        def keep(out):
            env["turned_k"] = out

        return run, (qkv_all,), keep

    def backward(b):
        before = () if b == 0 else env["totals"]

        def run(qkv_in, turned_in, grad_in, turned, lse, *before):
            return attend_back(
                qkv_in, turned_in, share, grad_in, turned, lse, tables, group, far, piece_items[b],
                prompt_count, before,
            )

        def keep(out):
            env["dq", b], env["dk", b], env["dv", b] = out[:3]
            env["totals"] = out[3:]

        ins = (qkv_all, env["turned_k"], grad_all, env["turned", b], env["lse", b], *before)
        return run, ins, keep

    def finish():
        def run(dk, dv):
            return finish_prompts(dk, dv, tables)

        def keep(out):
            env["prompt_grads"] = [array.reshape(ctx_count // 2, rows, share) for array in out]

        return run, env["totals"], keep

    def give_back(b):
        def run(prompts, dq, dk, dv):
            parts = []
            for c in range(ctx_count):
                at = c - ctx_count // 2
                near = slice(b * block, (b + 1) * block)
                key = prompts[0][c, near] if at < 0 else cut(dk, at)
                value = prompts[1][c, near] if at < 0 else cut(dv, at)
                parts.append(jnp.concatenate([cut(dq, c), key, value], axis=1))
            return start_exchange(parts)

        def keep(out):
            env["sent_back", b] = out

        return run, (env["prompt_grads"], env["dq", b], env["dk", b], env["dv", b]), keep

    def grad_part(b):
        def run(grad_exp, exp_weight, came, weight):
            grad = jnp.concatenate(end_exchange(came), axis=1)
            pairs = [(grad_exp, b, exp_weight, None), (grad, 0, weight, None)]
            part = products(block, width, None, pairs, "grad_part")
            return part, grad, jnp.sum(grad.astype(F32), axis=0)

        def keep(out):
            env["part", blocks + b], grad, env["qkv_sum", b] = out
            before = env.get("all_qkv", jnp.zeros((rows, 3 * local), BF16))
            env["all_qkv"] = lax.dynamic_update_slice(before, grad, (b * block, 0))

        return run, (env["grad_expand"], expand_weight, env["sent_back", b], qkv_weight), keep

    def weight_grad(name, left, right, axis, part, parts):
        def run(left, right):
            cut_out = lambda a: a[:, part * a.shape[1] // parts : (part + 1) * a.shape[1] // parts]
            left, right = (cut_out(left), right) if axis else (left, cut_out(right))
            return transpose_dot(left, right).astype(BF16)

        def keep(out):
            env[name, part] = lax.psum_scatter(
                out, ("dp", "ctx"), scatter_dimension=axis, tiled=True
            ).astype(F32)

        return run, (left, right), keep

    def put_out(b):
        def run(four, before):
            return place_total(flags, four, b, rows, before)

        def keep(out):
            env["layer_out"] = out

        return run, (env["total", b], env.get("layer_out")), keep

    def put_grad(b, begin, count):
        def run(four, tokens_in, cot_in, before):
            return norm_back(flags, four, b, tokens_in, cot_in, gain_row, before, begin, count)

        def keep(out):
            env["grad_tokens"] = out

        total = env["total", blocks + b]
        return run, (total, tokens, cotangent, env.get("grad_tokens")), keep

    def sums(b):
        def run(near, tokens_in):
            return norm_sums(flags, near, b, tokens_in)

        def keep(out):
            env["gain", b], env["shift", b] = out

        return run, (line.near, tokens), keep

    def add_all(name, axes, pieces):
        def run(arrays):
            return lax.psum(jnp.concatenate(arrays), axes)

        def keep(out):
            env[name] = out

        return run, (pieces(),), keep

    def share_sums():
        def run(parts):
            own = jnp.concatenate([sum(part) for part in parts])
            both = own + lax.ppermute(own, "tp", [(1, 2), (2, 1)])
            return jnp.where(line.outer, lax.ppermute(both, "tp", [(1, 0), (2, 3)]), both)

        def keep(out):
            env["norm_sums"] = out

        parts = [[env[name, b] for b in range(blocks)] for name in ("gain", "shift")]
        return run, (parts,), keep

    def all_pieces():
        total = sum(env["qkv_sum", b] for b in range(blocks))
        return [env["norm_sums"].reshape(-1), total, env["expand_sum"][0], env["cot_sum"][0]]

    def all_attended():
        return jnp.concatenate([env["whole", c] for c in range(ctx_count)], axis=1)

    ticks = 4 * blocks + 2
    plan = [[] for _ in range(ticks + 8)]
    after = [[] for _ in plan]
    turn = 2 * blocks
    last = blocks - 1
    add = lambda slot, make, *args: plan[slot].append(functools.partial(make, *args))
    for b in range(blocks):
        if b:
            add(b - 1, forward, b)
            add(b, out_part, b)
            add(turn + 2 * (b - 1), give_back, b)
        add(last + b, backward, b)
        if b:
            add(turn - 1 + 2 * b, grad_part, b)
        add(turn + 1 + 2 * b, put_out, b)
        add(turn + 2 * b + 2, sums, b)
        if b < last:
            add(turn + 2 * b + 4 + b % 2, put_grad, b, 0, 2)
    add(0, turn_keys)
    after[turn - 2].append(finish)
    add(turn - 1, give_back, 0)
    add(turn - 1, slope)
    after[turn - 1].append(functools.partial(grad_part, 0))
    add(turn, lambda: weight_grad("fc2", activated, cotangent, 1, 0, 1))
    add(turn + 2, lambda: weight_grad("fc1", hidden, env["grad_expand"], 0, 0, 2))
    add(turn + 4, lambda: weight_grad("fc1", hidden, env["grad_expand"], 0, 1, 2))
    add(2 * turn - 2, lambda: weight_grad("qkv", hidden, env["all_qkv"], 0, 0, 1))
    add(2 * turn - 1, lambda: weight_grad("dense", all_attended(), cotangent, 1, 0, 1))
    add(ticks - 1, share_sums)
    after[ticks - 1].append(functools.partial(add_all, "total", ("dp", "ctx"), all_pieces))
    add(ticks - 1, put_grad, last, 0, 1)
    add(ticks, put_grad, last, 1, 1)

    def perform(make):
        run, ins, keep = make()
        keep(run(*ins))

    perform(functools.partial(forward, 0))
    perform(functools.partial(out_part, 0))

    line = Line(flags, tokens, (b_dense.astype(F32) + b_fc2.astype(F32))[None])
    arrived = (None, None)
    for t in range(ticks):
        b, second = divmod(t, 2)
        if second:
            operands = line.middle(*arrived)
        else:
            if t > 0:
                total = line.end(*arrived)
                if total is not None:
                    env["total", b - 2] = total
            operands = line.begin(env.get(("part", b)), b < blocks)
        if t == ticks - 1:
            env["total", 2 * blocks - 1] = (line.first, line.near, line.first, line.near)
        stages = [s for s in (plan[t], after[t]) if s]
        sent = None
        for n, stage in enumerate(stages):
            work = [make() for make in stage]
            operands, ins = tie(operands, [w[1] for w in work])
            if sent is None:
                sent = send(*operands)
            outs = [w[0](*i) for w, i in zip(work, ins)]
            if n == len(stages) - 1:
                arrived, outs = tie(sent, outs)
            for w, out in zip(work, outs):
                w[2](out)
        if not stages:
            arrived = send(*operands)
    env["total", 2 * blocks - 1] = line.end(*arrived)
    for late in plan[ticks:]:
        for make in late:
            perform(make)

    layer_out, grad_tokens = env["layer_out"], env["grad_tokens"]
    sizes = (width, width, 3 * local, w_fc1.shape[1])
    gain_sum, shift_sum, qkv_sum, expand_total, out_sum = jnp.split(
        env["total"], [sum(sizes[: i + 1]) for i in range(len(sizes))]
    )

    def unmixed(array):
        lead = array.shape[:-1]
        parts = array.reshape(*lead, ctx_count, 3, share)
        return tuple(parts[..., t, :].reshape(*lead, local) for t in range(3))

    grad_query, grad_key, grad_value = unmixed(env["qkv", 0])
    sum_query, sum_key, sum_value = unmixed(qkv_sum)
    return (
        layer_out, grad_tokens, gain_sum, shift_sum, grad_query, sum_query, grad_key, sum_key,
        grad_value, sum_value, env["dense", 0], out_sum,
        jnp.concatenate([env["fc1", 0], env["fc1", 1]], axis=1), expand_total, env["fc2", 0], out_sum,
    )


def solution(mesh):
    rows = P(("dp", "ctx"), None)
    down, across = P(("dp", "ctx"), "tp"), P("tp", ("dp", "ctx"))
    wide = P("tp")
    ins = (
        rows, rows, P("dp", None), P(), P(), down, wide, down, wide, down, wide, across, P(), down,
        wide, across, P(),
    )
    outs = (
        rows, rows, P(), P(), down, wide, down, wide, down, wide, across, P(), down, wide, across,
        P(),
    )
    return jax.shard_map(body, mesh=mesh, in_specs=ins, out_specs=outs, check_vma=False)
```

```python
import functools

import jax
import jax.numpy as jnp
from jax import lax
from jax.experimental import pallas as pl
from jax.experimental.pallas import tpu as pltpu
from jax.sharding import PartitionSpec as P

HDIM = 64
ROT = 32
PLEN = 2048
CLEN = 256
GPR = 2
BLOCK = 1024
VMEM = 56 * 2**20
F32 = jnp.float32
BF16 = jnp.bfloat16
NT = (((1,), (1,)), ((), ()))
NN = (((1,), (0,)), ((), ()))


def cost(bytes_accessed, flops=0):
    return pl.CostEstimate(flops=flops, bytes_accessed=bytes_accessed, transcendentals=0)


def dot(left, right, dims):
    return lax.dot_general(left, right, dims, preferred_element_type=F32)


def transpose_dot(left, right):
    return jnp.einsum("ra,rb->ab", left, right, preferred_element_type=F32)


def dot_back(left, right):
    return jnp.einsum("rb,ab->ra", left, right, preferred_element_type=F32)


def norm_apply(matrix, norm_gain, norm_shift):
    center = matrix - jnp.mean(matrix, axis=-1, keepdims=True)
    spread = jnp.mean(center * center, axis=-1, keepdims=True)
    return center * lax.rsqrt(spread + 1e-05) * norm_gain + norm_shift


def gelu_parts(v):
    scale = (2.0 / jnp.pi) ** 0.5
    square = v * v
    t = jnp.tanh(v * (scale + (scale * 0.044715) * square))
    half = 0.5 * v
    value = half + half * t
    slope = (0.5 + 0.5 * t) + (half - half * t * t) * (scale + (scale * 3 * 0.044715) * square)
    return value, slope


def rotary_tables():
    half = ROT // 2
    positions = jnp.arange(PLEN + CLEN, dtype=F32)
    frequency = 10000.0 ** (-2.0 * jnp.arange(half, dtype=F32) / ROT)
    angles = positions[:, None] * frequency[None, :]
    cosine, sine = jnp.cos(angles), jnp.sin(angles)
    ones = jnp.ones((PLEN + CLEN, HDIM - ROT), F32)
    zeros = jnp.zeros_like(ones)
    none = jnp.zeros_like(sine)
    head = (
        jnp.concatenate([cosine, cosine, ones], axis=1),
        jnp.concatenate([-sine, none, zeros], axis=1),
        jnp.concatenate([none, sine, zeros], axis=1),
    )
    return tuple(jnp.concatenate([table, table], axis=1) for table in head)


def rotated(values, cosine, first, second):
    half = ROT // 2
    return (
        values * cosine
        + pltpu.roll(values, 2 * HDIM - half, 1) * first
        + pltpu.roll(values, half, 1) * second
    )


def ahead(count, first, second):
    held = first(0)
    for i in range(count):
        following = first(i + 1) if i + 1 < count else None
        second(i, held)
        held = following


def norm_kernel(x_ref, gain_ref, shift_ref, out_ref):
    x = x_ref[...].astype(F32)
    out_ref[...] = norm_apply(x, gain_ref[...], shift_ref[...]).astype(BF16)


def qkv_kernel(
    share, where_ref, hidden_ref, weight_ref, bias_ref, cos_ref, first_ref, second_ref, out_ref
):
    hidden = hidden_ref[...]
    cosine, first, second = cos_ref[...], first_ref[...], second_ref[...]
    lane = lax.broadcasted_iota(jnp.int32, (1, 2 * HDIM), 1)
    member_width = out_ref.shape[2]

    def linear(i):
        at = slice(i * 512, (i + 1) * 512)
        return dot(hidden, weight_ref[:, at], NN) + bias_ref[:, at]

    def turn(i, lin):
        begin = i * 512
        for column in range(0, 512, 2 * HDIM):
            part = lin[:, column : column + 2 * HDIM]
            turns = [((begin + column + off) // share) % 3 < 2 for off in (0, HDIM)]
            if any(turns):
                turned = rotated(part, cosine, first, second)
                if not all(turns):
                    keep = lane < HDIM if turns[0] else lane >= HDIM
                    turned = jnp.where(keep, turned, part)
                part = turned
            part = part.astype(BF16)
            size = min(2 * HDIM, share)
            for off in range(0, 2 * HDIM, size):
                member, place = divmod(begin + column + off, member_width)
                out_ref[member, :, place : place + size] = part[:, off : off + size]

    ahead(weight_ref.shape[1] // 512, linear, turn)


def qkv_project(hidden, weight, bias, tables, spots, share):
    rows, width = hidden.shape
    outs = weight.shape[1]
    count = 256
    whole = lambda shape: pl.BlockSpec(shape, lambda i, *_: (0, 0))
    table = pl.BlockSpec((count, 2 * HDIM), lambda i, spots: (spots[i], 0))
    return pl.pallas_call(
        functools.partial(qkv_kernel, share),
        grid_spec=pltpu.PrefetchScalarGridSpec(
            num_scalar_prefetch=1,
            grid=(rows // count,),
            in_specs=[
                pl.BlockSpec((count, width), lambda i, *_: (i, 0)),
                whole((width, outs)),
                whole((1, outs)),
                table,
                table,
                table,
            ],
            out_specs=pl.BlockSpec(
                (outs // (3 * share), count, 3 * share), lambda i, *_: (0, i, 0)
            ),
        ),
        out_shape=jax.ShapeDtypeStruct((outs // (3 * share), rows, 3 * share), BF16),
        compiler_params=pltpu.CompilerParams(vmem_limit_bytes=VMEM),
        cost_estimate=pl.CostEstimate(
            flops=2 * rows * width * outs, bytes_accessed=2 * rows * (2 * width + outs),
            transcendentals=0,
        ),
        name="qkv_project",
    )(spots, hidden, weight, bias, *tables)


def expand_kernel(hidden_ref, weight_ref, bias_ref, slope_ref, out_ref):
    hidden = hidden_ref[...]

    def linear(i):
        at = slice(i * 512, (i + 1) * 512)
        return dot(hidden, weight_ref[:, at], NN) + bias_ref[:, at]

    def keep(i, lin):
        at = slice(i * 512, (i + 1) * 512)
        value, slope = gelu_parts(lin)
        out_ref[:, at] = value.astype(BF16)
        slope_ref[:, at] = slope.astype(BF16)

    ahead(weight_ref.shape[1] // 512, linear, keep)


def shrink_kernel(act_ref, weight_ref, out_ref):
    out_ref[...] = dot(act_ref[...], weight_ref[...], NN).astype(BF16)


def slope_kernel(cot_ref, slope_ref, weight_ref, grad_ref, sum_ref, cot_sum_ref):
    @pl.when(pl.program_id(0) == 0)
    def _():
        sum_ref[...] = jnp.zeros_like(sum_ref)
        cot_sum_ref[...] = jnp.zeros_like(cot_sum_ref)

    cot = cot_ref[...]
    cot_sum_ref[...] += jnp.sum(cot.astype(F32), axis=0, keepdims=True)

    def back(i):
        return dot(cot, weight_ref[i * 512 : (i + 1) * 512, :], NT)

    def keep(i, grad):
        at = slice(i * 512, (i + 1) * 512)
        grad = (slope_ref[:, at].astype(F32) * grad).astype(BF16)
        grad_ref[:, at] = grad
        sum_ref[:, at] += jnp.sum(grad.astype(F32), axis=0, keepdims=True)

    ahead(weight_ref.shape[0] // 512, back, keep)


def grad_attended_kernel(cot_ref, weight_ref, out_ref):
    cot = cot_ref[...]
    share = out_ref.shape[2]
    whole = dot(cot, weight_ref[...], NT).astype(BF16)
    for c in range(out_ref.shape[0]):
        out_ref[c] = whole[:, c * share : (c + 1) * share]


def grad_attended(cotangent, weight, share):
    rows, width = cotangent.shape
    local = weight.shape[0]
    count = 512
    return pl.pallas_call(
        grad_attended_kernel,
        grid=(rows // count,),
        in_specs=[
            pl.BlockSpec((count, width), lambda i: (i, 0)),
            pl.BlockSpec((local, width), lambda i: (0, 0)),
        ],
        out_specs=pl.BlockSpec((local // share, count, share), lambda i: (0, i, 0)),
        out_shape=jax.ShapeDtypeStruct((local // share, rows, share), BF16),
        compiler_params=pltpu.CompilerParams(vmem_limit_bytes=VMEM),
        cost_estimate=pl.CostEstimate(
            flops=2 * rows * width * local, bytes_accessed=2 * rows * (width + local),
            transcendentals=0,
        ),
        name="grad_attended",
    )(cotangent, weight)


def row_call(kernel, name, count, rows, in_arrays, outs, flops):
    def spec(shape):
        if shape[0] == rows:
            return pl.BlockSpec((count, shape[1]), lambda i: (i, 0))
        return pl.BlockSpec(shape, lambda i: (0, 0))

    return pl.pallas_call(
        kernel,
        grid=(rows // count,),
        in_specs=[spec(a.shape) for a in in_arrays],
        out_specs=[spec(o.shape) for o in outs],
        out_shape=outs,
        compiler_params=pltpu.CompilerParams(vmem_limit_bytes=VMEM),
        cost_estimate=pl.CostEstimate(
            flops=flops,
            bytes_accessed=sum(a.size * a.dtype.itemsize for a in (*in_arrays, *outs)),
            transcendentals=0,
        ),
        name=name,
    )(*in_arrays)


def products_kernel(kinds, has_base, *refs):
    out_ref = refs[-1]
    base_ref = refs[0] if has_base else None
    pairs = refs[has_base:-1]
    count = 256

    @pl.loop(0, out_ref.shape[0] // count)
    def _(i):
        rows = pl.ds(pl.multiple_of(i * count, count), count)
        total = base_ref[rows, :].astype(F32) if has_base else None
        for n, dims in enumerate(kinds):
            step = dot(pairs[2 * n][rows, :], pairs[2 * n + 1][...], dims)
            total = step if total is None else total + step
        out_ref[rows, :] = total.astype(BF16)


def products(count, outs, base, pairs, name):
    tile = 512
    arrays, specs, kinds = [], [], []
    flops = 0
    if base is not None:
        arrays.append(base[0])
        specs.append(pl.BlockSpec((count, tile), lambda n, at=base[1]: (at, n)))
    for left, at, right, right_at in pairs:
        depth = left.shape[1]
        arrays += [left, right]
        specs.append(pl.BlockSpec((count, depth), lambda n, at=at: (at, 0)))
        if right_at is None:
            specs.append(pl.BlockSpec((tile, depth), lambda n: (n, 0)))
            kinds.append(NT)
        else:
            specs.append(pl.BlockSpec((depth, tile), lambda n, at=right_at: (at, n)))
            kinds.append(NN)
        flops += 2 * count * depth * outs
    return pl.pallas_call(
        functools.partial(products_kernel, kinds, base is not None),
        grid=(outs // tile,),
        in_specs=specs,
        out_specs=pl.BlockSpec((count, tile), lambda n: (0, n)),
        out_shape=jax.ShapeDtypeStruct((count, outs), BF16),
        compiler_params=pltpu.CompilerParams(vmem_limit_bytes=VMEM),
        cost_estimate=pl.CostEstimate(
            flops=flops, bytes_accessed=flops // 512, transcendentals=0
        ),
        name=name,
    )(*arrays)


def heads_split(array, heads):
    if heads == 1:
        return [array]
    lane = lax.broadcasted_iota(jnp.int32, array.shape, 1)
    return [jnp.where(lane // HDIM == h, array, jnp.zeros((), array.dtype)) for h in range(heads)]


def near_mask():
    key = lax.broadcasted_iota(jnp.int32, (CLEN, CLEN), 0)
    query = lax.broadcasted_iota(jnp.int32, (CLEN, CLEN), 1)
    return key <= query


def over_far(base, count, big, step):
    per = big // CLEN
    full = count // per

    @pl.loop(0, full)
    def _(i):
        step(pl.multiple_of(base + i * big, CLEN), big)

    @pl.loop(full * per, count)
    def _(i):
        step(pl.multiple_of(base + i * CLEN, CLEN), CLEN)


def attend_kernel(
    big, group_ref, far_ref, item_ref, q_ref, ko_ref, vo_ref, kp_ref, vt_s, o_ref, ot_ref,
    lse_ref, m_s, l_s, acc_s,
):
    heads = q_ref.shape[1] // HDIM
    item = item_ref[pl.program_id(1)]
    base = group_ref[item] * PLEN

    queries = heads_split(q_ref[...] * BF16(HDIM**-0.5), heads)
    mask = near_mask()
    keys = ko_ref[...]
    values = vo_ref[...].T
    spans = [slice(h * HDIM, (h + 1) * HDIM) for h in range(heads)]
    scores = [dot(keys, queries[h], NT) for h in range(heads)]
    for h in range(heads):
        s = jnp.where(mask, scores[h], -1e30)
        m = jnp.max(s, axis=0, keepdims=True)
        p = jnp.exp(s - m)
        m_s[h] = m
        l_s[h] = jnp.sum(p, axis=0, keepdims=True)
        acc_s[h] = dot(values[spans[h]], p.astype(BF16), NN)

    def step(first, size):
        k = kp_ref[pl.ds(first, size), :]
        scores = [dot(k, queries[h], NT) for h in range(heads)]
        for h in range(heads):
            old = m_s[h]
            m = jnp.maximum(old, jnp.max(scores[h], axis=0, keepdims=True))
            p = jnp.exp(scores[h] - m)
            a = jnp.exp(old - m)
            m_s[h] = m
            l_s[h] = l_s[h] * a + jnp.sum(p, axis=0, keepdims=True)
            acc_s[h] = acc_s[h] * a + dot(vt_s[spans[h], pl.ds(first, size)], p.astype(BF16), NN)

    over_far(base, far_ref[item], big, step)
    for h in range(heads):
        ot_ref[spans[h], :] = acc_s[h] * (1.0 / l_s[h])
        lse_ref[0, h : h + 1, :] = m_s[h] + jnp.log(l_s[h])
    o_ref[...] = ot_ref[...].T.astype(BF16)


def turn_kernel(in_ref, out_ref):
    for begin in range(0, in_ref.shape[0], CLEN):
        out_ref[:, begin : begin + CLEN] = in_ref[begin : begin + CLEN, :].T


def turn_prompts(qkv, width, which):
    wide = min(4 * HDIM, width)
    arrays, ats = split_columns(qkv, width)
    count = PLEN // 2
    return pl.pallas_call(
        turn_kernel,
        grid=(width // wide, GPR * PLEN // count),
        in_specs=[pl.BlockSpec((count, wide), lambda h, i: (i, ats[which] + h))],
        out_specs=pl.BlockSpec((wide, count), lambda h, i: (h, i)),
        out_shape=jax.ShapeDtypeStruct((width, GPR * PLEN), BF16),
        compiler_params=pltpu.CompilerParams(vmem_limit_bytes=VMEM),
        cost_estimate=cost(width * GPR * PLEN * 8),
        name="turn_prompts",
    )(arrays[which])


def turned_back(values, tables):
    width = values.shape[1]
    cosine, first, second = (ref[...] for ref in tables)
    wide = 2 * HDIM
    if width < wide:
        values = jnp.concatenate([values, values], axis=1)
    parts = [
        rotated(values[:, c : c + wide], cosine, -first, -second)
        for c in range(0, values.shape[1], wide)
    ]
    out = parts[0] if len(parts) == 1 else jnp.concatenate(parts, axis=1)
    return out[:, :width].astype(BF16)


def attend_back_kernel(big, first_piece, prompt_items, prompt_count, *refs):
    group_ref, far_ref, item_ref = refs[:3]
    q_ref, ko_ref, vo_ref, do_ref, ot_ref, lse_ref, kp_ref, vp_ref, kt_s = refs[3:12]
    tables = refs[12:15]
    before = () if first_piece else refs[15:17]
    dq_ref, dk_ref, dv_ref, dk_s, dv_s, dq_s, near_k, near_v = refs[15 + len(before) :]
    width = q_ref.shape[1]
    heads = width // HDIM
    turn = pl.program_id(1)
    item = item_ref[turn]
    base = group_ref[item] * PLEN

    @pl.when(turn == 0)
    def _():
        if first_piece:
            dk_s[...] = jnp.zeros_like(dk_s)
            dv_s[...] = jnp.zeros_like(dv_s)
        else:
            dk_s[...] = before[0][...]
            dv_s[...] = before[1][...]

    do = do_ref[...]
    queries = heads_split(q_ref[...] * BF16(HDIM**-0.5), heads)
    grads = heads_split(do, heads)
    query_cat = jnp.concatenate(queries, axis=0)
    grad_cat = jnp.concatenate(grads, axis=0)
    spans = [slice(h * HDIM, (h + 1) * HDIM) for h in range(heads)]
    product = ot_ref[...] * do.astype(F32).T
    center = [jnp.sum(product[span], axis=0, keepdims=True) for span in spans]
    lse = [lse_ref[0, h : h + 1, :] for h in range(heads)]
    mask = near_mask()

    def piece(k, v, kt, near):
        chance, grad_scores = [], []
        scores = [dot(k, queries[h], NT) for h in range(heads)]
        grad_chance = [dot(v, grads[h], NT) for h in range(heads)]
        for h in range(heads):
            p = jnp.exp(scores[h] - lse[h])
            if near:
                p = jnp.where(mask, p, 0.0)
            grad_scores.append((p * (grad_chance[h] - center[h])).astype(BF16))
            chance.append(p.astype(BF16))
        for h in range(heads):
            step = dot(kt(spans[h]), grad_scores[h], NN)
            if near:
                dq_s[spans[h], :] = step
            else:
                dq_s[spans[h], :] += step
        return (
            dot(jnp.concatenate(grad_scores, axis=1), query_cat, NN),
            dot(jnp.concatenate(chance, axis=1), grad_cat, NN),
        )

    own = ko_ref[...]
    own_t = own.T
    near_k[...], near_v[...] = piece(own, vo_ref[...], lambda span: own_t[span], True)

    @pl.when(turn < prompt_count)
    def _():
        rows = pl.ds(pl.multiple_of(item * CLEN, CLEN), CLEN)
        dk_s[rows, :] += near_k[...]
        dv_s[rows, :] += near_v[...]

    @pl.when(turn >= prompt_count)
    def _():
        dk_ref[...] = turned_back(near_k[...], tables)
        dv_ref[...] = near_v[...].astype(BF16)

    def step(first, size):
        rows = pl.ds(first, size)
        k_step, v_step = piece(
            kp_ref[rows, :], vp_ref[rows, :], lambda span: kt_s[span, rows], False
        )
        dk_s[rows, :] += k_step
        dv_s[rows, :] += v_step

    over_far(base, far_ref[item], big, step)
    dq_ref[...] = turned_back((dq_s[...] * (HDIM**-0.5)).T, tables)


def finish_kernel(dk_ref, dv_ref, cos_ref, first_ref, second_ref, ok_ref, ov_ref):
    ok_ref[...] = turned_back(dk_ref[...], (cos_ref, first_ref, second_ref))
    ov_ref[...] = dv_ref[...].astype(BF16)


def finish_prompts(dk, dv, tables):
    rows, width = dk.shape
    wide = min(4 * HDIM, width)
    count = PLEN // 2
    block = pl.BlockSpec((count, wide), lambda h, i: (i, h))
    table = pl.BlockSpec((count, 2 * HDIM), lambda h, i: (i % (PLEN // count), 0))
    return pl.pallas_call(
        finish_kernel,
        grid=(width // wide, rows // count),
        in_specs=[block, block, table, table, table],
        out_specs=[block, block],
        out_shape=[jax.ShapeDtypeStruct((rows, width), BF16)] * 2,
        compiler_params=pltpu.CompilerParams(vmem_limit_bytes=VMEM),
        cost_estimate=cost(rows * width * 30),
        name="finish_prompts",
    )(dk, dv, *tables)


def split_columns(qkv, width):
    wide = min(4 * HDIM, width)
    if wide % 128 == 0:
        return (qkv, qkv, qkv), tuple(t * width // wide for t in range(3))
    return tuple(qkv[:, t * width : (t + 1) * width] for t in range(3)), (0, 0, 0)


def attention_specs(width):
    wide = min(4 * HDIM, width)
    heads = wide // HDIM
    return (
        wide,
        heads,
        lambda at: pl.BlockSpec((CLEN, wide), lambda h, i, g, f, items: (items[i], at + h)),
        pl.BlockSpec((CLEN, wide), lambda h, i, *_: (i, h)),
        pl.BlockSpec((wide, CLEN), lambda h, i, *_: (h, i)),
        lambda at: pl.BlockSpec((GPR * PLEN, wide), lambda h, i, *_: (0, at + h)),
        pl.BlockSpec((1, heads, CLEN), lambda h, i, *_: (h, 0, i)),
    )


def attend(qkv, turned_v, width, group, far, items):
    rows = items.shape[0] * CLEN
    wide, heads, picked, block, turned, prompts, stats = attention_specs(width)
    (q, k, v), (qa, ka, va) = split_columns(qkv, width)
    pairs = rows * (PLEN + CLEN) * width // HDIM
    return pl.pallas_call(
        functools.partial(attend_kernel, 1024),
        grid_spec=pltpu.PrefetchScalarGridSpec(
            num_scalar_prefetch=3,
            grid=(width // wide, rows // CLEN),
            in_specs=[
                picked(qa), picked(ka), picked(va), prompts(ka),
                pl.BlockSpec((wide, GPR * PLEN), lambda h, i, *_: (h, 0)),
            ],
            out_specs=[block, turned, stats],
            scratch_shapes=[
                pltpu.VMEM((heads, 1, CLEN), F32),
                pltpu.VMEM((heads, 1, CLEN), F32),
                pltpu.VMEM((heads, HDIM, CLEN), F32),
            ],
        ),
        out_shape=[
            jax.ShapeDtypeStruct((rows, width), BF16),
            jax.ShapeDtypeStruct((width, rows), F32),
            jax.ShapeDtypeStruct((width // wide, heads, rows), F32),
        ],
        compiler_params=pltpu.CompilerParams(vmem_limit_bytes=VMEM),
        cost_estimate=pl.CostEstimate(
            flops=4 * pairs * 256, bytes_accessed=rows * width * 12, transcendentals=pairs
        ),
        name="attend",
    )(group, far, items, q, k, v, k, turned_v)


def attend_back(
    qkv, turned_k, width, grad, turned_out, lse, tables, group, far, items, prompt_count, before
):
    rows = items.shape[0] * CLEN
    wide, heads, picked, block, turned, prompts, stats = attention_specs(width)
    (q, k, v), (qa, ka, va) = split_columns(qkv, width)
    table = pl.BlockSpec((CLEN, 2 * HDIM), lambda h, i, g, f, items: (f[items[i]], 0))
    total = pl.BlockSpec((GPR * PLEN, wide), lambda h, i, *_: (0, h))
    late = pl.BlockSpec((CLEN, wide), lambda h, i, *_: (jnp.maximum(i - prompt_count, 0), h))
    pairs = rows * (PLEN + CLEN) * width // HDIM
    first = not before
    late_rows = rows - prompt_count * CLEN
    return pl.pallas_call(
        functools.partial(attend_back_kernel, 1024, first, GPR * PLEN // CLEN, prompt_count),
        grid_spec=pltpu.PrefetchScalarGridSpec(
            num_scalar_prefetch=3,
            grid=(width // wide, rows // CLEN),
            in_specs=[
                picked(qa), picked(ka), picked(va), picked(0), turned, stats, prompts(ka),
                prompts(va), pl.BlockSpec((wide, GPR * PLEN), lambda h, i, *_: (h, 0)), table, table,
                table,
            ]
            + [total] * len(before),
            out_specs=[block, late, late, total, total],
            scratch_shapes=[
                pltpu.VMEM((wide, CLEN), F32),
                pltpu.VMEM((CLEN, wide), F32),
                pltpu.VMEM((CLEN, wide), F32),
            ],
        ),
        out_shape=[jax.ShapeDtypeStruct((rows, width), BF16)]
        + [jax.ShapeDtypeStruct((late_rows, width), BF16)] * 2
        + [jax.ShapeDtypeStruct((GPR * PLEN, width), F32)] * 2,
        input_output_aliases={} if first else {15: 3, 16: 4},
        compiler_params=pltpu.CompilerParams(vmem_limit_bytes=VMEM),
        cost_estimate=pl.CostEstimate(
            flops=8 * pairs * 256, bytes_accessed=rows * width * 24, transcendentals=pairs
        ),
        name="attend_back",
    )(group, far, items, q, k, v, grad, turned_out, lse, k, v, turned_k, *tables, *before)


def tie(*trees):
    return lax.optimization_barrier(trees)


COUNT = 256


def begin_kernel(names, flag_ref, *refs):
    refs = dict(zip(names, refs))
    outer = flag_ref[0] == 1
    out_ref = refs["out"]

    @pl.when(outer)
    def _():
        out_ref[...] = refs["next"][...] if "next" in refs else jnp.zeros_like(out_ref)

    @pl.when(flag_ref[0] == 0)
    def _():
        if "part" not in refs:
            out_ref[...] = jnp.zeros_like(out_ref)
            return
        total = (
            refs["part"][...].astype(F32)
            + refs["swapped"][...].astype(F32)
            + refs["crossed"][...].astype(F32)
        )
        if "tokens" in refs:
            total = total + refs["tokens"][...].astype(F32) + refs["bias"][...]
        out_ref[...] = total.astype(BF16)


def middle_kernel(names, flag_ref, *refs):
    refs = dict(zip(names, refs))
    outer = flag_ref[0] == 1
    swap_ref = refs["swap"]

    @pl.when(outer)
    def _():
        swap_ref[...] = refs["near"][...] if "near" in refs else jnp.zeros_like(swap_ref)

    @pl.when(flag_ref[0] == 0)
    def _():
        swap_ref[...] = refs["crossed"][...] if "crossed" in refs else jnp.zeros_like(swap_ref)

    if "far" in refs:
        refs["cross"][...] = (
            refs["far"][...].astype(F32) + refs["swapped"][...].astype(F32)
        ).astype(BF16)


def line_call(kernel, flags, rows, width, ins, outs, name):
    steps = rows // COUNT

    def spec(shape, first, who):
        if shape[0] == 1:
            return pl.BlockSpec(shape, lambda i, flag: (0, 0))

        def index(i, flag):
            needed = {"all": 1, "outer": flag[0], "inner": 1 - flag[0]}[who]
            return (first(flag[1], steps) + i * needed, 0)

        return pl.BlockSpec((COUNT, width), index)

    return pl.pallas_call(
        functools.partial(kernel, [i[0] for i in ins] + outs),
        grid_spec=pltpu.PrefetchScalarGridSpec(
            num_scalar_prefetch=1,
            grid=(steps,),
            in_specs=[spec(array.shape, first, who) for _, array, first, who in ins],
            out_specs=[pl.BlockSpec((COUNT, width), lambda i, flag: (i, 0)) for _ in outs],
        ),
        out_shape=[jax.ShapeDtypeStruct((rows, width), BF16) for _ in outs],
        compiler_params=pltpu.CompilerParams(vmem_limit_bytes=VMEM),
        cost_estimate=cost(rows * width * 16),
        name=name,
    )(flags, *[i[1] for i in ins])


def total_specs(half, width, begin):
    outer = lambda flag: flag[0]
    inner = lambda flag: 1 - flag[0]

    def spec(part, who):
        return pl.BlockSpec(
            (COUNT, width), lambda p, i, flag: (i * who(flag) * (p + begin == part), 0)
        )

    return [spec(0, outer), spec(0, inner), spec(1, outer), spec(1, inner)]


def total_of(flag_ref, refs, keep, begin):
    part = pl.program_id(0) + begin
    for at, ref in enumerate(refs):
        right = (part == at // 2) & (flag_ref[0] == 1 - at % 2)

        @pl.when(right)
        def _(ref=ref):
            keep(ref[...])


def rows_of(block, half, begin):
    steps = half // COUNT

    def index(p, i, flag):
        return ((2 * block + (flag[1] + p + begin) % 2) * steps + i, 0)

    return index


def place_kernel(flag_ref, a, b, c, d, *rest):
    out_ref = rest[-1]

    def keep(value):
        out_ref[...] = value

    total_of(flag_ref, (a, b, c, d), keep, 0)


def place_total(flags, four, block, rows, before):
    half, width = four[0].shape
    return pl.pallas_call(
        place_kernel,
        grid_spec=pltpu.PrefetchScalarGridSpec(
            num_scalar_prefetch=1,
            grid=(2, half // COUNT),
            in_specs=total_specs(half, width, 0)
            + [pl.BlockSpec(memory_space=pl.ANY)] * (before is not None),
            out_specs=pl.BlockSpec((COUNT, width), rows_of(block, half, 0)),
        ),
        out_shape=jax.ShapeDtypeStruct((rows, width), BF16),
        input_output_aliases={} if before is None else {5: 0},
        compiler_params=pltpu.CompilerParams(vmem_limit_bytes=VMEM),
        cost_estimate=cost(half * width * 24),
        name="place_total",
    )(flags, *four, *(() if before is None else (before,)))


def normed_rows(tokens):
    x = tokens.astype(F32)
    center = x - jnp.mean(x, axis=-1, keepdims=True)
    inverse = lax.rsqrt(jnp.mean(center * center, axis=-1, keepdims=True) + 1e-05)
    return center * inverse, inverse


def norm_back_kernel(begin, flag_ref, a, b, c, d, x_ref, cot_ref, gain_ref, *rest):
    out_ref, held = rest[-2:]

    def keep(value):
        held[...] = value

    total_of(flag_ref, (a, b, c, d), keep, begin)
    normed, inverse = normed_rows(x_ref[...])
    scaled = held[...].astype(F32) * gain_ref[...]
    grad = scaled - jnp.mean(scaled, axis=-1, keepdims=True)
    grad = inverse * (grad - normed * jnp.mean(scaled * normed, axis=-1, keepdims=True))
    out_ref[...] = cot_ref[...].astype(F32) + grad


def norm_back(flags, four, block, tokens, cotangent, gain, before, begin, count):
    half, width = four[0].shape
    row = pl.BlockSpec((1, width), lambda p, i, flag: (0, 0))
    whole = pl.BlockSpec((COUNT, width), rows_of(block, half, begin))
    return pl.pallas_call(
        functools.partial(norm_back_kernel, begin),
        grid_spec=pltpu.PrefetchScalarGridSpec(
            num_scalar_prefetch=1,
            grid=(count, half // COUNT),
            in_specs=total_specs(half, width, begin)
            + [whole, whole, row]
            + [pl.BlockSpec(memory_space=pl.ANY)] * (before is not None),
            out_specs=whole,
            scratch_shapes=[pltpu.VMEM((COUNT, width), BF16)],
        ),
        out_shape=jax.ShapeDtypeStruct(tokens.shape, F32),
        input_output_aliases={} if before is None else {8: 0},
        compiler_params=pltpu.CompilerParams(vmem_limit_bytes=VMEM),
        cost_estimate=cost(half * width * 24 * count),
        name="norm_back",
    )(flags, *four, tokens, cotangent, gain, *(() if before is None else (before,)))


def norm_sums_kernel(flag_ref, total_ref, x_ref, gain_sum, shift_sum):
    @pl.when(pl.program_id(0) == 0)
    def _():
        gain_sum[...] = jnp.zeros_like(gain_sum)
        shift_sum[...] = jnp.zeros_like(shift_sum)

    @pl.when(flag_ref[0] == 0)
    def _():
        total = total_ref[...].astype(F32)
        gain_sum[...] += jnp.sum(total * normed_rows(x_ref[...])[0], axis=0, keepdims=True)
        shift_sum[...] += jnp.sum(total, axis=0, keepdims=True)


def norm_sums(flags, near, block, tokens):
    half, width = near.shape
    steps = half // COUNT
    row = pl.BlockSpec((1, width), lambda i, flag: (0, 0))
    return pl.pallas_call(
        norm_sums_kernel,
        grid_spec=pltpu.PrefetchScalarGridSpec(
            num_scalar_prefetch=1,
            grid=(steps,),
            in_specs=[
                pl.BlockSpec((COUNT, width), lambda i, flag: (i * (1 - flag[0]), 0)),
                pl.BlockSpec(
                    (COUNT, width),
                    lambda i, flag: ((2 * block + flag[1]) * steps + i * (1 - flag[0]), 0),
                ),
            ],
            out_specs=[row, row],
        ),
        out_shape=[jax.ShapeDtypeStruct((1, width), F32)] * 2,
        compiler_params=pltpu.CompilerParams(vmem_limit_bytes=VMEM),
        cost_estimate=cost(half * width * 10),
        name="norm_sums",
    )(flags, near, tokens)


class Line:
    def __init__(self, flags, tokens, bias):
        self.flags, self.tokens, self.bias = flags, tokens, bias
        self.outer = flags[0] == 1
        self.part = self.near = None
        self.block = -1

    def begin(self, part, with_input):
        zero = lambda side, steps: 0
        near = lambda side, steps: side * steps
        ins = []
        if self.part is not None:
            ins += [
                ("part", self.part, near, "inner"),
                ("swapped", self.swapped, zero, "inner"),
                ("crossed", self.crossed, zero, "inner"),
            ]
            if self.with_input:
                block = self.block
                ins += [
                    ("tokens", self.tokens, lambda side, steps: (2 * block + side) * steps, "inner"),
                    ("bias", self.bias, zero, "all"),
                ]
        if part is not None:
            ins.append(("next", part, lambda side, steps: (1 - side) * steps, "outer"))
        shape = (self.part if part is None else part).shape
        (out,) = line_call(
            begin_kernel, self.flags, shape[0] // 2, shape[1], ins, ["out"], "line_begin"
        )
        had = self.part is not None
        self.part, self.with_input = part, with_input
        self.block += 1
        self.near = out if had else None
        return out, self.near

    def middle(self, swapped, crossed):
        self.first, self.other = swapped, crossed
        ins = []
        if self.part is not None:
            ins += [
                ("near", self.part, lambda side, steps: side * steps, "outer"),
                ("far", self.part, lambda side, steps: (1 - side) * steps, "inner"),
                ("swapped", swapped, lambda side, steps: 0, "inner"),
            ]
        if crossed is not None:
            ins.append(("crossed", crossed, lambda side, steps: 0, "inner"))
        if self.part is None:
            return crossed, None
        return tuple(
            line_call(
                middle_kernel, self.flags, *swapped.shape, ins, ["swap", "cross"], "line_middle"
            )
        )

    def end(self, swapped, crossed):
        self.swapped, self.crossed = swapped, crossed
        if self.near is None:
            return None
        return self.first, self.near, swapped, self.other


def send(swap, cross):
    outer, middle = [(0, 1), (3, 2), (1, 0), (2, 3)], [(1, 2), (2, 1)]
    return (
        None if swap is None else lax.ppermute(swap, "tp", outer),
        None if cross is None else lax.ppermute(cross, "tp", middle),
    )


def body(
    tokens, cotangent, membership, ln_gain, ln_bias, w_query, b_query, w_key, b_key, w_value,
    b_value, w_dense, b_dense, w_fc1, b_fc1, w_fc2, b_fc2,
):
    rows, width = tokens.shape
    ctx_count = lax.axis_size("ctx")
    ctx_index = lax.axis_index("ctx")
    local = w_query.shape[1]
    share = local // ctx_count
    mine = 3 * share
    block = min(BLOCK, rows // 2)
    blocks = rows // block

    def mixed(query, key, value):
        lead = query.shape[:-1]
        stacked = jnp.stack(
            [a.reshape(*lead, ctx_count, share) for a in (query, key, value)], axis=-2
        )
        return stacked.reshape(*lead, 3 * local)

    gather = functools.partial(lax.all_gather, axis_name=("dp", "ctx"), tiled=True)
    qkv_weight = gather(mixed(w_query, w_key, w_value), axis=0)
    expand_weight = gather(w_fc1, axis=0)
    qkv_bias = mixed(b_query, b_key, b_value).astype(F32)[None]

    per_prompt = PLEN // CLEN
    prompt_items = GPR * per_prompt
    own_items = rows // CLEN
    items = jnp.arange(own_items * ctx_count, dtype=jnp.int32)
    far = jnp.where(items < prompt_items, items % per_prompt, per_prompt)
    group = jnp.concatenate([items[:prompt_items] // per_prompt, membership[0]])
    own_spots = lax.dynamic_slice_in_dim(far, ctx_index * own_items, own_items)
    tables = rotary_tables()
    per_block = block // CLEN
    item_table = items.reshape(ctx_count, blocks, per_block)
    piece_items = [item_table[:, b].reshape(-1) for b in range(blocks)]
    prompt_count = ctx_count // 2 * per_block

    gain = ln_gain.astype(F32)
    shift = ln_bias.astype(F32)
    (hidden,) = row_call(
        norm_kernel, "norm", 256, rows, (tokens, gain[None], shift[None]),
        (jax.ShapeDtypeStruct((rows, width), BF16),), 0,
    )
    hidden, tables, qkv_weight, fc2_shard = tie(hidden, tables, qkv_weight, w_fc2)
    shrink_weight = gather(fc2_shard, axis=1)
    qkv = qkv_project(hidden, qkv_weight, qkv_bias, tables, own_spots, share)

    def start_exchange(parts):
        if ctx_count == 2:
            low = ctx_index == 0
            away = jnp.where(low, parts[1], parts[0])
            stay = jnp.where(low, parts[0], parts[1])
            return stay, lax.ppermute(away, "ctx", [(0, 1), (1, 0)])
        return (lax.all_to_all(jnp.stack(parts), "ctx", split_axis=0, concat_axis=0, tiled=True),)

    def end_exchange(came):
        if ctx_count == 2:
            low = ctx_index == 0
            stay, came = came
            return [jnp.where(low, stay, came), jnp.where(low, came, stay)]
        return [came[0][c] for c in range(ctx_count)]

    def swap_whole(array):
        swapped = lax.all_to_all(array, "ctx", split_axis=0, concat_axis=0, tiled=True)
        return swapped.reshape(-1, array.shape[-1])

    qkv, hidden = tie(qkv, hidden)
    qkv_all = swap_whole(qkv)
    cut = lambda array, i: array[i * block : (i + 1) * block]

    gelu_slope, activated = row_call(
        expand_kernel, "expand", 256, rows, (hidden, expand_weight, b_fc1.astype(F32)[None]),
        (
            jax.ShapeDtypeStruct((rows, expand_weight.shape[1]), BF16),
            jax.ShapeDtypeStruct((rows, expand_weight.shape[1]), BF16),
        ),
        2 * rows * width * expand_weight.shape[1],
    )
    activated, dense_shard = tie(activated, w_dense)
    dense_weight = gather(dense_shard, axis=1)
    (mlp_out,) = row_call(
        shrink_kernel, "shrink", 256, rows, (activated, shrink_weight),
        (jax.ShapeDtypeStruct((rows, width), BF16),),
        2 * rows * width * expand_weight.shape[1],
    )
    mlp_out, cot_late = tie(mlp_out, cotangent)
    grad_att = grad_attended(cot_late, dense_weight, share)
    qkv_all, mlp_out, grad_att = tie(qkv_all, mlp_out, grad_att)
    grad_all = swap_whole(grad_att)
    turned_v = turn_prompts(qkv_all, share, 2)

    place = lax.axis_index("tp")
    flags = jnp.stack([((place == 0) | (place == 3)).astype(jnp.int32), place // 2])
    gain_row = gain[None]

    env = {}

    def forward(b):
        def run(qkv_in, turned_in):
            o, turned, lse = attend(qkv_in, turned_in, share, group, far, piece_items[b])
            return start_exchange([cut(o, c) for c in range(ctx_count)]), turned, lse

        def keep(out):
            came, env["turned", b], env["lse", b] = out
            env["attended", b] = end_exchange(came)
            for c, part in enumerate(env["attended", b]):
                before = env.get(("whole", c), jnp.zeros((rows, share), BF16))
                env["whole", c] = lax.dynamic_update_slice(before, part, (b * block, 0))

        return run, (qkv_all, turned_v), keep

    def out_part(b):
        def run(mlp, weight, *heads_out):
            pairs = [(part, 0, weight, c) for c, part in enumerate(heads_out)]
            return products(block, width, (mlp, b), pairs, "out_part")

        def keep(out):
            env["part", b] = out

        return run, (mlp_out, dense_weight, *env["attended", b]), keep

    def slope():
        def run(cot, gelu_slope, weight):
            return row_call(
                slope_kernel, "slope", 256, rows, (cot, gelu_slope, weight),
                (
                    jax.ShapeDtypeStruct(gelu_slope.shape, BF16),
                    jax.ShapeDtypeStruct((1, gelu_slope.shape[1]), F32),
                    jax.ShapeDtypeStruct((1, width), F32),
                ),
                2 * rows * width * gelu_slope.shape[1],
            )

        def keep(out):
            env["grad_expand"], env["expand_sum"], env["cot_sum"] = out

        return run, (cotangent, gelu_slope, shrink_weight), keep

    def turn_keys():
        def run(qkv_in):
            return turn_prompts(qkv_in, share, 1)

        def keep(out):
            env["turned_k"] = out

        return run, (qkv_all,), keep

    def backward(b):
        before = () if b == 0 else env["totals"]

        def run(qkv_in, turned_in, grad_in, turned, lse, *before):
            return attend_back(
                qkv_in, turned_in, share, grad_in, turned, lse, tables, group, far, piece_items[b],
                prompt_count, before,
            )

        def keep(out):
            env["dq", b], env["dk", b], env["dv", b] = out[:3]
            env["totals"] = out[3:]

        ins = (qkv_all, env["turned_k"], grad_all, env["turned", b], env["lse", b], *before)
        return run, ins, keep

    def finish():
        def run(dk, dv):
            return finish_prompts(dk, dv, tables)

        def keep(out):
            env["prompt_grads"] = [array.reshape(ctx_count // 2, rows, share) for array in out]

        return run, env["totals"], keep

    def give_back(b):
        def run(prompts, dq, dk, dv):
            parts = []
            for c in range(ctx_count):
                at = c - ctx_count // 2
                near = slice(b * block, (b + 1) * block)
                key = prompts[0][c, near] if at < 0 else cut(dk, at)
                value = prompts[1][c, near] if at < 0 else cut(dv, at)
                parts.append(jnp.concatenate([cut(dq, c), key, value], axis=1))
            return start_exchange(parts)

        def keep(out):
            env["sent_back", b] = out

        return run, (env["prompt_grads"], env["dq", b], env["dk", b], env["dv", b]), keep

    def grad_part(b):
        def run(grad_exp, exp_weight, came, weight):
            grad = jnp.concatenate(end_exchange(came), axis=1)
            pairs = [(grad_exp, b, exp_weight, None), (grad, 0, weight, None)]
            part = products(block, width, None, pairs, "grad_part")
            return part, grad, jnp.sum(grad.astype(F32), axis=0)

        def keep(out):
            env["part", blocks + b], grad, env["qkv_sum", b] = out
            before = env.get("all_qkv", jnp.zeros((rows, 3 * local), BF16))
            env["all_qkv"] = lax.dynamic_update_slice(before, grad, (b * block, 0))

        return run, (env["grad_expand"], expand_weight, env["sent_back", b], qkv_weight), keep

    def weight_grad(name, left, right, axis, part, parts):
        def run(left, right):
            cut_out = lambda a: a[:, part * a.shape[1] // parts : (part + 1) * a.shape[1] // parts]
            left, right = (cut_out(left), right) if axis else (left, cut_out(right))
            return transpose_dot(left, right).astype(BF16)

        def keep(out):
            env[name, part] = lax.psum_scatter(
                out, ("dp", "ctx"), scatter_dimension=axis, tiled=True
            ).astype(F32)

        return run, (left, right), keep

    def put_out(b):
        def run(four, before):
            return place_total(flags, four, b, rows, before)

        def keep(out):
            env["layer_out"] = out

        return run, (env["total", b], env.get("layer_out")), keep

    def put_grad(b, begin, count):
        def run(four, tokens_in, cot_in, before):
            return norm_back(flags, four, b, tokens_in, cot_in, gain_row, before, begin, count)

        def keep(out):
            env["grad_tokens"] = out

        total = env["total", blocks + b]
        return run, (total, tokens, cotangent, env.get("grad_tokens")), keep

    def sums(b):
        def run(near, tokens_in):
            return norm_sums(flags, near, b, tokens_in)

        def keep(out):
            env["gain", b], env["shift", b] = out

        return run, (line.near, tokens), keep

    def add_all(name, axes, pieces):
        def run(arrays):
            return lax.psum(jnp.concatenate(arrays), axes)

        def keep(out):
            env[name] = out

        return run, (pieces(),), keep

    def share_sums():
        def run(parts):
            own = jnp.concatenate([sum(part) for part in parts])
            both = own + lax.ppermute(own, "tp", [(1, 2), (2, 1)])
            return jnp.where(line.outer, lax.ppermute(both, "tp", [(1, 0), (2, 3)]), both)

        def keep(out):
            env["norm_sums"] = out

        parts = [[env[name, b] for b in range(blocks)] for name in ("gain", "shift")]
        return run, (parts,), keep

    def all_pieces():
        total = sum(env["qkv_sum", b] for b in range(blocks))
        return [env["norm_sums"].reshape(-1), total, env["expand_sum"][0], env["cot_sum"][0]]

    def all_attended():
        return jnp.concatenate([env["whole", c] for c in range(ctx_count)], axis=1)

    ticks = 4 * blocks + 2
    plan = [[] for _ in range(ticks + 8)]
    after = [[] for _ in plan]
    turn = 2 * blocks
    last = blocks - 1
    add = lambda slot, make, *args: plan[slot].append(functools.partial(make, *args))
    for b in range(blocks):
        if b:
            add(b - 1, forward, b)
            add(b, out_part, b)
            add(turn + 2 * (b - 1), give_back, b)
        add(last + b, backward, b)
        if b:
            add(turn - 1 + 2 * b, grad_part, b)
        add(turn + 1 + 2 * b, put_out, b)
        add(turn + 2 * b + 2, sums, b)
        if b < last - 1:
            add(turn + 2 * b + 4 + b % 2, put_grad, b, 0, 2)
    add(0, turn_keys)
    after[turn - 2].append(finish)
    add(turn - 1, give_back, 0)
    add(turn - 1, slope)
    after[turn - 1].append(functools.partial(grad_part, 0))
    add(turn, lambda: weight_grad("fc2", activated, cotangent, 1, 0, 1))
    add(turn + 2, lambda: weight_grad("fc1", hidden, env["grad_expand"], 0, 0, 2))
    add(turn + 4, lambda: weight_grad("fc1", hidden, env["grad_expand"], 0, 1, 2))
    add(2 * turn - 2, lambda: weight_grad("qkv", hidden, env["all_qkv"], 0, 0, 1))
    add(2 * turn - 1, lambda: weight_grad("dense", all_attended(), cotangent, 1, 0, 1))
    after[ticks - 2].append(share_sums)
    after[ticks - 2].append(functools.partial(put_grad, last - 1, 0, 2))
    add(ticks - 1, add_all, "total", ("dp", "ctx"), all_pieces)
    add(ticks - 1, put_grad, last, 0, 1)
    add(ticks, put_grad, last, 1, 1)

    def perform(make):
        run, ins, keep = make()
        keep(run(*ins))

    perform(functools.partial(forward, 0))
    perform(functools.partial(out_part, 0))

    line = Line(flags, tokens, (b_dense.astype(F32) + b_fc2.astype(F32))[None])
    arrived = (None, None)
    for t in range(ticks):
        b, second = divmod(t, 2)
        if second:
            operands = line.middle(*arrived)
        else:
            if t > 0:
                total = line.end(*arrived)
                if total is not None:
                    env["total", b - 2] = total
            operands = line.begin(env.get(("part", b)), b < blocks)
        if t == ticks - 1:
            env["total", 2 * blocks - 1] = (line.first, line.near, line.first, line.near)
        stages = [s for s in (plan[t], after[t]) if s]
        sent = None
        for n, stage in enumerate(stages):
            work = [make() for make in stage]
            operands, ins = tie(operands, [w[1] for w in work])
            if sent is None:
                sent = send(*operands)
            outs = [w[0](*i) for w, i in zip(work, ins)]
            if n == len(stages) - 1:
                arrived, outs = tie(sent, outs)
            for w, out in zip(work, outs):
                w[2](out)
        if not stages:
            arrived = send(*operands)
    env["total", 2 * blocks - 1] = line.end(*arrived)
    for late in plan[ticks:]:
        for make in late:
            perform(make)

    layer_out, grad_tokens = env["layer_out"], env["grad_tokens"]
    sizes = (width, width, 3 * local, w_fc1.shape[1])
    gain_sum, shift_sum, qkv_sum, expand_total, out_sum = jnp.split(
        env["total"], [sum(sizes[: i + 1]) for i in range(len(sizes))]
    )

    def unmixed(array):
        lead = array.shape[:-1]
        parts = array.reshape(*lead, ctx_count, 3, share)
        return tuple(parts[..., t, :].reshape(*lead, local) for t in range(3))

    grad_query, grad_key, grad_value = unmixed(env["qkv", 0])
    sum_query, sum_key, sum_value = unmixed(qkv_sum)
    return (
        layer_out, grad_tokens, gain_sum, shift_sum, grad_query, sum_query, grad_key, sum_key,
        grad_value, sum_value, env["dense", 0], out_sum,
        jnp.concatenate([env["fc1", 0], env["fc1", 1]], axis=1), expand_total, env["fc2", 0], out_sum,
    )


def solution(mesh):
    rows = P(("dp", "ctx"), None)
    down, across = P(("dp", "ctx"), "tp"), P("tp", ("dp", "ctx"))
    wide = P("tp")
    ins = (
        rows, rows, P("dp", None), P(), P(), down, wide, down, wide, down, wide, across, P(), down,
        wide, across, P(),
    )
    outs = (
        rows, rows, P(), P(), down, wide, down, wide, down, wide, across, P(), down, wide, across,
        P(),
    )
    return jax.shard_map(body, mesh=mesh, in_specs=ins, out_specs=outs, check_vma=False)
```

```python
import functools

import jax
import jax.numpy as jnp
from jax import lax
from jax.experimental import pallas as pl
from jax.experimental.pallas import tpu as pltpu
from jax.sharding import PartitionSpec as P

HDIM = 64
ROT = 32
PLEN = 2048
CLEN = 256
GPR = 2
BLOCK = 1024
VMEM = 56 * 2**20
F32 = jnp.float32
BF16 = jnp.bfloat16
NT = (((1,), (1,)), ((), ()))
NN = (((1,), (0,)), ((), ()))


def cost(bytes_accessed, flops=0):
    return pl.CostEstimate(flops=flops, bytes_accessed=bytes_accessed, transcendentals=0)


def dot(left, right, dims):
    return lax.dot_general(left, right, dims, preferred_element_type=F32)


def transpose_dot(left, right):
    return jnp.einsum("ra,rb->ab", left, right, preferred_element_type=F32)


def dot_back(left, right):
    return jnp.einsum("rb,ab->ra", left, right, preferred_element_type=F32)


def norm_apply(matrix, norm_gain, norm_shift):
    center = matrix - jnp.mean(matrix, axis=-1, keepdims=True)
    spread = jnp.mean(center * center, axis=-1, keepdims=True)
    return center * lax.rsqrt(spread + 1e-05) * norm_gain + norm_shift


def gelu_parts(v):
    scale = (2.0 / jnp.pi) ** 0.5
    square = v * v
    t = jnp.tanh(v * (scale + (scale * 0.044715) * square))
    half = 0.5 * v
    value = half + half * t
    slope = (0.5 + 0.5 * t) + (half - half * t * t) * (scale + (scale * 3 * 0.044715) * square)
    return value, slope


def rotary_tables():
    half = ROT // 2
    positions = jnp.arange(PLEN + CLEN, dtype=F32)
    frequency = 10000.0 ** (-2.0 * jnp.arange(half, dtype=F32) / ROT)
    angles = positions[:, None] * frequency[None, :]
    cosine, sine = jnp.cos(angles), jnp.sin(angles)
    ones = jnp.ones((PLEN + CLEN, HDIM - ROT), F32)
    zeros = jnp.zeros_like(ones)
    none = jnp.zeros_like(sine)
    head = (
        jnp.concatenate([cosine, cosine, ones], axis=1),
        jnp.concatenate([-sine, none, zeros], axis=1),
        jnp.concatenate([none, sine, zeros], axis=1),
    )
    return tuple(jnp.concatenate([table, table], axis=1) for table in head)


def rotated(values, cosine, first, second):
    half = ROT // 2
    return (
        values * cosine
        + pltpu.roll(values, 2 * HDIM - half, 1) * first
        + pltpu.roll(values, half, 1) * second
    )


def ahead(count, first, second):
    held = first(0)
    for i in range(count):
        following = first(i + 1) if i + 1 < count else None
        second(i, held)
        held = following


def norm_kernel(x_ref, gain_ref, shift_ref, out_ref):
    x = x_ref[...].astype(F32)
    out_ref[...] = norm_apply(x, gain_ref[...], shift_ref[...]).astype(BF16)


def qkv_kernel(
    share, where_ref, hidden_ref, weight_ref, bias_ref, cos_ref, first_ref, second_ref, out_ref
):
    hidden = hidden_ref[...]
    cosine, first, second = cos_ref[...], first_ref[...], second_ref[...]
    lane = lax.broadcasted_iota(jnp.int32, (1, 2 * HDIM), 1)
    member_width = out_ref.shape[2]

    def linear(i):
        at = slice(i * 512, (i + 1) * 512)
        return dot(hidden, weight_ref[:, at], NN) + bias_ref[:, at]

    def turn(i, lin):
        begin = i * 512
        for column in range(0, 512, 2 * HDIM):
            part = lin[:, column : column + 2 * HDIM]
            turns = [((begin + column + off) // share) % 3 < 2 for off in (0, HDIM)]
            if any(turns):
                turned = rotated(part, cosine, first, second)
                if not all(turns):
                    keep = lane < HDIM if turns[0] else lane >= HDIM
                    turned = jnp.where(keep, turned, part)
                part = turned
            part = part.astype(BF16)
            size = min(2 * HDIM, share)
            for off in range(0, 2 * HDIM, size):
                member, place = divmod(begin + column + off, member_width)
                out_ref[member, :, place : place + size] = part[:, off : off + size]

    ahead(weight_ref.shape[1] // 512, linear, turn)


def qkv_project(hidden, weight, bias, tables, spots, share):
    rows, width = hidden.shape
    outs = weight.shape[1]
    count = 256
    whole = lambda shape: pl.BlockSpec(shape, lambda i, *_: (0, 0))
    table = pl.BlockSpec((count, 2 * HDIM), lambda i, spots: (spots[i], 0))
    return pl.pallas_call(
        functools.partial(qkv_kernel, share),
        grid_spec=pltpu.PrefetchScalarGridSpec(
            num_scalar_prefetch=1,
            grid=(rows // count,),
            in_specs=[
                pl.BlockSpec((count, width), lambda i, *_: (i, 0)),
                whole((width, outs)),
                whole((1, outs)),
                table,
                table,
                table,
            ],
            out_specs=pl.BlockSpec(
                (outs // (3 * share), count, 3 * share), lambda i, *_: (0, i, 0)
            ),
        ),
        out_shape=jax.ShapeDtypeStruct((outs // (3 * share), rows, 3 * share), BF16),
        compiler_params=pltpu.CompilerParams(vmem_limit_bytes=VMEM),
        cost_estimate=pl.CostEstimate(
            flops=2 * rows * width * outs, bytes_accessed=2 * rows * (2 * width + outs),
            transcendentals=0,
        ),
        name="qkv_project",
    )(spots, hidden, weight, bias, *tables)


def expand_kernel(hidden_ref, weight_ref, bias_ref, slope_ref, out_ref):
    hidden = hidden_ref[...]

    def linear(i):
        at = slice(i * 512, (i + 1) * 512)
        return dot(hidden, weight_ref[:, at], NN) + bias_ref[:, at]

    def keep(i, lin):
        at = slice(i * 512, (i + 1) * 512)
        value, slope = gelu_parts(lin)
        out_ref[:, at] = value.astype(BF16)
        slope_ref[:, at] = slope.astype(BF16)

    ahead(weight_ref.shape[1] // 512, linear, keep)


def shrink_kernel(act_ref, weight_ref, out_ref):
    out_ref[...] = dot(act_ref[...], weight_ref[...], NN).astype(BF16)


def slope_kernel(cot_ref, slope_ref, weight_ref, grad_ref, sum_ref, cot_sum_ref):
    @pl.when(pl.program_id(0) == 0)
    def _():
        sum_ref[...] = jnp.zeros_like(sum_ref)
        cot_sum_ref[...] = jnp.zeros_like(cot_sum_ref)

    cot = cot_ref[...]
    cot_sum_ref[...] += jnp.sum(cot.astype(F32), axis=0, keepdims=True)

    def back(i):
        return dot(cot, weight_ref[i * 512 : (i + 1) * 512, :], NT)

    def keep(i, grad):
        at = slice(i * 512, (i + 1) * 512)
        grad = (slope_ref[:, at].astype(F32) * grad).astype(BF16)
        grad_ref[:, at] = grad
        sum_ref[:, at] += jnp.sum(grad.astype(F32), axis=0, keepdims=True)

    ahead(weight_ref.shape[0] // 512, back, keep)


def grad_attended_kernel(cot_ref, weight_ref, out_ref):
    cot = cot_ref[...]
    share = out_ref.shape[2]
    whole = dot(cot, weight_ref[...], NT).astype(BF16)
    for c in range(out_ref.shape[0]):
        out_ref[c] = whole[:, c * share : (c + 1) * share]


def grad_attended(cotangent, weight, share):
    rows, width = cotangent.shape
    local = weight.shape[0]
    count = 512
    return pl.pallas_call(
        grad_attended_kernel,
        grid=(rows // count,),
        in_specs=[
            pl.BlockSpec((count, width), lambda i: (i, 0)),
            pl.BlockSpec((local, width), lambda i: (0, 0)),
        ],
        out_specs=pl.BlockSpec((local // share, count, share), lambda i: (0, i, 0)),
        out_shape=jax.ShapeDtypeStruct((local // share, rows, share), BF16),
        compiler_params=pltpu.CompilerParams(vmem_limit_bytes=VMEM),
        cost_estimate=pl.CostEstimate(
            flops=2 * rows * width * local, bytes_accessed=2 * rows * (width + local),
            transcendentals=0,
        ),
        name="grad_attended",
    )(cotangent, weight)


def row_call(kernel, name, count, rows, in_arrays, outs, flops):
    def spec(shape):
        if shape[0] == rows:
            return pl.BlockSpec((count, shape[1]), lambda i: (i, 0))
        return pl.BlockSpec(shape, lambda i: (0, 0))

    return pl.pallas_call(
        kernel,
        grid=(rows // count,),
        in_specs=[spec(a.shape) for a in in_arrays],
        out_specs=[spec(o.shape) for o in outs],
        out_shape=outs,
        compiler_params=pltpu.CompilerParams(vmem_limit_bytes=VMEM),
        cost_estimate=pl.CostEstimate(
            flops=flops,
            bytes_accessed=sum(a.size * a.dtype.itemsize for a in (*in_arrays, *outs)),
            transcendentals=0,
        ),
        name=name,
    )(*in_arrays)


def products_kernel(kinds, has_base, *refs):
    out_ref = refs[-1]
    base_ref = refs[0] if has_base else None
    pairs = refs[has_base:-1]
    count = 256

    @pl.loop(0, out_ref.shape[0] // count)
    def _(i):
        rows = pl.ds(pl.multiple_of(i * count, count), count)
        total = base_ref[rows, :].astype(F32) if has_base else None
        for n, dims in enumerate(kinds):
            step = dot(pairs[2 * n][rows, :], pairs[2 * n + 1][...], dims)
            total = step if total is None else total + step
        out_ref[rows, :] = total.astype(BF16)


def products(count, outs, base, pairs, name):
    tile = 512
    arrays, specs, kinds = [], [], []
    flops = 0
    if base is not None:
        arrays.append(base[0])
        specs.append(pl.BlockSpec((count, tile), lambda n, at=base[1]: (at, n)))
    for left, at, right, right_at in pairs:
        depth = left.shape[1]
        arrays += [left, right]
        specs.append(pl.BlockSpec((count, depth), lambda n, at=at: (at, 0)))
        if right_at is None:
            specs.append(pl.BlockSpec((tile, depth), lambda n: (n, 0)))
            kinds.append(NT)
        else:
            specs.append(pl.BlockSpec((depth, tile), lambda n, at=right_at: (at, n)))
            kinds.append(NN)
        flops += 2 * count * depth * outs
    return pl.pallas_call(
        functools.partial(products_kernel, kinds, base is not None),
        grid=(outs // tile,),
        in_specs=specs,
        out_specs=pl.BlockSpec((count, tile), lambda n: (0, n)),
        out_shape=jax.ShapeDtypeStruct((count, outs), BF16),
        compiler_params=pltpu.CompilerParams(vmem_limit_bytes=VMEM),
        cost_estimate=pl.CostEstimate(
            flops=flops, bytes_accessed=flops // 512, transcendentals=0
        ),
        name=name,
    )(*arrays)


def heads_split(array, heads):
    if heads == 1:
        return [array]
    lane = lax.broadcasted_iota(jnp.int32, array.shape, 1)
    return [jnp.where(lane // HDIM == h, array, jnp.zeros((), array.dtype)) for h in range(heads)]


def near_mask():
    key = lax.broadcasted_iota(jnp.int32, (CLEN, CLEN), 0)
    query = lax.broadcasted_iota(jnp.int32, (CLEN, CLEN), 1)
    return key <= query


def over_far(base, count, big, step):
    per = big // CLEN
    full = count // per

    @pl.loop(0, full)
    def _(i):
        step(pl.multiple_of(base + i * big, CLEN), big)

    @pl.loop(full * per, count)
    def _(i):
        step(pl.multiple_of(base + i * CLEN, CLEN), CLEN)


def attend_kernel(
    big, group_ref, far_ref, item_ref, q_ref, ko_ref, vo_ref, kp_ref, vt_s, o_ref, ot_ref,
    lse_ref, m_s, l_s, acc_s,
):
    heads = q_ref.shape[1] // HDIM
    item = item_ref[pl.program_id(1)]
    base = group_ref[item] * PLEN

    queries = heads_split(q_ref[...] * BF16(HDIM**-0.5), heads)
    mask = near_mask()
    keys = ko_ref[...]
    values = vo_ref[...].T
    spans = [slice(h * HDIM, (h + 1) * HDIM) for h in range(heads)]
    scores = [dot(keys, queries[h], NT) for h in range(heads)]
    for h in range(heads):
        s = jnp.where(mask, scores[h], -1e30)
        m = jnp.max(s, axis=0, keepdims=True)
        p = jnp.exp(s - m)
        m_s[h] = m
        l_s[h] = jnp.sum(p, axis=0, keepdims=True)
        acc_s[h] = dot(values[spans[h]], p.astype(BF16), NN)

    def step(first, size):
        k = kp_ref[pl.ds(first, size), :]
        scores = [dot(k, queries[h], NT) for h in range(heads)]
        for h in range(heads):
            old = m_s[h]
            m = jnp.maximum(old, jnp.max(scores[h], axis=0, keepdims=True))
            p = jnp.exp(scores[h] - m)
            a = jnp.exp(old - m)
            m_s[h] = m
            l_s[h] = l_s[h] * a + jnp.sum(p, axis=0, keepdims=True)
            acc_s[h] = acc_s[h] * a + dot(vt_s[spans[h], pl.ds(first, size)], p.astype(BF16), NN)

    over_far(base, far_ref[item], big, step)
    for h in range(heads):
        ot_ref[spans[h], :] = acc_s[h] * (1.0 / l_s[h])
        lse_ref[0, h : h + 1, :] = m_s[h] + jnp.log(l_s[h])
    o_ref[...] = ot_ref[...].T.astype(BF16)


def turn_kernel(in_ref, out_ref):
    for begin in range(0, in_ref.shape[0], CLEN):
        out_ref[:, begin : begin + CLEN] = in_ref[begin : begin + CLEN, :].T


def turn_prompts(qkv, width, which):
    wide = min(4 * HDIM, width)
    arrays, ats = split_columns(qkv, width)
    count = PLEN // 2
    return pl.pallas_call(
        turn_kernel,
        grid=(width // wide, GPR * PLEN // count),
        in_specs=[pl.BlockSpec((count, wide), lambda h, i: (i, ats[which] + h))],
        out_specs=pl.BlockSpec((wide, count), lambda h, i: (h, i)),
        out_shape=jax.ShapeDtypeStruct((width, GPR * PLEN), BF16),
        compiler_params=pltpu.CompilerParams(vmem_limit_bytes=VMEM),
        cost_estimate=cost(width * GPR * PLEN * 8),
        name="turn_prompts",
    )(arrays[which])


def turned_back(values, tables):
    width = values.shape[1]
    cosine, first, second = (ref[...] for ref in tables)
    wide = 2 * HDIM
    if width < wide:
        values = jnp.concatenate([values, values], axis=1)
    parts = [
        rotated(values[:, c : c + wide], cosine, -first, -second)
        for c in range(0, values.shape[1], wide)
    ]
    out = parts[0] if len(parts) == 1 else jnp.concatenate(parts, axis=1)
    return out[:, :width].astype(BF16)


def attend_back_kernel(big, first_piece, prompt_items, prompt_count, *refs):
    group_ref, far_ref, item_ref = refs[:3]
    q_ref, ko_ref, vo_ref, do_ref, ot_ref, lse_ref, kp_ref, vp_ref, kt_s = refs[3:12]
    tables = refs[12:15]
    before = () if first_piece else refs[15:17]
    dq_ref, dk_ref, dv_ref, dk_s, dv_s, dq_s, near_k, near_v = refs[15 + len(before) :]
    width = q_ref.shape[1]
    heads = width // HDIM
    turn = pl.program_id(1)
    item = item_ref[turn]
    base = group_ref[item] * PLEN

    @pl.when(turn == 0)
    def _():
        if first_piece:
            dk_s[...] = jnp.zeros_like(dk_s)
            dv_s[...] = jnp.zeros_like(dv_s)
        else:
            dk_s[...] = before[0][...]
            dv_s[...] = before[1][...]

    do = do_ref[...]
    queries = heads_split(q_ref[...] * BF16(HDIM**-0.5), heads)
    grads = heads_split(do, heads)
    query_cat = jnp.concatenate(queries, axis=0)
    grad_cat = jnp.concatenate(grads, axis=0)
    spans = [slice(h * HDIM, (h + 1) * HDIM) for h in range(heads)]
    product = ot_ref[...] * do.astype(F32).T
    center = [jnp.sum(product[span], axis=0, keepdims=True) for span in spans]
    lse = [lse_ref[0, h : h + 1, :] for h in range(heads)]
    mask = near_mask()

    def piece(k, v, kt, near):
        chance, grad_scores = [], []
        scores = [dot(k, queries[h], NT) for h in range(heads)]
        grad_chance = [dot(v, grads[h], NT) for h in range(heads)]
        for h in range(heads):
            p = jnp.exp(scores[h] - lse[h])
            if near:
                p = jnp.where(mask, p, 0.0)
            grad_scores.append((p * (grad_chance[h] - center[h])).astype(BF16))
            chance.append(p.astype(BF16))
        for h in range(heads):
            step = dot(kt(spans[h]), grad_scores[h], NN)
            if near:
                dq_s[spans[h], :] = step
            else:
                dq_s[spans[h], :] += step
        return (
            dot(jnp.concatenate(grad_scores, axis=1), query_cat, NN),
            dot(jnp.concatenate(chance, axis=1), grad_cat, NN),
        )

    own = ko_ref[...]
    own_t = own.T
    near_k[...], near_v[...] = piece(own, vo_ref[...], lambda span: own_t[span], True)

    @pl.when(turn < prompt_count)
    def _():
        rows = pl.ds(pl.multiple_of(item * CLEN, CLEN), CLEN)
        dk_s[rows, :] += near_k[...]
        dv_s[rows, :] += near_v[...]

    @pl.when(turn >= prompt_count)
    def _():
        dk_ref[...] = turned_back(near_k[...], tables)
        dv_ref[...] = near_v[...].astype(BF16)

    def step(first, size):
        rows = pl.ds(first, size)
        k_step, v_step = piece(
            kp_ref[rows, :], vp_ref[rows, :], lambda span: kt_s[span, rows], False
        )
        dk_s[rows, :] += k_step
        dv_s[rows, :] += v_step

    over_far(base, far_ref[item], big, step)
    dq_ref[...] = turned_back((dq_s[...] * (HDIM**-0.5)).T, tables)


def finish_kernel(dk_ref, dv_ref, cos_ref, first_ref, second_ref, ok_ref, ov_ref):
    ok_ref[...] = turned_back(dk_ref[...], (cos_ref, first_ref, second_ref))
    ov_ref[...] = dv_ref[...].astype(BF16)


def finish_prompts(dk, dv, tables):
    rows, width = dk.shape
    wide = min(4 * HDIM, width)
    count = PLEN // 2
    block = pl.BlockSpec((count, wide), lambda h, i: (i, h))
    table = pl.BlockSpec((count, 2 * HDIM), lambda h, i: (i % (PLEN // count), 0))
    return pl.pallas_call(
        finish_kernel,
        grid=(width // wide, rows // count),
        in_specs=[block, block, table, table, table],
        out_specs=[block, block],
        out_shape=[jax.ShapeDtypeStruct((rows, width), BF16)] * 2,
        compiler_params=pltpu.CompilerParams(vmem_limit_bytes=VMEM),
        cost_estimate=cost(rows * width * 30),
        name="finish_prompts",
    )(dk, dv, *tables)


def split_columns(qkv, width):
    wide = min(4 * HDIM, width)
    if wide % 128 == 0:
        return (qkv, qkv, qkv), tuple(t * width // wide for t in range(3))
    return tuple(qkv[:, t * width : (t + 1) * width] for t in range(3)), (0, 0, 0)


def attention_specs(width):
    wide = min(4 * HDIM, width)
    heads = wide // HDIM
    return (
        wide,
        heads,
        lambda at: pl.BlockSpec((CLEN, wide), lambda h, i, g, f, items: (items[i], at + h)),
        pl.BlockSpec((CLEN, wide), lambda h, i, *_: (i, h)),
        pl.BlockSpec((wide, CLEN), lambda h, i, *_: (h, i)),
        lambda at: pl.BlockSpec((GPR * PLEN, wide), lambda h, i, *_: (0, at + h)),
        pl.BlockSpec((1, heads, CLEN), lambda h, i, *_: (h, 0, i)),
    )


def attend(qkv, turned_v, width, group, far, items):
    rows = items.shape[0] * CLEN
    wide, heads, picked, block, turned, prompts, stats = attention_specs(width)
    (q, k, v), (qa, ka, va) = split_columns(qkv, width)
    pairs = rows * (PLEN + CLEN) * width // HDIM
    return pl.pallas_call(
        functools.partial(attend_kernel, 1024),
        grid_spec=pltpu.PrefetchScalarGridSpec(
            num_scalar_prefetch=3,
            grid=(width // wide, rows // CLEN),
            in_specs=[
                picked(qa), picked(ka), picked(va), prompts(ka),
                pl.BlockSpec((wide, GPR * PLEN), lambda h, i, *_: (h, 0)),
            ],
            out_specs=[block, turned, stats],
            scratch_shapes=[
                pltpu.VMEM((heads, 1, CLEN), F32),
                pltpu.VMEM((heads, 1, CLEN), F32),
                pltpu.VMEM((heads, HDIM, CLEN), F32),
            ],
        ),
        out_shape=[
            jax.ShapeDtypeStruct((rows, width), BF16),
            jax.ShapeDtypeStruct((width, rows), F32),
            jax.ShapeDtypeStruct((width // wide, heads, rows), F32),
        ],
        compiler_params=pltpu.CompilerParams(vmem_limit_bytes=VMEM),
        cost_estimate=pl.CostEstimate(
            flops=4 * pairs * 256, bytes_accessed=rows * width * 12, transcendentals=pairs
        ),
        name="attend",
    )(group, far, items, q, k, v, k, turned_v)


def attend_back(
    qkv, turned_k, width, grad, turned_out, lse, tables, group, far, items, prompt_count, before
):
    rows = items.shape[0] * CLEN
    wide, heads, picked, block, turned, prompts, stats = attention_specs(width)
    (q, k, v), (qa, ka, va) = split_columns(qkv, width)
    table = pl.BlockSpec((CLEN, 2 * HDIM), lambda h, i, g, f, items: (f[items[i]], 0))
    total = pl.BlockSpec((GPR * PLEN, wide), lambda h, i, *_: (0, h))
    late = pl.BlockSpec((CLEN, wide), lambda h, i, *_: (jnp.maximum(i - prompt_count, 0), h))
    pairs = rows * (PLEN + CLEN) * width // HDIM
    first = not before
    late_rows = rows - prompt_count * CLEN
    return pl.pallas_call(
        functools.partial(attend_back_kernel, 1024, first, GPR * PLEN // CLEN, prompt_count),
        grid_spec=pltpu.PrefetchScalarGridSpec(
            num_scalar_prefetch=3,
            grid=(width // wide, rows // CLEN),
            in_specs=[
                picked(qa), picked(ka), picked(va), picked(0), turned, stats, prompts(ka),
                prompts(va), pl.BlockSpec((wide, GPR * PLEN), lambda h, i, *_: (h, 0)), table, table,
                table,
            ]
            + [total] * len(before),
            out_specs=[block, late, late, total, total],
            scratch_shapes=[
                pltpu.VMEM((wide, CLEN), F32),
                pltpu.VMEM((CLEN, wide), F32),
                pltpu.VMEM((CLEN, wide), F32),
            ],
        ),
        out_shape=[jax.ShapeDtypeStruct((rows, width), BF16)]
        + [jax.ShapeDtypeStruct((late_rows, width), BF16)] * 2
        + [jax.ShapeDtypeStruct((GPR * PLEN, width), F32)] * 2,
        input_output_aliases={} if first else {15: 3, 16: 4},
        compiler_params=pltpu.CompilerParams(vmem_limit_bytes=VMEM),
        cost_estimate=pl.CostEstimate(
            flops=8 * pairs * 256, bytes_accessed=rows * width * 24, transcendentals=pairs
        ),
        name="attend_back",
    )(group, far, items, q, k, v, grad, turned_out, lse, k, v, turned_k, *tables, *before)


def tie(*trees):
    return lax.optimization_barrier(trees)


COUNT = 256


def begin_kernel(names, flag_ref, *refs):
    refs = dict(zip(names, refs))
    outer = flag_ref[0] == 1
    out_ref = refs["out"]

    @pl.when(outer)
    def _():
        out_ref[...] = refs["next"][...] if "next" in refs else jnp.zeros_like(out_ref)

    @pl.when(flag_ref[0] == 0)
    def _():
        if "part" not in refs:
            out_ref[...] = jnp.zeros_like(out_ref)
            return
        total = (
            refs["part"][...].astype(F32)
            + refs["swapped"][...].astype(F32)
            + refs["crossed"][...].astype(F32)
        )
        if "tokens" in refs:
            total = total + refs["tokens"][...].astype(F32) + refs["bias"][...]
        out_ref[...] = total.astype(BF16)


def middle_kernel(names, flag_ref, *refs):
    refs = dict(zip(names, refs))
    outer = flag_ref[0] == 1
    swap_ref = refs["swap"]

    @pl.when(outer)
    def _():
        swap_ref[...] = refs["near"][...] if "near" in refs else jnp.zeros_like(swap_ref)

    @pl.when(flag_ref[0] == 0)
    def _():
        swap_ref[...] = refs["crossed"][...] if "crossed" in refs else jnp.zeros_like(swap_ref)

    if "far" in refs:
        refs["cross"][...] = (
            refs["far"][...].astype(F32) + refs["swapped"][...].astype(F32)
        ).astype(BF16)


def line_call(kernel, flags, rows, width, ins, outs, name):
    steps = rows // COUNT

    def spec(shape, first, who):
        if shape[0] == 1:
            return pl.BlockSpec(shape, lambda i, flag: (0, 0))

        def index(i, flag):
            needed = {"all": 1, "outer": flag[0], "inner": 1 - flag[0]}[who]
            return (first(flag[1], steps) + i * needed, 0)

        return pl.BlockSpec((COUNT, width), index)

    return pl.pallas_call(
        functools.partial(kernel, [i[0] for i in ins] + outs),
        grid_spec=pltpu.PrefetchScalarGridSpec(
            num_scalar_prefetch=1,
            grid=(steps,),
            in_specs=[spec(array.shape, first, who) for _, array, first, who in ins],
            out_specs=[pl.BlockSpec((COUNT, width), lambda i, flag: (i, 0)) for _ in outs],
        ),
        out_shape=[jax.ShapeDtypeStruct((rows, width), BF16) for _ in outs],
        compiler_params=pltpu.CompilerParams(vmem_limit_bytes=VMEM),
        cost_estimate=cost(rows * width * 16),
        name=name,
    )(flags, *[i[1] for i in ins])


def total_specs(half, width, begin):
    outer = lambda flag: flag[0]
    inner = lambda flag: 1 - flag[0]

    def spec(part, who):
        return pl.BlockSpec(
            (COUNT, width), lambda p, i, flag: (i * who(flag) * (p + begin == part), 0)
        )

    return [spec(0, outer), spec(0, inner), spec(1, outer), spec(1, inner)]


def total_of(flag_ref, refs, keep, begin):
    part = pl.program_id(0) + begin
    for at, ref in enumerate(refs):
        right = (part == at // 2) & (flag_ref[0] == 1 - at % 2)

        @pl.when(right)
        def _(ref=ref):
            keep(ref[...])


def rows_of(block, half, begin):
    steps = half // COUNT

    def index(p, i, flag):
        return ((2 * block + (flag[1] + p + begin) % 2) * steps + i, 0)

    return index


def place_kernel(flag_ref, a, b, c, d, *rest):
    out_ref = rest[-1]

    def keep(value):
        out_ref[...] = value

    total_of(flag_ref, (a, b, c, d), keep, 0)


def place_total(flags, four, block, rows, before):
    half, width = four[0].shape
    return pl.pallas_call(
        place_kernel,
        grid_spec=pltpu.PrefetchScalarGridSpec(
            num_scalar_prefetch=1,
            grid=(2, half // COUNT),
            in_specs=total_specs(half, width, 0)
            + [pl.BlockSpec(memory_space=pl.ANY)] * (before is not None),
            out_specs=pl.BlockSpec((COUNT, width), rows_of(block, half, 0)),
        ),
        out_shape=jax.ShapeDtypeStruct((rows, width), BF16),
        input_output_aliases={} if before is None else {5: 0},
        compiler_params=pltpu.CompilerParams(vmem_limit_bytes=VMEM),
        cost_estimate=cost(half * width * 24),
        name="place_total",
    )(flags, *four, *(() if before is None else (before,)))


def normed_rows(tokens):
    x = tokens.astype(F32)
    center = x - jnp.mean(x, axis=-1, keepdims=True)
    inverse = lax.rsqrt(jnp.mean(center * center, axis=-1, keepdims=True) + 1e-05)
    return center * inverse, inverse


def norm_back_kernel(begin, flag_ref, a, b, c, d, x_ref, cot_ref, gain_ref, *rest):
    out_ref, held = rest[-2:]

    def keep(value):
        held[...] = value

    total_of(flag_ref, (a, b, c, d), keep, begin)
    normed, inverse = normed_rows(x_ref[...])
    scaled = held[...].astype(F32) * gain_ref[...]
    grad = scaled - jnp.mean(scaled, axis=-1, keepdims=True)
    grad = inverse * (grad - normed * jnp.mean(scaled * normed, axis=-1, keepdims=True))
    out_ref[...] = cot_ref[...].astype(F32) + grad


def norm_back(flags, four, block, tokens, cotangent, gain, before, begin, count):
    half, width = four[0].shape
    row = pl.BlockSpec((1, width), lambda p, i, flag: (0, 0))
    whole = pl.BlockSpec((COUNT, width), rows_of(block, half, begin))
    return pl.pallas_call(
        functools.partial(norm_back_kernel, begin),
        grid_spec=pltpu.PrefetchScalarGridSpec(
            num_scalar_prefetch=1,
            grid=(count, half // COUNT),
            in_specs=total_specs(half, width, begin)
            + [whole, whole, row]
            + [pl.BlockSpec(memory_space=pl.ANY)] * (before is not None),
            out_specs=whole,
            scratch_shapes=[pltpu.VMEM((COUNT, width), BF16)],
        ),
        out_shape=jax.ShapeDtypeStruct(tokens.shape, F32),
        input_output_aliases={} if before is None else {8: 0},
        compiler_params=pltpu.CompilerParams(vmem_limit_bytes=VMEM),
        cost_estimate=cost(half * width * 24 * count),
        name="norm_back",
    )(flags, *four, tokens, cotangent, gain, *(() if before is None else (before,)))


def norm_sums_kernel(flag_ref, total_ref, x_ref, gain_sum, shift_sum):
    @pl.when(pl.program_id(0) == 0)
    def _():
        gain_sum[...] = jnp.zeros_like(gain_sum)
        shift_sum[...] = jnp.zeros_like(shift_sum)

    @pl.when(flag_ref[0] == 0)
    def _():
        total = total_ref[...].astype(F32)
        gain_sum[...] += jnp.sum(total * normed_rows(x_ref[...])[0], axis=0, keepdims=True)
        shift_sum[...] += jnp.sum(total, axis=0, keepdims=True)


def norm_sums(flags, near, block, tokens):
    half, width = near.shape
    steps = half // COUNT
    row = pl.BlockSpec((1, width), lambda i, flag: (0, 0))
    return pl.pallas_call(
        norm_sums_kernel,
        grid_spec=pltpu.PrefetchScalarGridSpec(
            num_scalar_prefetch=1,
            grid=(steps,),
            in_specs=[
                pl.BlockSpec((COUNT, width), lambda i, flag: (i * (1 - flag[0]), 0)),
                pl.BlockSpec(
                    (COUNT, width),
                    lambda i, flag: ((2 * block + flag[1]) * steps + i * (1 - flag[0]), 0),
                ),
            ],
            out_specs=[row, row],
        ),
        out_shape=[jax.ShapeDtypeStruct((1, width), F32)] * 2,
        compiler_params=pltpu.CompilerParams(vmem_limit_bytes=VMEM),
        cost_estimate=cost(half * width * 10),
        name="norm_sums",
    )(flags, near, tokens)


class Line:
    def __init__(self, flags, tokens, bias):
        self.flags, self.tokens, self.bias = flags, tokens, bias
        self.outer = flags[0] == 1
        self.part = self.near = None
        self.block = -1

    def begin(self, part, with_input):
        zero = lambda side, steps: 0
        near = lambda side, steps: side * steps
        ins = []
        if self.part is not None:
            ins += [
                ("part", self.part, near, "inner"),
                ("swapped", self.swapped, zero, "inner"),
                ("crossed", self.crossed, zero, "inner"),
            ]
            if self.with_input:
                block = self.block
                ins += [
                    ("tokens", self.tokens, lambda side, steps: (2 * block + side) * steps, "inner"),
                    ("bias", self.bias, zero, "all"),
                ]
        if part is not None:
            ins.append(("next", part, lambda side, steps: (1 - side) * steps, "outer"))
        shape = (self.part if part is None else part).shape
        (out,) = line_call(
            begin_kernel, self.flags, shape[0] // 2, shape[1], ins, ["out"], "line_begin"
        )
        had = self.part is not None
        self.part, self.with_input = part, with_input
        self.block += 1
        self.near = out if had else None
        return out, self.near

    def middle(self, swapped, crossed):
        self.first, self.other = swapped, crossed
        ins = []
        if self.part is not None:
            ins += [
                ("near", self.part, lambda side, steps: side * steps, "outer"),
                ("far", self.part, lambda side, steps: (1 - side) * steps, "inner"),
                ("swapped", swapped, lambda side, steps: 0, "inner"),
            ]
        if crossed is not None:
            ins.append(("crossed", crossed, lambda side, steps: 0, "inner"))
        if self.part is None:
            return crossed, None
        return tuple(
            line_call(
                middle_kernel, self.flags, *swapped.shape, ins, ["swap", "cross"], "line_middle"
            )
        )

    def end(self, swapped, crossed):
        self.swapped, self.crossed = swapped, crossed
        if self.near is None:
            return None
        return self.first, self.near, swapped, self.other


def send(swap, cross):
    outer, middle = [(0, 1), (3, 2), (1, 0), (2, 3)], [(1, 2), (2, 1)]
    return (
        None if swap is None else lax.ppermute(swap, "tp", outer),
        None if cross is None else lax.ppermute(cross, "tp", middle),
    )


def unwritten(shape):
    return pl.pallas_call(
        lambda out_ref: None,
        out_specs=pl.BlockSpec(memory_space=pl.ANY),
        out_shape=jax.ShapeDtypeStruct(shape, BF16),
        name="unwritten",
    )()


def body(
    tokens, cotangent, membership, ln_gain, ln_bias, w_query, b_query, w_key, b_key, w_value,
    b_value, w_dense, b_dense, w_fc1, b_fc1, w_fc2, b_fc2,
):
    rows, width = tokens.shape
    ctx_count = lax.axis_size("ctx")
    ctx_index = lax.axis_index("ctx")
    local = w_query.shape[1]
    share = local // ctx_count
    mine = 3 * share
    block = min(BLOCK, rows // 2)
    blocks = rows // block

    def mixed(query, key, value):
        lead = query.shape[:-1]
        stacked = jnp.stack(
            [a.reshape(*lead, ctx_count, share) for a in (query, key, value)], axis=-2
        )
        return stacked.reshape(*lead, 3 * local)

    gather = functools.partial(lax.all_gather, axis_name=("dp", "ctx"), tiled=True)
    qkv_weight = gather(mixed(w_query, w_key, w_value), axis=0)
    expand_weight = gather(w_fc1, axis=0)
    qkv_bias = mixed(b_query, b_key, b_value).astype(F32)[None]

    per_prompt = PLEN // CLEN
    prompt_items = GPR * per_prompt
    own_items = rows // CLEN
    items = jnp.arange(own_items * ctx_count, dtype=jnp.int32)
    far = jnp.where(items < prompt_items, items % per_prompt, per_prompt)
    group = jnp.concatenate([items[:prompt_items] // per_prompt, membership[0]])
    own_spots = lax.dynamic_slice_in_dim(far, ctx_index * own_items, own_items)
    tables = rotary_tables()
    per_block = block // CLEN
    item_table = items.reshape(ctx_count, blocks, per_block)
    piece_items = [item_table[:, b].reshape(-1) for b in range(blocks)]
    prompt_count = ctx_count // 2 * per_block

    gain = ln_gain.astype(F32)
    shift = ln_bias.astype(F32)
    (hidden,) = row_call(
        norm_kernel, "norm", 256, rows, (tokens, gain[None], shift[None]),
        (jax.ShapeDtypeStruct((rows, width), BF16),), 0,
    )
    hidden, tables, qkv_weight, fc2_shard = tie(hidden, tables, qkv_weight, w_fc2)
    shrink_weight = gather(fc2_shard, axis=1)
    qkv = qkv_project(hidden, qkv_weight, qkv_bias, tables, own_spots, share)

    def start_exchange(parts):
        if ctx_count == 2:
            low = ctx_index == 0
            away = jnp.where(low, parts[1], parts[0])
            stay = jnp.where(low, parts[0], parts[1])
            return stay, lax.ppermute(away, "ctx", [(0, 1), (1, 0)])
        return (lax.all_to_all(jnp.stack(parts), "ctx", split_axis=0, concat_axis=0, tiled=True),)

    def end_exchange(came):
        if ctx_count == 2:
            low = ctx_index == 0
            stay, came = came
            return [jnp.where(low, stay, came), jnp.where(low, came, stay)]
        return [came[0][c] for c in range(ctx_count)]

    def swap_whole(array):
        swapped = lax.all_to_all(array, "ctx", split_axis=0, concat_axis=0, tiled=True)
        return swapped.reshape(-1, array.shape[-1])

    qkv, hidden = tie(qkv, hidden)
    qkv_all = swap_whole(qkv)
    cut = lambda array, i: array[i * block : (i + 1) * block]

    gelu_slope, activated = row_call(
        expand_kernel, "expand", 256, rows, (hidden, expand_weight, b_fc1.astype(F32)[None]),
        (
            jax.ShapeDtypeStruct((rows, expand_weight.shape[1]), BF16),
            jax.ShapeDtypeStruct((rows, expand_weight.shape[1]), BF16),
        ),
        2 * rows * width * expand_weight.shape[1],
    )
    activated, dense_shard = tie(activated, w_dense)
    dense_weight = gather(dense_shard, axis=1)
    (mlp_out,) = row_call(
        shrink_kernel, "shrink", 256, rows, (activated, shrink_weight),
        (jax.ShapeDtypeStruct((rows, width), BF16),),
        2 * rows * width * expand_weight.shape[1],
    )
    mlp_out, cot_late = tie(mlp_out, cotangent)
    grad_att = grad_attended(cot_late, dense_weight, share)
    qkv_all, mlp_out, grad_att = tie(qkv_all, mlp_out, grad_att)
    grad_all = swap_whole(grad_att)
    turned_v = turn_prompts(qkv_all, share, 2)

    place = lax.axis_index("tp")
    flags = jnp.stack([((place == 0) | (place == 3)).astype(jnp.int32), place // 2])
    gain_row = gain[None]

    env = {}

    def forward(b):
        def run(qkv_in, turned_in):
            o, turned, lse = attend(qkv_in, turned_in, share, group, far, piece_items[b])
            return start_exchange([cut(o, c) for c in range(ctx_count)]), turned, lse

        def keep(out):
            came, env["turned", b], env["lse", b] = out
            env["attended", b] = end_exchange(came)
            whole = env["whole"] if b else unwritten((rows, local))
            for c, part in enumerate(env["attended", b]):
                whole = lax.dynamic_update_slice(whole, part, (b * block, c * share))
            env["whole"] = whole

        return run, (qkv_all, turned_v), keep

    def out_part(b):
        def run(mlp, weight, *heads_out):
            pairs = [(part, 0, weight, c) for c, part in enumerate(heads_out)]
            return products(block, width, (mlp, b), pairs, "out_part")

        def keep(out):
            env["part", b] = out

        return run, (mlp_out, dense_weight, *env["attended", b]), keep

    def slope():
        def run(cot, gelu_slope, weight):
            return row_call(
                slope_kernel, "slope", 256, rows, (cot, gelu_slope, weight),
                (
                    jax.ShapeDtypeStruct(gelu_slope.shape, BF16),
                    jax.ShapeDtypeStruct((1, gelu_slope.shape[1]), F32),
                    jax.ShapeDtypeStruct((1, width), F32),
                ),
                2 * rows * width * gelu_slope.shape[1],
            )

        def keep(out):
            env["grad_expand"], env["expand_sum"], env["cot_sum"] = out

        return run, (cotangent, gelu_slope, shrink_weight), keep

    def turn_keys():
        def run(qkv_in):
            return turn_prompts(qkv_in, share, 1)

        def keep(out):
            env["turned_k"] = out

        return run, (qkv_all,), keep

    def backward(b):
        before = () if b == 0 else env["totals"]

        def run(qkv_in, turned_in, grad_in, turned, lse, *before):
            return attend_back(
                qkv_in, turned_in, share, grad_in, turned, lse, tables, group, far, piece_items[b],
                prompt_count, before,
            )

        def keep(out):
            env["dq", b], env["dk", b], env["dv", b] = out[:3]
            env["totals"] = out[3:]

        ins = (qkv_all, env["turned_k"], grad_all, env["turned", b], env["lse", b], *before)
        return run, ins, keep

    def finish():
        def run(dk, dv):
            return finish_prompts(dk, dv, tables)

        def keep(out):
            env["prompt_grads"] = [array.reshape(ctx_count // 2, rows, share) for array in out]

        return run, env["totals"], keep

    def give_back(b):
        def run(prompts, dq, dk, dv):
            parts = []
            for c in range(ctx_count):
                at = c - ctx_count // 2
                near = slice(b * block, (b + 1) * block)
                key = prompts[0][c, near] if at < 0 else cut(dk, at)
                value = prompts[1][c, near] if at < 0 else cut(dv, at)
                parts.append(jnp.concatenate([cut(dq, c), key, value], axis=1))
            return start_exchange(parts)

        def keep(out):
            env["sent_back", b] = out

        return run, (env["prompt_grads"], env["dq", b], env["dk", b], env["dv", b]), keep

    def grad_part(b):
        def run(grad_exp, exp_weight, came, weight):
            grad = jnp.concatenate(end_exchange(came), axis=1)
            pairs = [(grad_exp, b, exp_weight, None), (grad, 0, weight, None)]
            part = products(block, width, None, pairs, "grad_part")
            return part, grad, jnp.sum(grad.astype(F32), axis=0)

        def keep(out):
            env["part", blocks + b], grad, env["qkv_sum", b] = out
            before = env["all_qkv"] if b else unwritten((rows, 3 * local))
            env["all_qkv"] = lax.dynamic_update_slice(before, grad, (b * block, 0))

        return run, (env["grad_expand"], expand_weight, env["sent_back", b], qkv_weight), keep

    def weight_grad(name, left, right, axis, part, parts):
        def run(left, right):
            cut_out = lambda a: a[:, part * a.shape[1] // parts : (part + 1) * a.shape[1] // parts]
            left, right = (cut_out(left), right) if axis else (left, cut_out(right))
            return transpose_dot(left, right).astype(BF16)

        def keep(out):
            env[name, part] = lax.psum_scatter(
                out, ("dp", "ctx"), scatter_dimension=axis, tiled=True
            ).astype(F32)

        return run, (left, right), keep

    def put_out(b):
        def run(four, before):
            return place_total(flags, four, b, rows, before)

        def keep(out):
            env["layer_out"] = out

        return run, (env["total", b], env.get("layer_out")), keep

    def put_grad(b, begin, count):
        def run(four, tokens_in, cot_in, before):
            return norm_back(flags, four, b, tokens_in, cot_in, gain_row, before, begin, count)

        def keep(out):
            env["grad_tokens"] = out

        total = env["total", blocks + b]
        return run, (total, tokens, cotangent, env.get("grad_tokens")), keep

    def sums(b):
        def run(near, tokens_in):
            return norm_sums(flags, near, b, tokens_in)

        def keep(out):
            env["gain", b], env["shift", b] = out

        return run, (line.near, tokens), keep

    def add_all(name, axes, pieces):
        def run(arrays):
            return lax.psum(jnp.concatenate(arrays), axes)

        def keep(out):
            env[name] = out

        return run, (pieces(),), keep

    def all_pieces():
        total = sum(env["qkv_sum", b] for b in range(blocks))
        own = [sum(env[name, b][0] for b in range(blocks)) for name in ("gain", "shift")]
        return [*own, total, env["expand_sum"][0], env["cot_sum"][0]]

    ticks = 4 * blocks + 2
    plan = [[] for _ in range(ticks + 8)]
    after = [[] for _ in plan]
    turn = 2 * blocks
    last = blocks - 1
    add = lambda slot, make, *args: plan[slot].append(functools.partial(make, *args))
    for b in range(blocks):
        if b:
            add(b - 1, forward, b)
            add(b, out_part, b)
            add(turn + 2 * (b - 1), give_back, b)
        add(last + b, backward, b)
        if b:
            add(turn - 1 + 2 * b, grad_part, b)
        add(turn + 1 + 2 * b, put_out, b)
        add(turn + 2 * b + 2, sums, b)
        if b < last:
            add(turn + 2 * b + 4 + b % 2, put_grad, b, 0, 2)
    add(0, turn_keys)
    after[turn - 2].append(finish)
    add(turn - 1, give_back, 0)
    add(turn - 1, slope)
    after[turn - 1].append(functools.partial(grad_part, 0))
    add(turn, lambda: weight_grad("fc2", activated, cotangent, 1, 0, 1))
    add(turn + 2, lambda: weight_grad("fc1", hidden, env["grad_expand"], 0, 0, 2))
    add(turn + 4, lambda: weight_grad("fc1", hidden, env["grad_expand"], 0, 1, 2))
    add(2 * turn - 2, lambda: weight_grad("qkv", hidden, env["all_qkv"], 0, 0, 1))
    add(2 * turn - 1, lambda: weight_grad("dense", env["whole"], cotangent, 1, 0, 1))
    add(ticks - 1, add_all, "total", ("dp", "ctx"), all_pieces)
    add(ticks - 1, put_grad, last, 0, 1)
    add(ticks, put_grad, last, 1, 1)

    def perform(make):
        run, ins, keep = make()
        keep(run(*ins))

    perform(functools.partial(forward, 0))
    perform(functools.partial(out_part, 0))

    line = Line(flags, tokens, (b_dense.astype(F32) + b_fc2.astype(F32))[None])
    arrived = (None, None)
    for t in range(ticks):
        b, second = divmod(t, 2)
        if second:
            operands = line.middle(*arrived)
        else:
            if t > 0:
                total = line.end(*arrived)
                if total is not None:
                    env["total", b - 2] = total
            operands = line.begin(env.get(("part", b)), b < blocks)
        if t == ticks - 1:
            env["total", 2 * blocks - 1] = (line.first, line.near, line.first, line.near)
        stages = [s for s in (plan[t], after[t]) if s]
        sent = None
        for n, stage in enumerate(stages):
            work = [make() for make in stage]
            operands, ins = tie(operands, [w[1] for w in work])
            if sent is None:
                sent = send(*operands)
            outs = [w[0](*i) for w, i in zip(work, ins)]
            if n == len(stages) - 1:
                arrived, outs = tie(sent, outs)
            for w, out in zip(work, outs):
                w[2](out)
        if not stages:
            arrived = send(*operands)
    env["total", 2 * blocks - 1] = line.end(*arrived)
    own = env["total"][: 2 * width]
    both = own + lax.ppermute(own, "tp", [(1, 2), (2, 1)])
    norm_total = jnp.where(line.outer, lax.ppermute(both, "tp", [(1, 0), (2, 3)]), both)
    for late in plan[ticks:]:
        for make in late:
            perform(make)

    layer_out, grad_tokens = env["layer_out"], env["grad_tokens"]
    gain_sum, shift_sum = jnp.split(norm_total, 2)
    qkv_sum, expand_total, out_sum = jnp.split(
        env["total"][2 * width :], (3 * local, 3 * local + w_fc1.shape[1])
    )

    def unmixed(array):
        lead = array.shape[:-1]
        parts = array.reshape(*lead, ctx_count, 3, share)
        return tuple(parts[..., t, :].reshape(*lead, local) for t in range(3))

    grad_query, grad_key, grad_value = unmixed(env["qkv", 0])
    sum_query, sum_key, sum_value = unmixed(qkv_sum)
    return (
        layer_out, grad_tokens, gain_sum, shift_sum, grad_query, sum_query, grad_key, sum_key,
        grad_value, sum_value, env["dense", 0], out_sum,
        jnp.concatenate([env["fc1", 0], env["fc1", 1]], axis=1), expand_total, env["fc2", 0], out_sum,
    )


def solution(mesh):
    rows = P(("dp", "ctx"), None)
    down, across = P(("dp", "ctx"), "tp"), P("tp", ("dp", "ctx"))
    wide = P("tp")
    ins = (
        rows, rows, P("dp", None), P(), P(), down, wide, down, wide, down, wide, across, P(), down,
        wide, across, P(),
    )
    outs = (
        rows, rows, P(), P(), down, wide, down, wide, down, wide, across, P(), down, wide, across,
        P(),
    )
    return jax.shard_map(body, mesh=mesh, in_specs=ins, out_specs=outs, check_vma=False)
```
